256 devices in a mesh: tm: 64 (over x, z, core), heads: 4 (over y).
Axes of the slice: x: 4, y: 4, z: 8, core: 2. Of those that a mesh axis runs over, the one named last changes fastest.
Arguments:
- slab_tokens: bfloat16 [32768, 3584], P('tm', 'heads'), may hold values from -14 to 14
- memory: bfloat16 [32768, 3584], P('tm', 'heads'), may hold values from -14 to 14
- query_weight: bfloat16 [3584, 3584], P(None, 'heads'), may hold values from -0.09375 to 0.09375
- key_weight: bfloat16 [3584, 512], P(None, 'heads'), may hold values from -0.09375 to 0.09375
- value_weight: bfloat16 [3584, 512], P(None, 'heads'), may hold values from -0.09375 to 0.09375
- query_down: bfloat16 [16, 3584], replicated, may hold values from -0.09375 to 0.09375
- query_up: bfloat16 [16, 3584], P(None, 'heads'), may hold values from -1.5 to 1.5
- value_down: bfloat16 [16, 3584], replicated, may hold values from -0.09375 to 0.09375
- value_up: bfloat16 [16, 512], P(None, 'heads'), may hold values from -1.5 to 1.5
- tag_weight: bfloat16 [3584, 8], P('heads'), may hold values from -0.75 to 0.75
- retrieval: int32 [256, 8], P('tm'), may hold values from 0 to 255, as said below
- boundary: int32 [256], P('tm'), may hold values from 0 to 127
- grad_tags: float32 [32768, 8], P('tm'), may hold values from -0.125 to 0.125
Outputs:
- tag_logits: float32 [32768, 8], P('tm')
- query_down_grad: float32 [16, 3584], P(None, 'heads')
- query_up_grad: float32 [16, 3584], P(None, 'heads')
- value_down_grad: float32 [16, 3584], P(None, 'heads')
- value_up_grad: float32 [16, 512], P(None, 'heads')
The draws below stay inside these ranges and needn't reach their ends.
Inputs may be any that keep to these rules, and one draw needn't show every extreme that they name: `retrieval`: each row names 8 different memory blocks; the rows of one index of tm name at most 1 different blocks held by any one index of tm.
All inputs are finite; a program needn't handle non-finite values.
Results may differ from the reference program's by a relative error of at most 0.035.
The reference program's roundings to bfloat16 on the way (of `queries`, `probs_low`, `attended`, `attended_grad`, `score_grad` and `query_grad`) count: a program that leaves them out, or rounds other values in their place, can miss the bound.
Values may be sent and summed in bfloat16 or wider, within the bound.
A program may use at most 128 MiB of HBM per device.

```python
import jax
import jax.numpy as jnp
from jax import lax

D = 3584
HEADS = 28
KVH = 4
HD = 128
RANK = 16
TOP = 8
BLK = 128
CAP = 1
TAGS = 8
MB_DEV = 4
SPANS = 256
TOKENS = 32768
NMEM = 256
MEMTOK = 32768
N_TM = 64


def draw_slab_tokens(key, part):
    key = jax.random.fold_in(key, 11)
    first_key = jax.random.fold_in(key, 0)
    values = jax.random.normal(first_key, (TOKENS, D), jnp.float32)
    return jnp.clip(values, -14.0, 14.0).astype(jnp.bfloat16)


def draw_memory(key, part):
    key = jax.random.fold_in(key, 12)
    first_key = jax.random.fold_in(key, 0)
    values = jax.random.normal(first_key, (MEMTOK, D), jnp.float32)
    return jnp.clip(values, -14.0, 14.0).astype(jnp.bfloat16)


def draw_retrieval(key, part):
    key = jax.random.fold_in(key, 31)
    rank_key, noise_key, owner_key, offset_key = jax.random.split(key, 4)
    block_total = MB_DEV * N_TM
    per_device = SPANS // N_TM
    order = jax.random.permutation(rank_key, block_total)
    popular = 2 ** 15 // (order + 1)
    noise = jax.random.randint(noise_key, (SPANS, block_total), 0, 2 ** 17)
    span_ids = jnp.arange(SPANS, dtype=jnp.int32)[:, None]
    device_ids = span_ids // per_device
    first_span = span_ids % per_device == 0
    block_ids = jnp.arange(block_total, dtype=jnp.int32)[None, :]
    owners = block_ids // MB_DEV
    within = block_ids % MB_DEV
    offset_table = jax.random.randint(offset_key, (N_TM, N_TM), 0, MB_DEV)
    pair_offset = offset_table[device_ids, owners]
    allowed = (within - pair_offset) % MB_DEV < CAP
    offsets = jax.random.randint(owner_key, (N_TM,), 0, N_TM)
    forced_owner = (device_ids + jnp.take(offsets, device_ids)) % N_TM
    forced = first_span & (owners == forced_owner) & allowed
    scores = noise + popular[None, :] + forced.astype(jnp.int32) * 2 ** 18
    scores = jnp.where(allowed, scores * block_total + block_ids, -1 - block_ids)
    chosen = lax.top_k(scores, TOP)[1]
    return chosen.astype(jnp.int32)


def with_ends(result, key, least, largest):
    longest = result.shape.index(max(result.shape))
    spots = []
    for shift in (0, 1):
        where = [jax.random.randint(jax.random.fold_in(key, axis), (), 0, length) for axis, length in enumerate(result.shape)]
        where[longest] = (where[longest] + shift) % result.shape[longest]
        spots.append(tuple(where))
    return result.at[spots[0]].set(least).at[spots[1]].set(largest)


def levels(stream_key, extent, shards, smallest, high):
    level = 1.0
    for position, blocks in shards:
        steps = jax.random.uniform(jax.random.fold_in(jax.random.fold_in(stream_key, 6), position), (blocks,), jnp.float32, smallest / len(shards), high / len(shards))
        level = level * jnp.repeat(jnp.exp(steps), extent[position] // blocks).reshape((-1,) + (1,) * (len(extent) - 1 - position))
    return level


def centred(stream_key, shape, scale, most, cuts=(), kind=jnp.bfloat16):
    entries = scale * jax.random.normal(stream_key, shape, jnp.float32)
    if cuts:
        entries = entries * levels(stream_key, shape, cuts, -0.22, 0.18)
    return jnp.clip(entries, -most, most).astype(kind)


def setup_inputs(seed: int = 0) -> dict:
    keys = jax.random.split(jax.random.key(seed), 14)
    slab_tokens = draw_slab_tokens(jax.random.fold_in(keys[13], 71), 0)
    memory = draw_memory(jax.random.fold_in(keys[13], 71), 0)
    query_weight = centred(keys[2], (D, HEADS * HD), D ** -0.5, 0.09375, ((1, 4),))
    key_weight = centred(keys[3], (D, KVH * HD), D ** -0.5, 0.09375, ((1, 4),))
    value_weight = centred(keys[4], (D, KVH * HD), D ** -0.5, 0.09375, ((1, 4),))
    query_down = centred(keys[5], (RANK, D), D ** -0.5, 0.09375)
    query_up = centred(keys[6], (RANK, HEADS * HD), RANK ** -0.5, 1.5, ((1, 4),))
    value_down = centred(keys[7], (RANK, D), D ** -0.5, 0.09375)
    value_up = centred(keys[8], (RANK, KVH * HD), RANK ** -0.5, 1.5, ((1, 4),))
    tag_weight = centred(keys[9], (HEADS * HD, TAGS), 64 ** -0.5, 0.75, ((0, 4),))
    retrieval = draw_retrieval(jax.random.fold_in(keys[13], 71), 0)
    boundary = with_ends(jax.random.randint(keys[11], (SPANS,), 0, BLK), jax.random.fold_in(keys[11], 1), 0, BLK - 1).astype(jnp.int32)
    grad_tags = centred(keys[12], (TOKENS, TAGS), (4.0 / TOKENS ** 0.5), 0.125, ((0, 64),), jnp.float32)
    return dict(slab_tokens=slab_tokens, memory=memory, query_weight=query_weight, key_weight=key_weight, value_weight=value_weight, query_down=query_down, query_up=query_up, value_down=value_down, value_up=value_up, tag_weight=tag_weight, retrieval=retrieval, boundary=boundary, grad_tags=grad_tags)


HIGHEST = lax.Precision.HIGHEST


def attend(query, all_keys, all_values, split_row, out_grad):
    span_count, row_count, query_width = query.shape
    key_count, kv_width = all_keys.shape[1], all_keys.shape[2]
    kv_heads = kv_width // HD
    group_size = query_width // kv_width
    score_scale = HD ** -0.5
    query_heads = query.astype(jnp.float32).reshape(span_count, row_count, kv_heads, group_size, HD)
    key_heads = all_keys.astype(jnp.float32).reshape(span_count, key_count, kv_heads, HD)
    value_heads = all_values.astype(jnp.float32).reshape(span_count, key_count, kv_heads, HD)
    grad_heads = out_grad.astype(jnp.float32).reshape(span_count, row_count, kv_heads, group_size, HD)
    scores = jnp.einsum("crngd,cknd->cngrk", query_heads, key_heads, precision=HIGHEST) * score_scale
    row_ids = jnp.arange(row_count, dtype=jnp.int32)[:, None]
    col_ids = jnp.arange(BLK, dtype=jnp.int32)[None, :]
    edge_at = split_row[:, None, None]
    local_seen = (col_ids <= row_ids) & ((col_ids >= edge_at) | (row_ids < edge_at))
    visible = jnp.concatenate([jnp.ones((span_count, row_count, key_count - BLK), jnp.bool_), local_seen], axis=2)
    scores = jnp.where(visible[:, None, None], scores, -jnp.inf)
    row_max = jnp.max(scores, axis=-1, keepdims=True)
    weights = jnp.exp(scores - row_max)
    probs = weights / jnp.sum(weights, axis=-1, keepdims=True)
    probs_low = probs.astype(jnp.bfloat16).astype(jnp.float32)
    attended = jnp.einsum("cngrk,cknd->crngd", probs_low, value_heads, precision=HIGHEST).astype(jnp.bfloat16)
    prob_grad = jnp.einsum("crngd,cknd->cngrk", grad_heads, value_heads, precision=HIGHEST)
    row_dot = jnp.sum(grad_heads * attended.astype(jnp.float32), axis=-1)
    row_dot = jnp.transpose(row_dot, (0, 2, 3, 1))[..., None]
    score_grad = (probs * (prob_grad - row_dot) * score_scale).astype(jnp.bfloat16).astype(jnp.float32)
    query_grad = jnp.einsum("cngrk,cknd->crngd", score_grad, key_heads, precision=HIGHEST).astype(jnp.bfloat16)
    value_grad = jnp.einsum("cngrk,crngd->cknd", probs_low, grad_heads, precision=HIGHEST)
    return (attended.reshape(span_count, row_count, query_width),
            query_grad.reshape(span_count, row_count, query_width),
            value_grad.reshape(span_count, key_count, kv_width))


def reference(slab_tokens, memory, query_weight, key_weight, value_weight, query_down, query_up, value_down, value_up, tag_weight, retrieval, boundary, grad_tags):
    def project(left_side, right_side):
        return jnp.dot(left_side, right_side, preferred_element_type=jnp.float32)

    low_query = project(slab_tokens, query_down.T).astype(jnp.bfloat16)
    low_value = project(slab_tokens, value_down.T).astype(jnp.bfloat16)
    memory_low = project(memory, value_down.T).astype(jnp.bfloat16)
    queries = (project(slab_tokens, query_weight) + project(low_query, query_up)).astype(jnp.bfloat16)
    keys_local = project(slab_tokens, key_weight).astype(jnp.bfloat16)
    values_local = (project(slab_tokens, value_weight) + project(low_value, value_up)).astype(jnp.bfloat16)
    memory_keys = project(memory, key_weight).astype(jnp.bfloat16)
    memory_values = (project(memory, value_weight) + project(memory_low, value_up)).astype(jnp.bfloat16)
    kv_width = key_weight.shape[1]
    query_width = query_weight.shape[1]
    attended_grad = jnp.dot(grad_tags, tag_weight.astype(jnp.float32).T, precision=HIGHEST).astype(jnp.bfloat16)
    block_keys = memory_keys.reshape(NMEM, BLK, kv_width)
    block_values = memory_values.reshape(NMEM, BLK, kv_width)

    def span_step(memory_grad, inputs):
        query_block, key_block, value_block, grad_block, block_ids, split_row = inputs
        all_keys = jnp.concatenate([block_keys[block_ids].reshape(TOP * BLK, kv_width), key_block], 0)
        all_values = jnp.concatenate([block_values[block_ids].reshape(TOP * BLK, kv_width), value_block], 0)
        attended, query_grad, value_grad = attend(query_block[None], all_keys[None], all_values[None], split_row[None], grad_block[None])
        slot_grad = value_grad[0, :TOP * BLK].reshape(TOP, BLK, kv_width)
        memory_grad = memory_grad.at[block_ids].add(slot_grad)
        return memory_grad, (attended[0], query_grad[0], value_grad[0, TOP * BLK:])

    start_grad = jnp.zeros((NMEM, BLK, kv_width), jnp.float32)
    memory_grad, (attended, query_grad, local_grad) = lax.scan(
        span_step, start_grad,
        (queries.reshape(SPANS, BLK, query_width), keys_local.reshape(SPANS, BLK, kv_width),
         values_local.reshape(SPANS, BLK, kv_width), attended_grad.reshape(SPANS, BLK, query_width),
         retrieval, boundary))
    attended = attended.reshape(TOKENS, query_width)
    query_grad = query_grad.reshape(TOKENS, query_width)
    local_grad = local_grad.reshape(TOKENS, kv_width)
    memory_grad = memory_grad.reshape(MEMTOK, kv_width)
    tag_logits = project(attended, tag_weight)
    up_wide = value_up.astype(jnp.float32)
    query_low_grad = project(query_grad, query_up.T).astype(jnp.bfloat16)
    value_low_grad = jnp.dot(local_grad, up_wide.T, precision=HIGHEST).astype(jnp.bfloat16)
    memory_low_grad = jnp.dot(memory_grad, up_wide.T, precision=HIGHEST).astype(jnp.bfloat16)
    query_up_grad = project(low_query.T, query_grad)
    value_up_grad = (jnp.dot(low_value.astype(jnp.float32).T, local_grad, precision=HIGHEST)
                     + jnp.dot(memory_low.astype(jnp.float32).T, memory_grad, precision=HIGHEST))
    query_down_grad = project(query_low_grad.T, slab_tokens)
    value_down_grad = project(value_low_grad.T, slab_tokens) + project(memory_low_grad.T, memory)
    return tag_logits, query_down_grad, query_up_grad, value_down_grad, value_up_grad
```

```python
import functools
import jax, jax.numpy as jnp
from jax import lax
from jax.sharding import PartitionSpec as P
from jax.experimental import pallas as pl
from jax.experimental.pallas import tpu as pltpu
BLK=128; HD=128; TOP=8; RANK=16; TAGS=8
HIGHEST=lax.Precision.HIGHEST
NT=(((1,),(1,)),((),()))
TN=(((0,),(0,)),((),()))
f32=jnp.float32; bf16=jnp.bfloat16
MB=4; OWNERS=64; ROWS=272; CH=384
def attend_kernel(ret,bnd, q_ref, kl_ref, vl_ref, low_ref, gt_ref, tw_ref, twt_ref, qup_ref, vup_ref, pool_ref,
                  cols_ref, qug_ref, vug_ref, mcot_ref,
                  land, kk, vv, lt, qs, gm, gs, st, pb, sg, at, qg, vg, sems):
    c=pl.program_id(0)
    heads=q_ref.shape[1]//HD
    wide=heads*BLK
    nkeys=(TOP+1)*BLK
    def fetch(i):
        return pltpu.make_async_copy(pool_ref.at[ret[lax.div(i,TOP),lax.rem(i,TOP)]], land.at[i], sems.at[i])
    @pl.when(c==0)
    def _():
        def go(i,_):
            fetch(i).start(); return 0
        lax.fori_loop(0,4*TOP,go,0)
        qug_ref[...]=jnp.zeros_like(qug_ref)
        vug_ref[...]=jnp.zeros_like(vug_ref)
        mcot_ref[...]=jnp.zeros_like(mcot_ref)
    rows=pl.ds(pl.multiple_of(c*BLK,BLK),BLK)
    grads=gt_ref[:,rows]
    for h in range(heads):
        cols=slice(h*HD,(h+1)*HD)
        g=jnp.dot(tw_ref[cols,:].astype(f32),grads,precision=HIGHEST,preferred_element_type=f32).astype(bf16)
        gm[:,cols]=g
        gs[cols,:]=g.T
        qs[cols,:]=q_ref[rows,cols]
    for s in range(TOP):
        i=c*TOP+s
        fetch(i).wait()
        kk[s*BLK:(s+1)*BLK,:]=land[i,0:128,:]
        vv[s*BLK:(s+1)*BLK,:]=land[i,128:256,:]
        lt[:,s*BLK:(s+1)*BLK]=land[i,256:272,:]
    own=slice(TOP*BLK,nkeys)
    kk[own,:]=kl_ref[rows,:]
    vv[own,:]=vl_ref[rows,:]
    lt[:,own]=low_ref[RANK:,rows]
    edge=bnd[c]
    def p1(j,m):
        r=pl.ds(pl.multiple_of(j*CH,CH),CH)
        s=lax.dot_general(kk[r,:],qs[...],NT,preferred_element_type=f32)
        st[r,:]=s
        return jnp.maximum(m,jnp.max(s[:CH-BLK],axis=0,keepdims=True)), s
    m=jnp.full((1,wide),-jnp.inf,f32)
    scale=HD**-0.5
    n_ch=nkeys//CH
    for j in range(n_ch):
        r=slice(j*CH,(j+1)*CH)
        s=lax.dot_general(kk[r,:],qs[...],NT,preferred_element_type=f32)*scale
        if j==n_ch-1:
            key=lax.broadcasted_iota(jnp.int32,(BLK,BLK),0)
            row=lax.broadcasted_iota(jnp.int32,(BLK,BLK),1)
            seen=(key<=row)&((key>=edge)|(row<edge))
            bias=jnp.where(seen,0.0,-jnp.inf).astype(f32)
            bias=jnp.concatenate([bias]*heads,axis=1)
            last=s[CH-BLK:]+bias
            s=jnp.concatenate([s[:CH-BLK],last],axis=0)
        st[r,:]=s
        m=jnp.maximum(m,jnp.max(s,axis=0,keepdims=True))
    tot=jnp.zeros((1,wide),f32)
    for j in range(n_ch):
        r=slice(j*CH,(j+1)*CH)
        e=jnp.exp(st[r,:]-m)
        st[r,:]=e
        tot=tot+jnp.sum(e,axis=0,keepdims=True)
    inv=1.0/tot
    acc=jnp.zeros((HD,wide),f32)
    for j in range(n_ch):
        r=slice(j*CH,(j+1)*CH)
        p=st[r,:]*inv
        st[r,:]=p
        pl_=p.astype(bf16)
        pb[r,:]=pl_
        acc=acc+lax.dot_general(vv[r,:],pl_,TN,preferred_element_type=f32)
    att=acc.astype(bf16)
    at[...]=att
    dot_row=jnp.sum(gm[...].astype(f32)*att.astype(f32),axis=0,keepdims=True)
    logits=jnp.zeros((TAGS,BLK),f32)
    for h in range(heads):
        cols=slice(h*HD,(h+1)*HD)
        logits=logits+jnp.dot(twt_ref[:,cols],at[:,cols],preferred_element_type=f32)
    cols_ref[c,0:TAGS,:]=logits
    acc=jnp.zeros((HD,wide),f32)
    for j in range(n_ch):
        r=slice(j*CH,(j+1)*CH)
        pg=jnp.dot(vv[r,:],gm[...],preferred_element_type=f32)
        sgr=(st[r,:]*(pg-dot_row)*scale).astype(bf16)
        acc=acc+lax.dot_general(kk[r,:],sgr,TN,preferred_element_type=f32)
        vg[r,:]=jnp.dot(pb[r,:],gs[...],preferred_element_type=f32)
    qg[...]=acc.astype(bf16)
    qcot=jnp.zeros((RANK,BLK),f32)
    for h in range(heads):
        cols=slice(h*HD,(h+1)*HD)
        qgh=qg[:,cols]
        qcot=qcot+jnp.dot(qup_ref[:,cols],qgh,preferred_element_type=f32)
        qug_ref[:,cols]+=lax.dot_general(low_ref[:RANK,rows],qgh,NT,preferred_element_type=f32)
    cols_ref[c,TAGS:TAGS+RANK,:]=qcot
    cot=lax.dot_general(vup_ref[...].astype(f32),vg[...],NT,precision=HIGHEST,preferred_element_type=f32)
    cols_ref[c,TAGS+RANK:,:]=cot[:,own]
    for s in range(TOP):
        mcot_ref[lax.div(ret[c,s],MB)]+=cot[:,s*BLK:(s+1)*BLK]
    vug_ref[...]+=jnp.dot(lt[...].astype(f32),vg[...],precision=HIGHEST,preferred_element_type=f32)

def attend(retrieval,boundary,q,kl,vl,low_t,grad_t,tw,tw_t,qup,vup,pool):
    n=q.shape[0]; wide=q.shape[1]; nk=(TOP+1)*BLK; spans=n//BLK
    vm=pl.BlockSpec(memory_space=pltpu.VMEM)
    shp=lambda *s: jax.ShapeDtypeStruct(s,f32)
    return pl.pallas_call(attend_kernel,
        grid_spec=pltpu.PrefetchScalarGridSpec(num_scalar_prefetch=2,grid=(spans,),
            in_specs=[vm]*9+[pl.BlockSpec(memory_space=pl.ANY)],
            out_specs=[vm]*4,
            scratch_shapes=[pltpu.VMEM((spans*TOP,ROWS,HD),bf16),pltpu.VMEM((nk,HD),bf16),pltpu.VMEM((nk,HD),bf16),pltpu.VMEM((RANK,nk),bf16),
              pltpu.VMEM((wide,HD),bf16),pltpu.VMEM((HD,wide),bf16),pltpu.VMEM((wide,HD),bf16),
              pltpu.VMEM((nk,wide),f32),pltpu.VMEM((nk,wide),bf16),pltpu.VMEM((8,128),bf16),
              pltpu.VMEM((HD,wide),bf16),pltpu.VMEM((HD,wide),bf16),pltpu.VMEM((nk,HD),f32),
              pltpu.SemaphoreType.DMA((spans*TOP,))]),
        out_shape=[shp(spans,TAGS+2*RANK,BLK),shp(RANK,wide),shp(RANK,HD),shp(OWNERS,RANK,BLK)],
        compiler_params=pltpu.CompilerParams(vmem_limit_bytes=50*2**20,dimension_semantics=("arbitrary",)),
    )(retrieval,boundary,q,kl,vl,low_t,grad_t,tw,tw_t,qup,vup,pool)

X=4; Y=4; Z=8; ZC=16; MESH=pl.DeviceIdType.MESH

def place():
    t=lax.axis_index("tm"); y=lax.axis_index("heads")
    return lax.div(t,ZC), y, lax.rem(t,ZC)

def reduce_kernel(w_ref, cols_ref, qug_ref, vug_ref, mcot_ref, slab_ref, mem_ref,
                  logit_out, grad_out,
                  xbuf, tbuf, ybuf, mbuf, zbuf, mall, cbuf, csum, lall, call, g1, r1, x1, o1, g2, r2, x2, o2,
                  xs, ys, zs, ms, cs, ls, ks, a1, b1, d1, a2, b2, d2):
    x,y,q=place()
    def xp(k): return (lax.rem(x+k,X)*ZC+q, y)
    def yp(k): return (x*ZC+q, lax.rem(y+k,Y))
    def zp(k): return (x*ZC+lax.rem(q+k,ZC), y)
    def each(n,do):
        def body(k,_):
            do(k); return 0
        lax.fori_loop(1,n,body,0)
    def rc(src,dst,sems,k,dev):
        return pltpu.make_async_remote_copy(src_ref=src,dst_ref=dst,send_sem=sems.at[0,k],recv_sem=sems.at[1,k],device_id=dev,device_id_type=MESH)
    bar=pltpu.get_barrier_semaphore()
    each(X,lambda k: pl.semaphore_signal(bar,inc=1,device_id=xp(k),device_id_type=MESH))
    each(Y,lambda k: pl.semaphore_signal(bar,inc=1,device_id=yp(k),device_id_type=MESH))
    each(ZC,lambda k: pl.semaphore_signal(bar,inc=1,device_id=zp(k),device_id_type=MESH))
    pl.semaphore_wait(bar,X+Y+ZC-3)
    mx=lambda k: rc(mcot_ref.at[pl.ds(lax.rem(x+k,X)*ZC,ZC)],xbuf.at[k],xs,k,xp(k))
    cy=lambda k: rc(cols_ref.at[lax.rem(y+k,Y)],cbuf.at[k],cs,k,yp(k))
    each(Y,lambda k: cy(k).start())
    each(X,lambda k: mx(k).start())
    each(Y,lambda k: cy(k).wait())
    total=cols_ref[y]+cbuf[1]+cbuf[2]+cbuf[3]
    lall[y]=total[:TAGS]
    call[y]=total[TAGS:].astype(bf16)
    ly=lambda k: rc(lall.at[y],lall.at[y],ls,k,yp(k))
    ky=lambda k: rc(call.at[y],call.at[y],ks,k,yp(k))
    each(Y,lambda k: ky(k).start())
    each(Y,lambda k: ly(k).start())
    each(X,lambda k: mx(k).wait())
    def expand(o,_):
        parts=[mcot_ref[x*ZC+o]]+[xbuf[k,o] for k in range(1,X)]
        for m in range(MB):
            acc=parts[0]*w_ref[x,o*MB+m]
            for k in range(1,X):
                acc=acc+parts[k]*w_ref[lax.rem(x+X-k,X),o*MB+m]
            tbuf[m,o]=acc
        return 0
    lax.fori_loop(0,ZC,expand,0)
    ty=lambda k: rc(tbuf.at[lax.rem(y+k,Y)],ybuf.at[k],ys,k,yp(k))
    each(Y,lambda k: ty(k).start())
    each(Y,lambda k: ky(k).wait())
    def split(ref,first,value):
        for j in range(value.shape[1]//128):
            ref[first+2*j]=value[0:8,j*128:(j+1)*128]
            ref[first+2*j+1]=value[8:16,j*128:(j+1)*128]
    qdg=jnp.zeros(qug_ref.shape,f32); vdg=jnp.zeros(qug_ref.shape,f32)
    for s in range(Y):
        piece=slab_ref[s*BLK:(s+1)*BLK,:]
        qdg=qdg+jnp.dot(call[s,0:RANK],piece,preferred_element_type=f32)
        vdg=vdg+jnp.dot(call[s,RANK:],piece,preferred_element_type=f32)
    split(g1,0,qdg); split(g1,14,qug_ref[...]); split(g1,28,vug_ref[...])
    g1[30]=jnp.zeros((8,128),f32); g1[31]=jnp.zeros((8,128),f32)
    ga=lambda k: rc(g1.at[pl.ds(lax.rem(q+k,ZC)*2,2)],r1.at[k],a1,k,zp(k))
    each(ZC,lambda k: ga(k).start())
    each(Y,lambda k: ty(k).wait())
    def ysum(o,_):
        mbuf[o]=tbuf[y,o]+ybuf[1,o]+ybuf[2,o]+ybuf[3,o]
        return 0
    lax.fori_loop(0,ZC,ysum,0)
    mz=lambda k: rc(mbuf.at[lax.rem(q+k,ZC)],zbuf.at[k],zs,k,zp(k))
    each(ZC,lambda k: mz(k).start())
    each(ZC,lambda k: ga(k).wait())
    acc=g1[pl.ds(q*2,2)]
    for k in range(1,ZC): acc=acc+r1[k]
    x1[x]=acc
    gb=lambda k: rc(x1.at[x],x1.at[x],b1,k,xp(k))
    each(X,lambda k: gb(k).start())
    each(ZC,lambda k: mz(k).wait())
    acc=mbuf[q]
    for k in range(1,ZC): acc=acc+zbuf[k]
    mall[y]=acc.astype(bf16)
    my=lambda k: rc(mall.at[y],mall.at[y],ms,k,yp(k))
    each(Y,lambda k: my(k).start())
    each(X,lambda k: gb(k).wait())
    o1[q]=x1[0]+x1[1]+x1[2]+x1[3]
    gd=lambda k: rc(o1.at[q],o1.at[q],d1,k,zp(k))
    each(ZC,lambda k: gd(k).start())
    each(Y,lambda k: my(k).wait())
    for m in range(MB):
        vdg=vdg+jnp.dot(mall[m],mem_ref[m*BLK:(m+1)*BLK,:],preferred_element_type=f32)
    split(g2,0,vdg)
    g2[14]=jnp.zeros((8,128),f32); g2[15]=jnp.zeros((8,128),f32)
    ha=lambda k: rc(g2.at[lax.rem(q+k,ZC)],r2.at[k],a2,k,zp(k))
    each(ZC,lambda k: ha(k).start())
    each(ZC,lambda k: ha(k).wait())
    acc=g2[q]
    for k in range(1,ZC): acc=acc+r2[k]
    x2[x]=acc
    hb=lambda k: rc(x2.at[x],x2.at[x],b2,k,xp(k))
    each(X,lambda k: hb(k).start())
    each(X,lambda k: hb(k).wait())
    o2[q]=x2[0]+x2[1]+x2[2]+x2[3]
    hd=lambda k: rc(o2.at[q],o2.at[q],d2,k,zp(k))
    each(ZC,lambda k: hd(k).start())
    each(Y,lambda k: ly(k).wait())
    for s in range(Y):
        logit_out[:,s*BLK:(s+1)*BLK]=lall[s]
    each(ZC,lambda k: gd(k).wait())
    for k in range(15):
        for i in range(2):
            grad_out[i*8:(i+1)*8,k*128:(k+1)*128]=o1[k,i]
    each(ZC,lambda k: hd(k).wait())
    for k in range(14):
        grad_out[(k%2)*8:(k%2)*8+8,(15+k//2)*128:(16+k//2)*128]=o2[k]

def reduce_all(w,cols,qug,vug,mcot,slab,mem):
    vm=pl.BlockSpec(memory_space=pltpu.VMEM)
    wide=qug.shape[1]
    V=pltpu.VMEM
    sem=lambda n: pltpu.SemaphoreType.DMA((2,n))
    return pl.pallas_call(reduce_kernel,
        in_specs=[pl.BlockSpec(memory_space=pltpu.SMEM)]+[vm]*6,
        out_specs=[vm,vm],
        out_shape=[jax.ShapeDtypeStruct((TAGS,slab.shape[0]),f32),jax.ShapeDtypeStruct((RANK,3*wide+HD),f32)],
        scratch_shapes=[V((X,ZC,RANK,BLK),f32),V((MB,ZC,RANK,BLK),f32),V((Y,ZC,RANK,BLK),f32),V((ZC,RANK,BLK),f32),V((ZC,RANK,BLK),f32),V((MB,RANK,BLK),bf16),
            V((Y,TAGS+2*RANK,BLK),f32),V((8,128),f32),V((Y,TAGS,BLK),f32),V((Y,2*RANK,BLK),bf16),
            V((32,8,128),f32),V((ZC,2,8,128),f32),V((X,2,8,128),f32),V((ZC,2,8,128),f32),
            V((16,8,128),f32),V((ZC,8,128),f32),V((X,8,128),f32),V((ZC,8,128),f32),
            sem(X),sem(Y),sem(ZC),sem(Y),sem(Y),sem(Y),sem(Y),sem(ZC),sem(X),sem(ZC),sem(ZC),sem(X),sem(ZC)],
        compiler_params=pltpu.CompilerParams(collective_id=1,has_side_effects=True,vmem_limit_bytes=32*2**20),
    )(w,cols,qug,vug,mcot,slab,mem)

def local(slab_tokens,memory,query_weight,key_weight,value_weight,query_down,query_up,value_down,value_up,tag_weight,retrieval,boundary,grad_tags):
    x,y,q=place()
    every=lax.all_gather(retrieval,"tm",axis=0,tiled=True).reshape(OWNERS,-1)
    mine=jnp.stack([lax.dynamic_index_in_dim(every,k*ZC+q,0,False) for k in range(X)])
    blocks=x*ZC*MB+jnp.arange(ZC*MB,dtype=jnp.int32)
    w=jnp.any(mine[:,:,None]==blocks[None,None,:],axis=1).astype(f32)
    pair_weight=jnp.concatenate([key_weight,value_weight],1)
    adapter_pair=jnp.concatenate([query_down,value_down],0)
    mem_full=lax.all_gather(memory,"heads",axis=1,tiled=True)
    tok_full=lax.all_gather(slab_tokens,"heads",axis=1,tiled=True)
    dot=lambda a,b: jnp.dot(a,b,preferred_element_type=f32)
    pair=lambda full,low: (dot(full,pair_weight)+jnp.pad(dot(low,value_up),((0,0),(HD,0)))).astype(bf16)
    mem_low=lax.dot_general(mem_full,value_down,NT,preferred_element_type=f32).astype(bf16)
    mem_pair=pair(mem_full,mem_low).reshape(MB,BLK,2*HD)
    piece=jnp.concatenate([mem_pair[:,:,:HD],mem_pair[:,:,HD:],mem_low.reshape(MB,BLK,RANK).transpose(0,2,1)],1)
    pool=lax.all_gather(piece,"tm",axis=0,tiled=True)
    low_t=lax.dot_general(adapter_pair,tok_full,NT,preferred_element_type=f32).astype(bf16)
    tok_pair=pair(tok_full,low_t[RANK:].T)
    queries=(dot(tok_full,query_weight)+dot(low_t[:RANK].T,query_up)).astype(bf16)
    cols,qug,vug,mcot=attend(retrieval,boundary,queries,tok_pair[:,:HD],tok_pair[:,HD:],low_t,grad_tags.T,tag_weight,tag_weight.T,query_up,value_up,pool)
    logits,grads=reduce_all(w,cols,qug,vug,mcot,slab_tokens,memory)
    wide=qug.shape[1]
    return logits.T,grads[:,:wide],grads[:,wide:2*wide],grads[:,2*wide+HD:],grads[:,2*wide:2*wide+HD]


def solution(mesh):
    in_specs=(P("tm","heads"),P("tm","heads"),P(None,"heads"),P(None,"heads"),P(None,"heads"),P(),P(None,"heads"),P(),P(None,"heads"),P("heads",None),P("tm",None),P("tm"),P("tm",None))
    out_specs=(P("tm",None),P(None,"heads"),P(None,"heads"),P(None,"heads"),P(None,"heads"))
    return jax.shard_map(local,mesh=mesh,in_specs=in_specs,out_specs=out_specs,check_vma=False)
```

```python
import functools
import jax, jax.numpy as jnp
from jax import lax
from jax.sharding import PartitionSpec as P
from jax.experimental import pallas as pl
from jax.experimental.pallas import tpu as pltpu
BLK=128; HD=128; TOP=8; RANK=16; TAGS=8
HIGHEST=lax.Precision.HIGHEST
NT=(((1,),(1,)),((),()))
TN=(((0,),(0,)),((),()))
f32=jnp.float32; bf16=jnp.bfloat16
MB=4; OWNERS=64; ROWS=272; CH=384
def attend_kernel(ret,bnd, q_ref, kl_ref, vl_ref, low_ref, gt_ref, tw_ref, twt_ref, qup_ref, vup_ref, pool_ref,
                  cols_ref, qug_ref, vug_ref, mcot_ref,
                  land, kk, vv, lt, qs, gm, gs, st, pb, sg, at, qg, vg, sems):
    c=pl.program_id(0)
    heads=q_ref.shape[1]//HD
    wide=heads*BLK
    nkeys=(TOP+1)*BLK
    def fetch(i):
        return pltpu.make_async_copy(pool_ref.at[ret[lax.div(i,TOP),lax.rem(i,TOP)]], land.at[i], sems.at[i])
    @pl.when(c==0)
    def _():
        def go(i,_):
            fetch(i).start(); return 0
        lax.fori_loop(0,4*TOP,go,0)
        qug_ref[...]=jnp.zeros_like(qug_ref)
        vug_ref[...]=jnp.zeros_like(vug_ref)
        mcot_ref[...]=jnp.zeros_like(mcot_ref)
    rows=pl.ds(pl.multiple_of(c*BLK,BLK),BLK)
    grads=gt_ref[:,rows]
    for h in range(heads):
        cols=slice(h*HD,(h+1)*HD)
        g=jnp.dot(tw_ref[cols,:].astype(f32),grads,precision=HIGHEST,preferred_element_type=f32).astype(bf16)
        gm[:,cols]=g
        gs[cols,:]=g.T
        qs[cols,:]=q_ref[rows,cols]
    for s in range(TOP):
        i=c*TOP+s
        fetch(i).wait()
        kk[s*BLK:(s+1)*BLK,:]=land[i,0:128,:]
        vv[s*BLK:(s+1)*BLK,:]=land[i,128:256,:]
        lt[:,s*BLK:(s+1)*BLK]=land[i,256:272,:]
    own=slice(TOP*BLK,nkeys)
    kk[own,:]=kl_ref[rows,:]
    vv[own,:]=vl_ref[rows,:]
    lt[:,own]=low_ref[RANK:,rows]
    edge=bnd[c]
    def p1(j,m):
        r=pl.ds(pl.multiple_of(j*CH,CH),CH)
        s=lax.dot_general(kk[r,:],qs[...],NT,preferred_element_type=f32)
        st[r,:]=s
        return jnp.maximum(m,jnp.max(s[:CH-BLK],axis=0,keepdims=True)), s
    m=jnp.full((1,wide),-jnp.inf,f32)
    scale=HD**-0.5
    n_ch=nkeys//CH
    for j in range(n_ch):
        r=slice(j*CH,(j+1)*CH)
        s=lax.dot_general(kk[r,:],qs[...],NT,preferred_element_type=f32)*scale
        if j==n_ch-1:
            key=lax.broadcasted_iota(jnp.int32,(BLK,BLK),0)
            row=lax.broadcasted_iota(jnp.int32,(BLK,BLK),1)
            seen=(key<=row)&((key>=edge)|(row<edge))
            bias=jnp.where(seen,0.0,-jnp.inf).astype(f32)
            bias=jnp.concatenate([bias]*heads,axis=1)
            last=s[CH-BLK:]+bias
            s=jnp.concatenate([s[:CH-BLK],last],axis=0)
        st[r,:]=s
        m=jnp.maximum(m,jnp.max(s,axis=0,keepdims=True))
    tot=jnp.zeros((1,wide),f32)
    for j in range(n_ch):
        r=slice(j*CH,(j+1)*CH)
        e=jnp.exp(st[r,:]-m)
        st[r,:]=e
        tot=tot+jnp.sum(e,axis=0,keepdims=True)
    inv=1.0/tot
    acc=jnp.zeros((HD,wide),f32)
    for j in range(n_ch):
        r=slice(j*CH,(j+1)*CH)
        p=st[r,:]*inv
        st[r,:]=p
        pl_=p.astype(bf16)
        pb[r,:]=pl_
        acc=acc+lax.dot_general(vv[r,:],pl_,TN,preferred_element_type=f32)
    att=acc.astype(bf16)
    at[...]=att
    dot_row=jnp.sum(gm[...].astype(f32)*att.astype(f32),axis=0,keepdims=True)
    logits=jnp.zeros((TAGS,BLK),f32)
    for h in range(heads):
        cols=slice(h*HD,(h+1)*HD)
        logits=logits+jnp.dot(twt_ref[:,cols],at[:,cols],preferred_element_type=f32)
    cols_ref[c,0:TAGS,:]=logits
    acc=jnp.zeros((HD,wide),f32)
    for j in range(n_ch):
        r=slice(j*CH,(j+1)*CH)
        pg=jnp.dot(vv[r,:],gm[...],preferred_element_type=f32)
        sgr=(st[r,:]*(pg-dot_row)*scale).astype(bf16)
        acc=acc+lax.dot_general(kk[r,:],sgr,TN,preferred_element_type=f32)
        vg[r,:]=jnp.dot(pb[r,:],gs[...],preferred_element_type=f32)
    qg[...]=acc.astype(bf16)
    qcot=jnp.zeros((RANK,BLK),f32)
    for h in range(heads):
        cols=slice(h*HD,(h+1)*HD)
        qgh=qg[:,cols]
        qcot=qcot+jnp.dot(qup_ref[:,cols],qgh,preferred_element_type=f32)
        qug_ref[:,cols]+=lax.dot_general(low_ref[:RANK,rows],qgh,NT,preferred_element_type=f32)
    cols_ref[c,TAGS:TAGS+RANK,:]=qcot
    cot=lax.dot_general(vup_ref[...].astype(f32),vg[...],NT,precision=HIGHEST,preferred_element_type=f32)
    cols_ref[c,TAGS+RANK:,:]=cot[:,own]
    for s in range(TOP):
        mcot_ref[lax.div(ret[c,s],MB)]+=cot[:,s*BLK:(s+1)*BLK]
    vug_ref[...]+=jnp.dot(lt[...].astype(f32),vg[...],precision=HIGHEST,preferred_element_type=f32)

def attend(retrieval,boundary,q,kl,vl,low_t,grad_t,tw,tw_t,qup,vup,pool):
    n=q.shape[0]; wide=q.shape[1]; nk=(TOP+1)*BLK; spans=n//BLK
    vm=pl.BlockSpec(memory_space=pltpu.VMEM)
    shp=lambda *s: jax.ShapeDtypeStruct(s,f32)
    return pl.pallas_call(attend_kernel,
        grid_spec=pltpu.PrefetchScalarGridSpec(num_scalar_prefetch=2,grid=(spans,),
            in_specs=[vm]*9+[pl.BlockSpec(memory_space=pl.ANY)],
            out_specs=[vm]*4,
            scratch_shapes=[pltpu.VMEM((spans*TOP,ROWS,HD),bf16),pltpu.VMEM((nk,HD),bf16),pltpu.VMEM((nk,HD),bf16),pltpu.VMEM((RANK,nk),bf16),
              pltpu.VMEM((wide,HD),bf16),pltpu.VMEM((HD,wide),bf16),pltpu.VMEM((wide,HD),bf16),
              pltpu.VMEM((nk,wide),f32),pltpu.VMEM((nk,wide),bf16),pltpu.VMEM((8,128),bf16),
              pltpu.VMEM((HD,wide),bf16),pltpu.VMEM((HD,wide),bf16),pltpu.VMEM((nk,HD),f32),
              pltpu.SemaphoreType.DMA((spans*TOP,))]),
        out_shape=[shp(spans,TAGS+2*RANK,BLK),shp(RANK,wide),shp(RANK,HD),shp(OWNERS,RANK,BLK)],
        compiler_params=pltpu.CompilerParams(vmem_limit_bytes=50*2**20,dimension_semantics=("arbitrary",)),
    )(retrieval,boundary,q,kl,vl,low_t,grad_t,tw,tw_t,qup,vup,pool)

X=4; Y=4; Z=8; ZC=16; MESH=pl.DeviceIdType.MESH

def place():
    t=lax.axis_index("tm"); y=lax.axis_index("heads")
    return lax.div(t,ZC), y, lax.rem(t,ZC)

def reduce_kernel(w_ref, cols_ref, qug_ref, vug_ref, mcot_ref, slab_ref, mem_ref,
                  logit_out, grad_out,
                  xbuf, tbuf, ybuf, mbuf, zbuf, mall, cbuf, csum, lall, call, g1, r1, x1, o1, g2, r2, x2, o2,
                  xs, ys, zs, ms, cs, ls, ks, a1, b1, d1, a2, b2, d2):
    x,y,q=place()
    def xp(k): return (lax.rem(x+k,X)*ZC+q, y)
    def yp(k): return (x*ZC+q, lax.rem(y+k,Y))
    def zp(k): return (x*ZC+lax.rem(q+k,ZC), y)
    def each(n,do):
        def body(k,_):
            do(k); return 0
        lax.fori_loop(1,n,body,0)
    def rc(src,dst,sems,k,dev):
        return pltpu.make_async_remote_copy(src_ref=src,dst_ref=dst,send_sem=sems.at[0,k],recv_sem=sems.at[1,k],device_id=dev,device_id_type=MESH)
    bar=pltpu.get_barrier_semaphore()
    each(X,lambda k: pl.semaphore_signal(bar,inc=1,device_id=xp(k),device_id_type=MESH))
    each(Y,lambda k: pl.semaphore_signal(bar,inc=1,device_id=yp(k),device_id_type=MESH))
    each(ZC,lambda k: pl.semaphore_signal(bar,inc=1,device_id=zp(k),device_id_type=MESH))
    pl.semaphore_wait(bar,X+Y+ZC-3)
    mx=lambda k: rc(mcot_ref.at[pl.ds(lax.rem(x+k,X)*ZC,ZC)],xbuf.at[k],xs,k,xp(k))
    cy=lambda k: rc(cols_ref.at[lax.rem(y+k,Y)],cbuf.at[k],cs,k,yp(k))
    each(Y,lambda k: cy(k).start())
    each(X,lambda k: mx(k).start())
    each(Y,lambda k: cy(k).wait())
    total=cols_ref[y]+cbuf[1]+cbuf[2]+cbuf[3]
    lall[y]=total[:TAGS]
    call[y]=total[TAGS:].astype(bf16)
    ly=lambda k: rc(lall.at[y],lall.at[y],ls,k,yp(k))
    ky=lambda k: rc(call.at[y],call.at[y],ks,k,yp(k))
    each(Y,lambda k: ky(k).start())
    each(Y,lambda k: ly(k).start())
    each(X,lambda k: mx(k).wait())
    def expand(o,_):
        parts=[mcot_ref[x*ZC+o]]+[xbuf[k,o] for k in range(1,X)]
        for m in range(MB):
            acc=parts[0]*w_ref[0,o*MB+m]
            for k in range(1,X):
                acc=acc+parts[k]*w_ref[k,o*MB+m]
            tbuf[m,o]=acc
        return 0
    lax.fori_loop(0,ZC,expand,0)
    ty=lambda k: rc(tbuf.at[lax.rem(y+k,Y)],ybuf.at[k],ys,k,yp(k))
    each(Y,lambda k: ty(k).start())
    each(Y,lambda k: ky(k).wait())
    def split(ref,first,value):
        for j in range(value.shape[1]//128):
            ref[first+2*j]=value[0:8,j*128:(j+1)*128]
            ref[first+2*j+1]=value[8:16,j*128:(j+1)*128]
    qdg=jnp.zeros(qug_ref.shape,f32); vdg=jnp.zeros(qug_ref.shape,f32)
    for s in range(Y):
        piece=slab_ref[s*BLK:(s+1)*BLK,:]
        qdg=qdg+jnp.dot(call[s,0:RANK],piece,preferred_element_type=f32)
        vdg=vdg+jnp.dot(call[s,RANK:],piece,preferred_element_type=f32)
    split(g1,0,qdg); split(g1,14,qug_ref[...]); split(g1,28,vug_ref[...])
    g1[30]=jnp.zeros((8,128),f32); g1[31]=jnp.zeros((8,128),f32)
    ga=lambda k: rc(g1.at[pl.ds(lax.rem(q+k,ZC)*2,2)],r1.at[k],a1,k,zp(k))
    each(ZC,lambda k: ga(k).start())
    each(Y,lambda k: ty(k).wait())
    def ysum(o,_):
        mbuf[o]=tbuf[y,o]+ybuf[1,o]+ybuf[2,o]+ybuf[3,o]
        return 0
    lax.fori_loop(0,ZC,ysum,0)
    mz=lambda k: rc(mbuf.at[lax.rem(q+k,ZC)],zbuf.at[k],zs,k,zp(k))
    each(ZC,lambda k: mz(k).start())
    each(ZC,lambda k: ga(k).wait())
    acc=g1[pl.ds(q*2,2)]
    for k in range(1,ZC): acc=acc+r1[k]
    x1[x]=acc
    gb=lambda k: rc(x1.at[x],x1.at[x],b1,k,xp(k))
    each(X,lambda k: gb(k).start())
    each(ZC,lambda k: mz(k).wait())
    acc=mbuf[q]
    for k in range(1,ZC): acc=acc+zbuf[k]
    mall[y]=acc.astype(bf16)
    my=lambda k: rc(mall.at[y],mall.at[y],ms,k,yp(k))
    each(Y,lambda k: my(k).start())
    each(X,lambda k: gb(k).wait())
    o1[q]=x1[0]+x1[1]+x1[2]+x1[3]
    gd=lambda k: rc(o1.at[q],o1.at[q],d1,k,zp(k))
    each(ZC,lambda k: gd(k).start())
    each(Y,lambda k: my(k).wait())
    for m in range(MB):
        vdg=vdg+jnp.dot(mall[m],mem_ref[m*BLK:(m+1)*BLK,:],preferred_element_type=f32)
    split(g2,0,vdg)
    g2[14]=jnp.zeros((8,128),f32); g2[15]=jnp.zeros((8,128),f32)
    ha=lambda k: rc(g2.at[lax.rem(q+k,ZC)],r2.at[k],a2,k,zp(k))
    each(ZC,lambda k: ha(k).start())
    each(ZC,lambda k: ha(k).wait())
    acc=g2[q]
    for k in range(1,ZC): acc=acc+r2[k]
    x2[x]=acc
    hb=lambda k: rc(x2.at[x],x2.at[x],b2,k,xp(k))
    each(X,lambda k: hb(k).start())
    each(X,lambda k: hb(k).wait())
    o2[q]=x2[0]+x2[1]+x2[2]+x2[3]
    hd=lambda k: rc(o2.at[q],o2.at[q],d2,k,zp(k))
    each(ZC,lambda k: hd(k).start())
    each(Y,lambda k: ly(k).wait())
    for s in range(Y):
        logit_out[:,s*BLK:(s+1)*BLK]=lall[s]
    each(ZC,lambda k: gd(k).wait())
    for k in range(15):
        for i in range(2):
            grad_out[i*8:(i+1)*8,k*128:(k+1)*128]=o1[k,i]
    each(ZC,lambda k: hd(k).wait())
    for k in range(14):
        grad_out[(k%2)*8:(k%2)*8+8,(15+k//2)*128:(16+k//2)*128]=o2[k]

def reduce_all(w,cols,qug,vug,mcot,slab,mem):
    vm=pl.BlockSpec(memory_space=pltpu.VMEM)
    wide=qug.shape[1]
    V=pltpu.VMEM
    sem=lambda n: pltpu.SemaphoreType.DMA((2,n))
    return pl.pallas_call(reduce_kernel,
        in_specs=[pl.BlockSpec(memory_space=pltpu.SMEM)]+[vm]*6,
        out_specs=[vm,vm],
        out_shape=[jax.ShapeDtypeStruct((TAGS,slab.shape[0]),f32),jax.ShapeDtypeStruct((RANK,3*wide+HD),f32)],
        scratch_shapes=[V((X,ZC,RANK,BLK),f32),V((MB,ZC,RANK,BLK),f32),V((Y,ZC,RANK,BLK),f32),V((ZC,RANK,BLK),f32),V((ZC,RANK,BLK),f32),V((MB,RANK,BLK),bf16),
            V((Y,TAGS+2*RANK,BLK),f32),V((8,128),f32),V((Y,TAGS,BLK),f32),V((Y,2*RANK,BLK),bf16),
            V((32,8,128),f32),V((ZC,2,8,128),f32),V((X,2,8,128),f32),V((ZC,2,8,128),f32),
            V((16,8,128),f32),V((ZC,8,128),f32),V((X,8,128),f32),V((ZC,8,128),f32),
            sem(X),sem(Y),sem(ZC),sem(Y),sem(Y),sem(Y),sem(Y),sem(ZC),sem(X),sem(ZC),sem(ZC),sem(X),sem(ZC)],
        compiler_params=pltpu.CompilerParams(collective_id=1,has_side_effects=True,vmem_limit_bytes=32*2**20),
    )(w,cols,qug,vug,mcot,slab,mem)

UNITS=8

def gather_kernel(mem_ref, slab_ref, wq_ref, wk_ref, wv_ref, qdown_ref, vdown_ref, qup_ref, vup_ref, ret_ref,
                  pool, q_out, k_out, v_out, low_out, asked_out,
                  feat, wq, wkv, stage, mine, ysem, ssem, rsem, lsem, osem, xsem):
    t=lax.axis_index("tm"); y=lax.axis_index("heads")
    x=lax.div(t,ZC); z=lax.rem(lax.div(t,2),Z); c=lax.rem(t,2)
    def tm(xx,zz,cc): return (xx*Z+zz)*2+cc
    def devx(k): return (tm(lax.rem(x+k,X),z,c),y)
    def devz(d): return (tm(x,lax.rem(z+d+Z,Z),c),y)
    devc=(tm(x,z,1-c),y)
    def devy(d): return (t,lax.rem(y+d+Y,Y))
    def loop(lo,hi,do):
        def body(k,_):
            do(k); return 0
        lax.fori_loop(lo,hi,body,0)
    bar=pltpu.get_barrier_semaphore()
    def greet(dev): pl.semaphore_signal(bar,inc=1,device_id=dev,device_id_type=MESH)
    loop(1,X,lambda k: greet(devx(k)))
    for d in (1,-1):
        greet(devz(d)); greet(devy(d))
    greet(devc)
    loads=[pltpu.make_async_copy(wk_ref,wkv.at[:,0:HD],lsem.at[0]),pltpu.make_async_copy(wv_ref,wkv.at[:,HD:2*HD],lsem.at[1]),pltpu.make_async_copy(wq_ref,wq,lsem.at[2])]
    loads[0].start(); loads[1].start()
    def rows_of(u):
        return (mem_ref if u<MB else slab_ref).at[pl.ds((u%MB)*BLK,BLK)]
    own=lambda u: pltpu.make_async_copy(rows_of(u),feat.at[u,y],osem.at[u])
    for u in range(UNITS): own(u).start()
    mine[...]=jnp.zeros_like(mine)
    mine[0:MB,0:TOP]=ret_ref[...]
    loads[2].start()
    pl.semaphore_wait(bar,X-1+5)

    def rc(src,dst,s,r,dev):
        return pltpu.make_async_remote_copy(src_ref=src,dst_ref=dst,send_sem=s,recv_sem=r,device_id=dev,device_id_type=MESH)
    left=lax.rem(y+Y-1,Y); right=lax.rem(y+1,Y); far=lax.rem(y+2,Y)
    H=BLK//2
    def y_first(u): return [rc(rows_of(u),feat.at[u,y],ysem.at[0,u,0],ysem.at[1,u,0],devy(1)),
                            rc(rows_of(u),feat.at[u,y],ysem.at[0,u,1],ysem.at[1,u,1],devy(-1))]
    def y_pass(u): return [rc(feat.at[u,left,pl.ds(0,H)],feat.at[u,left,pl.ds(0,H)],ysem.at[0,u,2],ysem.at[1,u,2],devy(1)),
                           rc(feat.at[u,right,pl.ds(H,H)],feat.at[u,right,pl.ds(H,H)],ysem.at[0,u,3],ysem.at[1,u,3],devy(-1))]
    def start(cs):
        for cp in cs: cp.start()
    asked=lambda k: rc(mine,asked_out.at[k],xsem.at[0,k],xsem.at[1,k],devx(k))

    def bid(xx,zz,cc,b): return tm(xx,zz,cc)*MB+b
    def at_x(k): return lax.rem(x+X-k,X)
    def at_z(d,l): return lax.rem(z+Z-d*l,Z)
    def sent(b,i): return ssem.at[b,i]
    def share(b,i,g): rc(pool.at[g],pool.at[g],sent(b,i),rsem.at[g],devc).start()
    def move(b,i,g,dev): rc(pool.at[g],pool.at[g],sent(b,i),rsem.at[g],dev).start()
    def arrive(g): rc(pool.at[g],pool.at[g],ssem.at[0,0],rsem.at[g],devc).wait_recv()
    def begin(b):
        g=bid(x,z,c,b)
        src=stage.at[b]
        loop(1,X,lambda k: rc(src,pool.at[g],sent(b,k-1),rsem.at[g],devx(k)).start())
        rc(src,pool.at[g],sent(b,3),rsem.at[g],devz(1)).start()
        rc(src,pool.at[g],sent(b,4),rsem.at[g],devz(-1)).start()
        rc(src,pool.at[g],sent(b,35),rsem.at[g],devc).start()
        pltpu.make_async_copy(src,pool.at[g],lsem.at[3+b]).start()
    def core0(b,phase):
        if phase==1:
            def go(k):
                g=bid(at_x(k),z,0,b)
                arrive(g)
                move(b,3+2*k,g,devz(1)); move(b,4+2*k,g,devz(-1)); share(b,35+k,g)
            loop(1,X,go)
        elif phase in (2,3,4):
            l=phase-1
            def go(k):
                xx=at_x(k)
                for i,d in enumerate((1,-1)):
                    g=bid(xx,at_z(d,l),0,b)
                    arrive(g)
                    if l<3:
                        move(b,3+8*l+2*k+i,g,devz(d))
                    else:
                        pl.when((xx<2) if d==1 else (xx>=2))(lambda g=g,d=d: move(b,27+k,g,devz(d)))
                    share(b,39+8*(l-1)+2*k+i,g)
            loop(0,X,go)
        else:
            def go(k):
                g=bid(at_x(k),at_z(1,4),0,b)
                arrive(g)
                share(b,63+k,g)
            loop(0,X,go)
    def core1(b,phase):
        def spread(j,g):
            loop(1,X,lambda k: move(b,8+3*j+k,g,devx(k)))
        if phase in (1,2,3):
            l=phase
            for i,d in enumerate((1,-1)):
                g=bid(x,at_z(d,l),1,b)
                arrive(g)
                if l<3: move(b,3+2*l+i,g,devz(d))
                elif (b%2==0)==(d==1): move(b,9,g,devz(d))
                spread(2*l-1+i,g)
                share(b,35+2*l-1+i,g)
        elif phase==4:
            g=bid(x,at_z(1,4),1,b)
            arrive(g); spread(7,g); share(b,35+7,g)
        else:
            def go(j):
                k=lax.div(j,Z)+1
                g=bid(at_x(k),lax.rem(z+j,Z),1,b)
                arrive(g)
                share(b,43+j,g)
            loop(0,3*Z,go)
    def step(b,phase):
        pl.when(c==0)(lambda: core0(b,phase))
        pl.when(c==1)(lambda: core1(b,phase))

    def project(u):
        own(u).wait()
        if u==0:
            loads[0].wait(); loads[1].wait()
        if u==MB: loads[2].wait()
        memory=u<MB
        pair=jnp.zeros((BLK,2*HD),f32)
        low=jnp.zeros((RANK if memory else 2*RANK,BLK),f32)
        wide=wq.shape[1]
        for h in range(Y):
            cols=slice(h*wide,(h+1)*wide)
            piece=feat[u,h]
            pair=pair+jnp.dot(piece,wkv[cols,:],preferred_element_type=f32)
            down=vdown_ref[:,cols] if memory else jnp.concatenate([qdown_ref[:,cols],vdown_ref[:,cols]],axis=0)
            low=low+lax.dot_general(down,piece,NT,preferred_element_type=f32)
        low=low.astype(bf16)
        keys=pair[:,:HD].astype(bf16)
        values=(pair[:,HD:]+lax.dot_general(low[-RANK:],vup_ref[...],TN,preferred_element_type=f32)).astype(bf16)
        if memory:
            stage[u,0:BLK,:]=keys
            stage[u,BLK:2*BLK,:]=values
            stage[u,2*BLK:,:]=low
        else:
            b=u-MB
            rows=slice(b*BLK,(b+1)*BLK)
            k_out[rows,:]=keys
            v_out[rows,:]=values
            low_out[:,rows]=low
            acc=lax.dot_general(low[:RANK],qup_ref[...],TN,preferred_element_type=f32)
            for h in range(Y):
                acc=acc+jnp.dot(feat[u,h],wq[h*wide:(h+1)*wide,:],preferred_element_type=f32)
            q_out[rows,:]=acc.astype(bf16)

    start(y_first(0)); start(y_first(1))
    loop(1,X,lambda k: asked(k).start())
    asked_out[0]=mine[...]
    middle={1:[(0,1),(0,2)],2:[(0,3),(0,4)],3:[(1,2)],4:[(1,4)],5:[(2,2)],6:[(2,4)],7:[(3,3)]}
    end={2:[(0,5),(1,1)],3:[(1,3)],4:[(1,5),(2,1)],5:[(2,3)],6:[(2,5),(3,1),(3,2)],7:[(3,4),(3,5)]}
    for u in range(UNITS):
        for cp in y_first(u): cp.wait_recv()
        start(y_pass(u))
        if u+2<UNITS: start(y_first(u+2))
        for b,p in middle.get(u,[]): step(b,p)
        for cp in y_pass(u): cp.wait_recv()
        project(u)
        if u<MB: begin(u)
        for b,p in end.get(u,[]): step(b,p)
    loop(0,X*Z*MB,lambda j: arrive(bid(lax.div(j,Z*MB),lax.rem(lax.div(j,MB),Z),1-c,lax.rem(j,MB))))
    loop(1,X,lambda k: asked(k).wait())
    for u in range(UNITS):
        for cp in y_first(u)+y_pass(u): cp.wait_send()
    def gone(b,i): rc(stage.at[0],pool.at[0],ssem.at[b,i],rsem.at[0],devc).wait_send()
    for b in range(MB):
        pltpu.make_async_copy(stage.at[b],pool.at[0],lsem.at[3+b]).wait()
        loop(35,67,lambda i: gone(b,i))
        @pl.when(c==0)
        def _():
            loop(0,31,lambda i: gone(b,i))
        @pl.when(c==1)
        def _():
            loop(0,10,lambda i: gone(b,i))
            loop(12,33,lambda i: gone(b,i))

def gather_all(mem,slab,wq,wk,wv,qdown,vdown,qup,vup,ret):
    vm=pl.BlockSpec(memory_space=pltpu.VMEM); hbm=pl.BlockSpec(memory_space=pl.ANY)
    n=slab.shape[0]; wide=wq.shape[1]
    S=jax.ShapeDtypeStruct; V=pltpu.VMEM; D=pltpu.SemaphoreType.DMA
    return pl.pallas_call(gather_kernel,
        in_specs=[hbm]*5+[vm]*5,
        out_specs=[hbm]+[vm]*5,
        out_shape=[S((OWNERS*MB,ROWS,HD),bf16),S((n,wide),bf16),S((n,HD),bf16),S((n,HD),bf16),S((2*RANK,n),bf16),S((X,8,128),jnp.int32)],
        scratch_shapes=[V((UNITS,Y,BLK,wide),bf16),V(wq.shape,bf16),V((wq.shape[0],2*HD),bf16),V((MB,ROWS,HD),bf16),V((8,128),jnp.int32),
            D((2,UNITS,4)),D((MB,68)),D((OWNERS*MB,)),D((3+MB,)),D((UNITS,)),D((2,X))],
        compiler_params=pltpu.CompilerParams(collective_id=2,has_side_effects=True,vmem_limit_bytes=40*2**20),
    )(mem,slab,wq,wk,wv,qdown,vdown,qup,vup,ret)

def local(slab_tokens,memory,query_weight,key_weight,value_weight,query_down,query_up,value_down,value_up,tag_weight,retrieval,boundary,grad_tags):
    x,y,q=place()
    pool,queries,keys,values,low_t,asked=gather_all(memory,slab_tokens,query_weight,key_weight,value_weight,query_down,value_down,query_up,value_up,retrieval)
    blocks=x*ZC*MB+jnp.arange(ZC*MB,dtype=jnp.int32)
    w=jnp.any(asked[:,:MB,:TOP].reshape(X,-1)[:,:,None]==blocks[None,None,:],axis=1).astype(f32)
    cols,qug,vug,mcot=attend(retrieval,boundary,queries,keys,values,low_t,grad_tags.T,tag_weight,tag_weight.T,query_up,value_up,pool)
    logits,grads=reduce_all(w,cols,qug,vug,mcot,slab_tokens,memory)
    wide=qug.shape[1]
    return logits.T,grads[:,:wide],grads[:,wide:2*wide],grads[:,2*wide+HD:],grads[:,2*wide:2*wide+HD]


def solution(mesh):
    in_specs=(P("tm","heads"),P("tm","heads"),P(None,"heads"),P(None,"heads"),P(None,"heads"),P(),P(None,"heads"),P(),P(None,"heads"),P("heads",None),P("tm",None),P("tm"),P("tm",None))
    out_specs=(P("tm",None),P(None,"heads"),P(None,"heads"),P(None,"heads"),P(None,"heads"))
    return jax.shard_map(local,mesh=mesh,in_specs=in_specs,out_specs=out_specs,check_vma=False)
```

```python
import functools
import jax, jax.numpy as jnp
from jax import lax
from jax.sharding import PartitionSpec as P
from jax.experimental import pallas as pl
from jax.experimental.pallas import tpu as pltpu
BLK=128; HD=128; TOP=8; RANK=16; TAGS=8
HIGHEST=lax.Precision.HIGHEST
NT=(((1,),(1,)),((),()))
TN=(((0,),(0,)),((),()))
f32=jnp.float32; bf16=jnp.bfloat16
MB=4; OWNERS=64; ROWS=272; CH=384; X=4; Y=4; Z=8; ZC=16; LOG2E=1.4426950408889634; MESH=pl.DeviceIdType.MESH
def attend_kernel(ret,bnd, q_hbm, kl_hbm, vl_hbm, low_hbm, gt_hbm, twt_hbm, qup_hbm, vup_hbm, pool_ref,
                  cols_ref, qug_ref, vug_ref, mcot_ref,
                  q_ref, kl_ref, vl_ref, low_ref, gt_ref, twt_ref, qup_ref, vup_ref,
                  land, kk, vv, lt, qs, gm, gs, st, pb, at, qg, vg, mc, sems, lsem):
    c=pl.program_id(0)
    heads=q_ref.shape[1]//HD
    wide=heads*BLK
    nkeys=(TOP+1)*BLK
    z=lax.rem(lax.div(lax.axis_index("tm"),2),Z)
    def fetch(i):
        g=ret[lax.div(i,TOP),lax.rem(i,TOP)]
        o=lax.div(g,MB)
        d=lax.rem(lax.rem(lax.div(o,2),Z)+Z-z,Z)
        slot=jnp.where(d==0,0,jnp.where(d<Z//2,2*d,jnp.where(d==Z//2,Z-1,2*(Z-d)-1)))
        return pltpu.make_async_copy(pool_ref.at[lax.rem(g,MB),lax.rem(o,2),lax.div(o,ZC),slot], land.at[i], sems.at[i])
    loads=[pltpu.make_async_copy(src,dst,lsem.at[i]) for i,(src,dst) in enumerate([(q_hbm,q_ref),(kl_hbm,kl_ref),(vl_hbm,vl_ref),(low_hbm,low_ref),(gt_hbm,gt_ref),(twt_hbm,twt_ref),(qup_hbm,qup_ref),(vup_hbm,vup_ref)])]
    @pl.when(c==0)
    def _():
        for cp in loads: cp.start()
        def go(i,_):
            fetch(i).start(); return 0
        lax.fori_loop(0,4*TOP,go,0)
        qug_ref[...]=jnp.zeros_like(qug_ref)
        vug_ref[...]=jnp.zeros_like(vug_ref)
        mc[...]=jnp.zeros_like(mc)
        for cp in loads: cp.wait()
    rows=pl.ds(pl.multiple_of(c*BLK,BLK),BLK)
    part=gt_ref[:,rows]
    terms=[]
    for _ in range(3):
        low=part.astype(bf16).astype(f32)
        terms.append(low); part=part-low
    grads=jnp.concatenate(terms+[jnp.zeros_like(part)],axis=0).astype(bf16)
    tags=jnp.concatenate([twt_ref[...].astype(f32)]*4,axis=0).astype(bf16)
    across=lax.dot_general(tags,grads,TN,preferred_element_type=f32).astype(bf16)
    down=lax.dot_general(grads,tags,TN,preferred_element_type=f32).astype(bf16)
    for h in range(heads):
        cols=slice(h*HD,(h+1)*HD)
        gm[:,cols]=across[cols,:]
        gs[cols,:]=down[:,cols]
        qs[cols,:]=q_ref[rows,cols]
    for s in range(TOP):
        i=c*TOP+s
        fetch(i).wait()
        kk[s*BLK:(s+1)*BLK,:]=land[i,0:128,:]
        vv[s*BLK:(s+1)*BLK,:]=land[i,128:256,:]
        lt[:,s*BLK:(s+1)*BLK]=land[i,256:272,:]
    own=slice(TOP*BLK,nkeys)
    kk[own,:]=kl_ref[rows,:]
    vv[own,:]=vl_ref[rows,:]
    lt[:,own]=low_ref[RANK:,rows]
    edge=bnd[c]
    m=jnp.full((1,wide),-jnp.inf,f32)
    scale=HD**-0.5
    n_ch=nkeys//CH
    for j in range(n_ch):
        r=slice(j*CH,(j+1)*CH)
        s=lax.dot_general(kk[r,:],qs[...],NT,preferred_element_type=f32)
        if j==n_ch-1:
            key=lax.broadcasted_iota(jnp.int32,(BLK,BLK),0)
            row=lax.broadcasted_iota(jnp.int32,(BLK,BLK),1)
            seen=(key<=row)&((key>=edge)|(row<edge))
            bias=jnp.where(seen,0.0,-jnp.inf).astype(f32)
            bias=jnp.concatenate([bias]*heads,axis=1)
            last=s[CH-BLK:]+bias
            s=jnp.concatenate([s[:CH-BLK],last],axis=0)
        st[r,:]=s
        m=jnp.maximum(m,jnp.max(s,axis=0,keepdims=True))
    tot=jnp.zeros((1,wide),f32)
    for j in range(n_ch):
        r=slice(j*CH,(j+1)*CH)
        e=jnp.exp2((st[r,:]-m)*(scale*LOG2E))
        st[r,:]=e
        tot=tot+jnp.sum(e,axis=0,keepdims=True)
    inv=1.0/tot
    acc=jnp.zeros((HD,wide),f32)
    for j in range(n_ch):
        r=slice(j*CH,(j+1)*CH)
        pl_=(st[r,:]*inv).astype(bf16)
        pb[r,:]=pl_
        acc=acc+lax.dot_general(vv[r,:],pl_,TN,preferred_element_type=f32)
    att=acc.astype(bf16)
    at[...]=att
    dot_row=jnp.sum(gm[...].astype(f32)*att.astype(f32),axis=0,keepdims=True)
    inv=inv*scale
    acc=jnp.zeros((HD,wide),f32)
    for j in range(n_ch):
        r=slice(j*CH,(j+1)*CH)
        pg=jnp.dot(vv[r,:],gm[...],preferred_element_type=f32)
        sgr=((st[r,:]*inv)*(pg-dot_row)).astype(bf16)
        acc=acc+lax.dot_general(kk[r,:],sgr,TN,preferred_element_type=f32)
        vg[r,:]=jnp.dot(pb[r,:],gs[...],preferred_element_type=f32)
    qg[...]=acc.astype(bf16)
    logits=jnp.zeros((TAGS,BLK),f32)
    qcot=jnp.zeros((RANK,BLK),f32)
    for h in range(heads):
        cols=slice(h*HD,(h+1)*HD)
        qgh=qg[:,cols]
        logits=logits+jnp.dot(twt_ref[:,cols],at[:,cols],preferred_element_type=f32)
        qcot=qcot+jnp.dot(qup_ref[:,cols],qgh,preferred_element_type=f32)
        qug_ref[:,cols]+=lax.dot_general(low_ref[:RANK,rows],qgh,NT,preferred_element_type=f32)
    cols_ref[c,0:TAGS,:]=logits
    cols_ref[c,TAGS:TAGS+RANK,:]=qcot
    whole=vg[...]
    high=whole.astype(bf16)
    rest=(whole-high.astype(f32)).astype(bf16)
    up=vup_ref[...]
    cot=lax.dot_general(up,high,NT,preferred_element_type=f32)+lax.dot_general(up,rest,NT,preferred_element_type=f32)
    cols_ref[c,TAGS+RANK:,:]=cot[:,own]
    for s in range(TOP):
        o=lax.div(ret[c,s],MB)
        zo=lax.rem(lax.div(o,2),Z)
        mc[lax.div(o,ZC)*ZC+lax.rem(zo,Y)*4+lax.div(zo,Y)*2+lax.rem(o,2)]+=cot[:,s*BLK:(s+1)*BLK]
    side=lt[...]
    vug_ref[...]+=jnp.dot(side,high,preferred_element_type=f32)+jnp.dot(side,rest,preferred_element_type=f32)
    @pl.when(c==pl.num_programs(0)-1)
    def _():
        mcot_ref[...]=mc[...].astype(bf16)

def attend(retrieval,boundary,q,kl,vl,low_t,grad_t,tw_t,qup,vup,pool):
    n=q.shape[0]; wide=q.shape[1]; nk=(TOP+1)*BLK; spans=n//BLK
    vm=pl.BlockSpec(memory_space=pltpu.VMEM)
    V=pltpu.VMEM
    shp=lambda *s: jax.ShapeDtypeStruct(s,f32)
    return pl.pallas_call(attend_kernel,
        grid_spec=pltpu.PrefetchScalarGridSpec(num_scalar_prefetch=2,grid=(spans,),
            in_specs=[pl.BlockSpec(memory_space=pl.ANY)]*9,
            out_specs=[vm]*4,
            scratch_shapes=[V(a.shape,a.dtype) for a in (q,kl,vl,low_t,grad_t,tw_t,qup,vup)]+[
              V((spans*TOP,ROWS,HD),bf16),V((nk,HD),bf16),V((nk,HD),bf16),V((RANK,nk),bf16),
              V((wide,HD),bf16),V((HD,wide),bf16),V((wide,HD),bf16),
              V((nk,wide),f32),V((nk,wide),bf16),
              V((HD,wide),bf16),V((HD,wide),bf16),V((nk,HD),f32),V((OWNERS,RANK,BLK),f32),
              pltpu.SemaphoreType.DMA((spans*TOP,)),pltpu.SemaphoreType.DMA((8,))]),
        out_shape=[shp(spans,TAGS+2*RANK,BLK),shp(RANK,wide),shp(RANK,HD),jax.ShapeDtypeStruct((OWNERS,RANK,BLK),bf16)],
        compiler_params=pltpu.CompilerParams(vmem_limit_bytes=60*2**20,dimension_semantics=("arbitrary",)),
    )(retrieval,boundary,q,kl,vl,low_t,grad_t,tw_t,qup,vup,pool)

def place():
    t=lax.axis_index("tm"); y=lax.axis_index("heads")
    return lax.div(t,ZC), y, lax.rem(t,ZC)

def reduce_kernel(w_ref, cols_ref, qug_ref, vug_ref, mcot_ref, slab_hbm, mem_hbm,
                  logit_out, grad_out,
                  slab_ref, mem_ref, xbuf, tbuf, zbuf, mall, cbuf, lall, call, g1, r1, x1, o1, g2, r2, x2, o2,
                  xs, ys, zs, ms, cs, ls, ks, a1, b1, d1, a2, b2, d2, lsem):
    x,y,q=place()
    def xp(k): return (lax.rem(x+k,X)*ZC+q, y)
    def yp(k): return (x*ZC+q, lax.rem(y+k,Y))
    def zp(k): return (x*ZC+lax.rem(q+k,ZC), y)
    def xyp(k): return (lax.rem(x+lax.div(k,Y),X)*ZC+q, lax.rem(y+lax.rem(k,Y),Y))
    def each(n,do):
        def body(k,_):
            do(k); return 0
        lax.fori_loop(1,n,body,0)
    def rc(src,dst,sems,k,dev):
        return pltpu.make_async_remote_copy(src_ref=src,dst_ref=dst,send_sem=sems.at[0,k],recv_sem=sems.at[1,k],device_id=dev,device_id_type=MESH)
    loads=[pltpu.make_async_copy(slab_hbm,slab_ref,lsem.at[0]),pltpu.make_async_copy(mem_hbm,mem_ref,lsem.at[1])]
    for cp in loads: cp.start()
    bar=pltpu.get_barrier_semaphore()
    each(X*Y,lambda k: pl.semaphore_signal(bar,inc=1,device_id=xyp(k),device_id_type=MESH))
    each(ZC,lambda k: pl.semaphore_signal(bar,inc=1,device_id=zp(k),device_id_type=MESH))
    pl.semaphore_wait(bar,X*Y+ZC-2)
    def slots(k): return pl.ds(lax.rem(x+lax.div(k,Y),X)*ZC+lax.rem(y+lax.rem(k,Y),Y)*4,4)
    mx=lambda k: rc(mcot_ref.at[slots(k)],xbuf.at[k],xs,k,xyp(k))
    cy=lambda k: rc(cols_ref.at[lax.rem(y+k,Y)],cbuf.at[k],cs,k,yp(k))
    each(X*Y,lambda k: mx(k).start())
    each(Y,lambda k: cy(k).start())
    each(Y,lambda k: cy(k).wait())
    total=cols_ref[y]+cbuf[1]+cbuf[2]+cbuf[3]
    lall[y]=total[:TAGS]
    call[y]=total[TAGS:].astype(bf16)
    ly=lambda k: rc(lall.at[y],lall.at[y],ls,k,yp(k))
    ky=lambda k: rc(call.at[y],call.at[y],ks,k,yp(k))
    each(Y,lambda k: ky(k).start())
    each(Y,lambda k: ly(k).start())
    xbuf[0]=mcot_ref[slots(0)]
    each(X*Y,lambda k: mx(k).wait())
    def owner(j):
        half,core=(j//2,j%2) if isinstance(j,int) else (lax.div(j,2),lax.rem(j,2))
        return (y+Y*half)*2+core
    def expand(j,_):
        parts=[]
        for k in range(X):
            s=xbuf[Y*k,j].astype(f32)
            for i in range(1,Y): s=s+xbuf[Y*k+i,j].astype(f32)
            parts.append(s)
        for m in range(MB):
            at=owner(j)*MB+m
            acc=parts[0]*w_ref[0,at]
            for k in range(1,X):
                acc=acc+parts[k]*w_ref[k,at]
            tbuf[j,m]=acc.astype(bf16)
        return 0
    lax.fori_loop(0,4,expand,0)
    home=lax.rem(lax.div(q,2),Y)==y
    for j in range(4):
        @pl.when(owner(j)!=q)
        def _():
            pltpu.make_async_remote_copy(src_ref=tbuf.at[j],dst_ref=zbuf.at[q],send_sem=ys.at[0,j],recv_sem=zs.at[1,q],device_id=(x*ZC+owner(j),y),device_id_type=MESH).start()
    each(Y,lambda k: ky(k).wait())
    def split(ref,first,value):
        for j in range(value.shape[1]//128):
            ref[first+2*j]=value[0:8,j*128:(j+1)*128]
            ref[first+2*j+1]=value[8:16,j*128:(j+1)*128]
    qdg=jnp.zeros(qug_ref.shape,f32); vdg=jnp.zeros(qug_ref.shape,f32)
    loads[0].wait()
    for s in range(Y):
        piece=slab_ref[s*BLK:(s+1)*BLK,:]
        qdg=qdg+jnp.dot(call[s,0:RANK],piece,preferred_element_type=f32)
        vdg=vdg+jnp.dot(call[s,RANK:],piece,preferred_element_type=f32)
    split(g1,0,qdg); split(g1,14,qug_ref[...]); split(g1,28,vug_ref[...])
    g1[30]=jnp.zeros((8,128),f32); g1[31]=jnp.zeros((8,128),f32)
    ga=lambda k: rc(g1.at[pl.ds(lax.rem(q+k,ZC)*2,2)],r1.at[k],a1,k,zp(k))
    each(ZC,lambda k: ga(k).start())
    from_y=lax.rem(lax.div(q,2),Y)
    my=lambda k: rc(mall,mall,ms,k,yp(k))
    @pl.when(home)
    def _():
        zbuf[q]=tbuf[lax.div(q,8)*2+lax.rem(q,2)]
        def arrive(s,_):
            @pl.when(s!=q)
            def _(): rc(tbuf.at[0],zbuf.at[s],zs,s,(x*ZC+q,y)).wait_recv()
            return 0
        lax.fori_loop(0,ZC,arrive,0)
        for m in range(MB):
            acc=zbuf[0,m].astype(f32)
            for s in range(1,ZC): acc=acc+zbuf[s,m].astype(f32)
            mall[m]=acc.astype(bf16)
        each(Y,lambda k: my(k).start())
    each(ZC,lambda k: ga(k).wait())
    acc=g1[pl.ds(q*2,2)]
    for k in range(1,ZC): acc=acc+r1[k]
    x1[x]=acc
    gb=lambda k: rc(x1.at[x],x1.at[x],b1,k,xp(k))
    each(X,lambda k: gb(k).start())
    @pl.when(jnp.logical_not(home))
    def _(): my(lax.rem(y+Y-from_y,Y)).wait_recv()
    loads[1].wait()
    for m in range(MB):
        vdg=vdg+jnp.dot(mall[m],mem_ref[m*BLK:(m+1)*BLK,:],preferred_element_type=f32)
    split(g2,0,vdg)
    g2[14]=jnp.zeros((8,128),f32); g2[15]=jnp.zeros((8,128),f32)
    ha=lambda k: rc(g2.at[lax.rem(q+k,ZC)],r2.at[k],a2,k,zp(k))
    each(ZC,lambda k: ha(k).start())
    each(X,lambda k: gb(k).wait())
    o1[q]=x1[0]+x1[1]+x1[2]+x1[3]
    gd=lambda k: rc(o1.at[q],o1.at[q],d1,k,zp(k))
    each(ZC,lambda k: gd(k).start())
    each(ZC,lambda k: ha(k).wait())
    acc=g2[q]
    for k in range(1,ZC): acc=acc+r2[k]
    x2[x]=acc
    hb=lambda k: rc(x2.at[x],x2.at[x],b2,k,xp(k))
    each(X,lambda k: hb(k).start())
    each(X,lambda k: hb(k).wait())
    o2[q]=x2[0]+x2[1]+x2[2]+x2[3]
    hd=lambda k: rc(o2.at[q],o2.at[q],d2,k,zp(k))
    each(ZC,lambda k: hd(k).start())
    each(Y,lambda k: ly(k).wait())
    for s in range(Y):
        logit_out[:,s*BLK:(s+1)*BLK]=lall[s]
    for j in range(4):
        @pl.when(owner(j)!=q)
        def _(): pltpu.make_async_remote_copy(src_ref=tbuf.at[j],dst_ref=zbuf.at[q],send_sem=ys.at[0,j],recv_sem=zs.at[1,q],device_id=(x*ZC+owner(j),y),device_id_type=MESH).wait_send()
    @pl.when(home)
    def _(): each(Y,lambda k: my(k).wait_send())
    each(ZC,lambda k: gd(k).wait())
    for k in range(15):
        for i in range(2):
            grad_out[i*8:(i+1)*8,k*128:(k+1)*128]=o1[k,i]
    each(ZC,lambda k: hd(k).wait())
    for k in range(14):
        grad_out[(k%2)*8:(k%2)*8+8,(15+k//2)*128:(16+k//2)*128]=o2[k]

def reduce_all(w,cols,qug,vug,mcot,slab,mem):
    vm=pl.BlockSpec(memory_space=pltpu.VMEM)
    wide=qug.shape[1]
    V=pltpu.VMEM
    sem=lambda n: pltpu.SemaphoreType.DMA((2,n))
    return pl.pallas_call(reduce_kernel,
        in_specs=[pl.BlockSpec(memory_space=pltpu.SMEM)]+[vm]*4+[pl.BlockSpec(memory_space=pl.ANY)]*2,
        out_specs=[vm,vm],
        out_shape=[jax.ShapeDtypeStruct((TAGS,slab.shape[0]),f32),jax.ShapeDtypeStruct((RANK,3*wide+HD),f32)],
        scratch_shapes=[V(slab.shape,bf16),V(mem.shape,bf16),V((X*Y,4,RANK,BLK),bf16),V((4,MB,RANK,BLK),bf16),V((ZC,MB,RANK,BLK),bf16),V((MB,RANK,BLK),bf16),
            V((Y,TAGS+2*RANK,BLK),f32),V((Y,TAGS,BLK),f32),V((Y,2*RANK,BLK),bf16),
            V((32,8,128),f32),V((ZC,2,8,128),f32),V((X,2,8,128),f32),V((ZC,2,8,128),f32),
            V((16,8,128),f32),V((ZC,8,128),f32),V((X,8,128),f32),V((ZC,8,128),f32),
            sem(X*Y),sem(4),sem(ZC),sem(Y),sem(Y),sem(Y),sem(Y),sem(ZC),sem(X),sem(ZC),sem(ZC),sem(X),sem(ZC),pltpu.SemaphoreType.DMA((2,))],
        compiler_params=pltpu.CompilerParams(collective_id=1,has_side_effects=True,vmem_limit_bytes=60*2**20),
    )(w,cols,qug,vug,mcot,slab,mem)

UNITS=8
AHEAD=1
PLAN={(1, 0): [(0, 1)], (2, 0): [(1, 1), (0, 2)], (2, 1): [], (3, 0): [(2, 1), (1, 2), (0, 3)], (4, 0): [(3, 1), (2, 2), (1, 3), (0, 4)], (5, 0): [(3, 2), (2, 3), (1, 4), (0, 5)], (6, 0): [(3, 3), (2, 4), (1, 5)], (7, 0): [(3, 4), (2, 5)], (7, 1): [(3, 5)]}

def gather_kernel(mem_ref, slab_ref, wq_ref, wk_ref, wv_ref, qdown_hbm, vdown_hbm, qup_hbm, vup_hbm, ret_hbm,
                  pool, q_out, k_out, v_out, low_out, asked_out,
                  feat, wq, wkv, qdown_ref, vdown_ref, qup_ref, vup_ref, ret_ref, stage, mine, ysem, ssem, rsem, lsem, psem, osem, xsem):
    t=lax.axis_index("tm"); y=lax.axis_index("heads")
    x=lax.div(t,ZC); z=lax.rem(lax.div(t,2),Z); c=lax.rem(t,2)
    def tm(xx,zz,cc): return (xx*Z+zz)*2+cc
    xk=[lax.rem(x+k,X) for k in range(X)]
    devx=[(tm(xk[k],z,c),y) for k in range(X)]
    devz=[(tm(x,lax.rem(z+1,Z),c),y),(tm(x,lax.rem(z+Z-1,Z),c),y)]
    devc=(tm(x,z,1-c),y)
    devy=[(t,lax.rem(y+1,Y)),(t,lax.rem(y+Y-1,Y))]
    def rows_of(u):
        return (mem_ref if u<MB else slab_ref).at[pl.ds((u%MB)*BLK,BLK)]
    own=lambda u: pltpu.make_async_copy(rows_of(u),feat.at[u,y],osem.at[u])
    loads=[pltpu.make_async_copy(a,b,lsem.at[i]) for i,(a,b) in enumerate([(wk_ref,wkv.at[:,0:HD]),(wv_ref,wkv.at[:,HD:2*HD]),(vdown_hbm,vdown_ref),(vup_hbm,vup_ref),(ret_hbm,ret_ref),(wq_ref,wq),(qdown_hbm,qdown_ref),(qup_hbm,qup_ref)])]
    bar=pltpu.get_barrier_semaphore()
    for dev in devx[1:]+devz+devy+[devc]:
        pl.semaphore_signal(bar,inc=1,device_id=dev,device_id_type=MESH)
    for cp in loads: cp.start()
    for u in range(UNITS): own(u).start()
    mine[...]=jnp.zeros_like(mine)
    loads[4].wait()
    mine[0:MB,0:TOP]=ret_ref[...]
    pl.semaphore_wait(bar,X-1+5)

    def rc(src,dst,s,r,dev):
        return pltpu.make_async_remote_copy(src_ref=src,dst_ref=dst,send_sem=s,recv_sem=r,device_id=dev,device_id_type=MESH)
    left=lax.rem(y+Y-1,Y); right=lax.rem(y+1,Y)
    H=BLK//2
    def y_first(u): return [rc(rows_of(u),feat.at[u,y],ysem.at[0,u,i],ysem.at[1,u,i],devy[i]) for i in range(2)]
    def y_pass(u): return [rc(feat.at[u,left,pl.ds(0,H)],feat.at[u,left,pl.ds(0,H)],ysem.at[0,u,2],ysem.at[1,u,2],devy[0]),
                           rc(feat.at[u,right,pl.ds(H,H)],feat.at[u,right,pl.ds(H,H)],ysem.at[0,u,3],ysem.at[1,u,3],devy[1])]
    def start(cs):
        for cp in cs: cp.start()
    asked=lambda k: rc(mine,asked_out.at[k],xsem.at[0,k],xsem.at[1,k],devx[k])

    def part(b,cc,xs,zs): return pool.at[b,cc,xs,zs]
    every=pl.ds(0,X)
    GROUP=[pl.ds(0,1),pl.ds(1,2),pl.ds(3,2),pl.ds(5,2),pl.ds(7,1)]
    def share(b,cc,g): return rc(part(b,cc,every,GROUP[g]),part(b,cc,every,GROUP[g]),ssem.at[b,27+g],rsem.at[b,27+g],devc)
    def keep(b): return pltpu.make_async_copy(stage.at[b],pool.at[b,c,x,0],psem.at[b])
    def x_own(b,k): return rc(stage.at[b],pool.at[b,0,x,0],ssem.at[b,k-1],rsem.at[b,k],devx[k])
    def hop0(b,l,i):
        if l<3:
            src=0 if l==0 else 2*l-1+i
            return rc(part(b,0,every,src),part(b,0,every,2*l+1+i),ssem.at[b,3+2*l+i],rsem.at[b,4+2*l+i],devz[i])
        xs=pl.ds(2*i,2)
        return rc(part(b,0,xs,5+i),part(b,0,xs,7),ssem.at[b,9+i],rsem.at[b,10+i],devz[i])
    def core0(b,phase):
        if phase==1:
            for k in range(1,X): x_own(b,k).wait_recv()
            keep(b).wait()
            for i in range(2): hop0(b,0,i).start()
        else:
            l=phase-1
            for i in range(2):
                hop0(b,l-1,i).wait_recv()
                if l<4: hop0(b,l,i).start()
        share(b,0,phase-1).start()
    def hop1(b,l,i):
        src=stage.at[b] if l==0 else pool.at[b,1,x,2*l-1+i]
        return rc(src,pool.at[b,1,x,2*l+1+i if l<3 else 7],ssem.at[b,3+2*l+i if l<3 else 9],rsem.at[b,4+2*l+i if l<3 else 10],devz[i])
    def spread(b,g,k):
        src=part(b,1,x,GROUP[g])
        return rc(stage.at[pl.ds(b,1)] if g==0 else src,src,ssem.at[b,12+5*(k-1)+g],rsem.at[b,12+5*(k-1)+g],devx[k])
    def pass_on(b,g):
        for k in range(1,X): spread(b,g,k).wait_recv()
        share(b,1,g).start()
    def core1(b,phase):
        if phase<4:
            l=phase
            for i in range(2):
                hop1(b,l-1,i).wait_recv()
                if l<3 or b%2==i: hop1(b,l,i).start()
            for k in range(1,X): spread(b,l,k).start()
        elif phase==4:
            hop1(b,3,b%2).wait_recv()
            for k in range(1,X): spread(b,4,k).start()
        if phase==1: keep(b).wait()
        if phase in (2,3,4): pass_on(b,phase-2)
        if phase==5:
            pass_on(b,3); pass_on(b,4)
    def begin(b):
        keep(b).start()
        @pl.when(c==0)
        def _():
            for k in range(1,X): x_own(b,k).start()
        @pl.when(c==1)
        def _():
            for i in range(2): hop1(b,0,i).start()
            for k in range(1,X): spread(b,0,k).start()
    def step(b,phase):
        pl.when(c==0)(lambda: core0(b,phase))
        pl.when(c==1)(lambda: core1(b,phase))

    def project(u):
        own(u).wait()
        if u==0:
            for i in range(4): loads[i].wait()
        if u==MB:
            for i in range(5,8): loads[i].wait()
        memory=u<MB
        pair=jnp.zeros((BLK,2*HD),f32)
        low=jnp.zeros((RANK if memory else 2*RANK,BLK),f32)
        wide=wq.shape[1]
        for h in range(Y):
            cols=slice(h*wide,(h+1)*wide)
            piece=feat[u,h]
            pair=pair+jnp.dot(piece,wkv[cols,:],preferred_element_type=f32)
            down=vdown_ref[:,cols] if memory else jnp.concatenate([qdown_ref[:,cols],vdown_ref[:,cols]],axis=0)
            low=low+lax.dot_general(down,piece,NT,preferred_element_type=f32)
        low=low.astype(bf16)
        keys=pair[:,:HD].astype(bf16)
        values=(pair[:,HD:]+lax.dot_general(low[-RANK:],vup_ref[...],TN,preferred_element_type=f32)).astype(bf16)
        if memory:
            stage[u,0:BLK,:]=keys
            stage[u,BLK:2*BLK,:]=values
            stage[u,2*BLK:,:]=low
        else:
            b=u-MB
            rows=slice(b*BLK,(b+1)*BLK)
            k_out[rows,:]=keys
            v_out[rows,:]=values
            low_out[:,rows]=low
            acc=lax.dot_general(low[:RANK],qup_ref[...],TN,preferred_element_type=f32)
            for h in range(Y):
                acc=acc+jnp.dot(feat[u,h],wq[h*wide:(h+1)*wide,:],preferred_element_type=f32)
            q_out[rows,:]=acc.astype(bf16)

    for u in range(AHEAD): start(y_first(u))
    for k in range(1,X): asked(k).start()
    asked_out[0]=mine[...]
    for u in range(UNITS):
        for cp in y_first(u): cp.wait_recv()
        start(y_pass(u))
        if u+AHEAD<UNITS: start(y_first(u+AHEAD))
        for b,p in PLAN.get((u,0),[]): step(b,p)
        for cp in y_pass(u): cp.wait_recv()
        project(u)
        if u<MB: begin(u)
        for b,p in PLAN.get((u,1),[]): step(b,p)
    for k in range(1,X): asked(k).wait()
    for u in range(UNITS):
        for cp in y_first(u)+y_pass(u): cp.wait_send()
    for b in range(MB):
        for g in range(5):
            share(b,1-c,g).wait_recv()
            share(b,c,g).wait_send()
        @pl.when(c==0)
        def _():
            for k in range(1,X): x_own(b,k).wait_send()
            for l in range(4):
                for i in range(2): hop0(b,l,i).wait_send()
        @pl.when(c==1)
        def _():
            for l in range(3):
                for i in range(2): hop1(b,l,i).wait_send()
            hop1(b,3,b%2).wait_send()
            for g in range(5):
                for k in range(1,X): spread(b,g,k).wait_send()

def gather_all(mem,slab,wq,wk,wv,qdown,vdown,qup,vup,ret):
    vm=pl.BlockSpec(memory_space=pltpu.VMEM); hbm=pl.BlockSpec(memory_space=pl.ANY)
    n=slab.shape[0]; wide=wq.shape[1]
    S=jax.ShapeDtypeStruct; V=pltpu.VMEM; D=pltpu.SemaphoreType.DMA
    return pl.pallas_call(gather_kernel,
        in_specs=[hbm]*10,
        out_specs=[hbm]+[vm]*5,
        out_shape=[S((MB,2,X,Z,ROWS,HD),bf16),S((n,wide),bf16),S((n,HD),bf16),S((n,HD),bf16),S((2*RANK,n),bf16),S((X,8,128),jnp.int32)],
        scratch_shapes=[V((UNITS,Y,BLK,wide),bf16),V(wq.shape,bf16),V((wq.shape[0],2*HD),bf16),V(qdown.shape,bf16),V(vdown.shape,bf16),V(qup.shape,bf16),V(vup.shape,bf16),V(ret.shape,jnp.int32),
            V((MB,ROWS,HD),bf16),V((8,128),jnp.int32),
            D((2,UNITS,4)),D((MB,32)),D((MB,32)),D((8,)),D((MB,)),D((UNITS,)),D((2,X))],
        compiler_params=pltpu.CompilerParams(collective_id=2,has_side_effects=True,vmem_limit_bytes=60*2**20),
    )(mem,slab,wq,wk,wv,qdown,vdown,qup,vup,ret)

def local(slab_tokens,memory,query_weight,key_weight,value_weight,query_down,query_up,value_down,value_up,tag_weight,retrieval,boundary,grad_tags):
    x,y,q=place()
    pool,queries,keys,values,low_t,asked=gather_all(memory,slab_tokens,query_weight,key_weight,value_weight,query_down,value_down,query_up,value_up,retrieval)
    blocks=x*ZC*MB+jnp.arange(ZC*MB,dtype=jnp.int32)
    w=jnp.any(asked[:,:MB,:TOP].reshape(X,-1)[:,:,None]==blocks[None,None,:],axis=1).astype(f32)
    cols,qug,vug,mcot=attend(retrieval,boundary,queries,keys,values,low_t,grad_tags.T,tag_weight.T,query_up,value_up,pool)
    logits,grads=reduce_all(w,cols,qug,vug,mcot,slab_tokens,memory)
    wide=qug.shape[1]
    return logits.T,grads[:,:wide],grads[:,wide:2*wide],grads[:,2*wide+HD:],grads[:,2*wide:2*wide+HD]


def solution(mesh):
    in_specs=(P("tm","heads"),P("tm","heads"),P(None,"heads"),P(None,"heads"),P(None,"heads"),P(),P(None,"heads"),P(),P(None,"heads"),P("heads",None),P("tm",None),P("tm"),P("tm",None))
    out_specs=(P("tm",None),P(None,"heads"),P(None,"heads"),P(None,"heads"),P(None,"heads"))
    return jax.shard_map(local,mesh=mesh,in_specs=in_specs,out_specs=out_specs,check_vma=False)
```

```python
import functools
import jax, jax.numpy as jnp
from jax import lax
from jax.sharding import PartitionSpec as P
from jax.experimental import pallas as pl
from jax.experimental.pallas import tpu as pltpu
BLK=128; HD=128; TOP=8; RANK=16; TAGS=8
HIGHEST=lax.Precision.HIGHEST
NT=(((1,),(1,)),((),()))
TN=(((0,),(0,)),((),()))
f32=jnp.float32; bf16=jnp.bfloat16
MB=4; OWNERS=64; ROWS=272; CH=384; X=4; Y=4; Z=8; ZC=16; LOG2E=1.4426950408889634; MESH=pl.DeviceIdType.MESH
def attend_kernel(ret,bnd, q_hbm, kl_hbm, vl_hbm, low_hbm, gt_hbm, twt_hbm, qup_hbm, vup_hbm, pool_ref,
                  cols_ref, qug_ref, vug_ref, mcot_ref,
                  q_ref, kl_ref, vl_ref, low_ref, gt_ref, twt_ref, qup_ref, vup_ref,
                  land, kk, vv, lt, qs, gm, gs, st, pb, at, qg, vg, mc, sems, lsem):
    c=pl.program_id(0)
    heads=q_ref.shape[1]//HD
    wide=heads*BLK
    nkeys=(TOP+1)*BLK
    z=lax.rem(lax.div(lax.axis_index("tm"),2),Z)
    def fetch(i):
        g=ret[lax.div(i,TOP),lax.rem(i,TOP)]
        o=lax.div(g,MB)
        d=lax.rem(lax.rem(lax.div(o,2),Z)+Z-z,Z)
        slot=jnp.where(d==0,0,jnp.where(d<Z//2,2*d,jnp.where(d==Z//2,Z-1,2*(Z-d)-1)))
        return pltpu.make_async_copy(pool_ref.at[lax.rem(g,MB),lax.rem(o,2),lax.div(o,ZC),slot], land.at[i], sems.at[i])
    loads=[pltpu.make_async_copy(src,dst,lsem.at[i]) for i,(src,dst) in enumerate([(q_hbm,q_ref),(kl_hbm,kl_ref),(vl_hbm,vl_ref),(low_hbm,low_ref),(gt_hbm,gt_ref),(twt_hbm,twt_ref),(qup_hbm,qup_ref),(vup_hbm,vup_ref)])]
    @pl.when(c==0)
    def _():
        for cp in loads: cp.start()
        def go(i,_):
            fetch(i).start(); return 0
        lax.fori_loop(0,4*TOP,go,0)
        qug_ref[...]=jnp.zeros_like(qug_ref)
        vug_ref[...]=jnp.zeros_like(vug_ref)
        mc[...]=jnp.zeros_like(mc)
        for cp in loads: cp.wait()
    rows=pl.ds(pl.multiple_of(c*BLK,BLK),BLK)
    part=gt_ref[:,rows]
    terms=[]
    for _ in range(3):
        low=part.astype(bf16).astype(f32)
        terms.append(low); part=part-low
    grads=jnp.concatenate(terms+[jnp.zeros_like(part)],axis=0).astype(bf16)
    tags=jnp.concatenate([twt_ref[...].astype(f32)]*4,axis=0).astype(bf16)
    across=lax.dot_general(tags,grads,TN,preferred_element_type=f32).astype(bf16)
    down=lax.dot_general(grads,tags,TN,preferred_element_type=f32).astype(bf16)
    for h in range(heads):
        cols=slice(h*HD,(h+1)*HD)
        gm[:,cols]=across[cols,:]
        gs[cols,:]=down[:,cols]
        qs[cols,:]=q_ref[rows,cols]
    for s in range(TOP):
        i=c*TOP+s
        fetch(i).wait()
        kk[s*BLK:(s+1)*BLK,:]=land[i,0:128,:]
        vv[s*BLK:(s+1)*BLK,:]=land[i,128:256,:]
        lt[:,s*BLK:(s+1)*BLK]=land[i,256:272,:]
    own=slice(TOP*BLK,nkeys)
    kk[own,:]=kl_ref[rows,:]
    vv[own,:]=vl_ref[rows,:]
    lt[:,own]=low_ref[RANK:,rows]
    edge=bnd[c]
    scale=HD**-0.5
    n_ch=nkeys//CH
    split=(heads+1)//2*HD
    groups=[slice(0,split),slice(split,wide)]
    span=[slice(j*CH,(j+1)*CH) for j in range(n_ch)]
    key=lax.broadcasted_iota(jnp.int32,(BLK,BLK),0)
    row=lax.broadcasted_iota(jnp.int32,(BLK,BLK),1)
    seen=(key<=row)&((key>=edge)|(row<edge))
    bias=jnp.where(seen,0.0,-jnp.inf).astype(f32)
    most=[jnp.full((1,g.stop-g.start),-jnp.inf,f32) for g in groups]
    total=[jnp.zeros((1,g.stop-g.start),f32) for g in groups]
    out=[jnp.zeros((HD,g.stop-g.start),f32) for g in groups]
    back=[jnp.zeros((HD,g.stop-g.start),f32) for g in groups]
    inv=[None,None]; dots=[None,None]
    def scores(n,j):
        g=groups[n]
        s=lax.dot_general(kk[span[j],:],qs[g,:],NT,preferred_element_type=f32)
        if j==n_ch-1:
            last=s[CH-BLK:]+jnp.concatenate([bias]*((g.stop-g.start)//BLK),axis=1)
            s=jnp.concatenate([s[:CH-BLK],last],axis=0)
        st[span[j],g]=s
        most[n]=jnp.maximum(most[n],jnp.max(s,axis=0,keepdims=True))
    def expo(n,j):
        e=jnp.exp2((st[span[j],groups[n]]-most[n])*(scale*LOG2E))
        st[span[j],groups[n]]=e
        total[n]=total[n]+jnp.sum(e,axis=0,keepdims=True)
    def attended(n,j):
        if j==0: inv[n]=1.0/total[n]
        low=(st[span[j],groups[n]]*inv[n]).astype(bf16)
        pb[span[j],groups[n]]=low
        out[n]=out[n]+lax.dot_general(vv[span[j],:],low,TN,preferred_element_type=f32)
    def backward(n,j):
        g=groups[n]
        if j==0:
            low=out[n].astype(bf16)
            for h in range(g.start//HD,g.stop//HD):
                at[h*HD:(h+1)*HD,:]=low[:,h*HD-g.start:(h+1)*HD-g.start]
            dots[n]=jnp.sum(gm[:,g].astype(f32)*low.astype(f32),axis=0,keepdims=True)
            inv[n]=inv[n]*scale
        pg=jnp.dot(vv[span[j],:],gm[:,g],preferred_element_type=f32)
        sg=((st[span[j],g]*inv[n])*(pg-dots[n])).astype(bf16)
        back[n]=back[n]+lax.dot_general(kk[span[j],:],sg,TN,preferred_element_type=f32)
        if j==n_ch-1:
            low=back[n].astype(bf16)
            for h in range(g.start//HD,g.stop//HD):
                qg[h*HD:(h+1)*HD,:]=low[:,h*HD-g.start:(h+1)*HD-g.start]
    for j in range(n_ch): scores(0,j)
    for j in range(n_ch): scores(1,j); expo(0,j)
    for j in range(n_ch): attended(0,j); expo(1,j)
    for j in range(n_ch): attended(1,j); backward(0,j)
    for j in range(n_ch):
        backward(1,j)
        vg[span[j],:]=jnp.dot(pb[span[j],:],gs[...],preferred_element_type=f32)
    cols_ref[c,0:TAGS,:]=jnp.dot(twt_ref[...],at[...],preferred_element_type=f32)
    cols_ref[c,TAGS:TAGS+RANK,:]=jnp.dot(qup_ref[...],qg[...],preferred_element_type=f32)
    qug_ref[...]+=lax.dot_general(low_ref[:RANK,rows],qg[...],NT,preferred_element_type=f32)
    whole=vg[...]
    high=whole.astype(bf16)
    rest=(whole-high.astype(f32)).astype(bf16)
    up=vup_ref[...]
    cot=lax.dot_general(up,high,NT,preferred_element_type=f32)+lax.dot_general(up,rest,NT,preferred_element_type=f32)
    cols_ref[c,TAGS+RANK:,:]=cot[:,own]
    for s in range(TOP):
        o=lax.div(ret[c,s],MB)
        zo=lax.rem(lax.div(o,2),Z)
        mc[lax.div(o,ZC)*ZC+lax.rem(zo,Y)*4+lax.div(zo,Y)*2+lax.rem(o,2)]+=cot[:,s*BLK:(s+1)*BLK]
    side=lt[...]
    vug_ref[...]+=jnp.dot(side,high,preferred_element_type=f32)+jnp.dot(side,rest,preferred_element_type=f32)
    @pl.when(c==pl.num_programs(0)-1)
    def _():
        mcot_ref[...]=mc[...].astype(bf16)

def attend(retrieval,boundary,q,kl,vl,low_t,grad_t,tw_t,qup,vup,pool):
    n=q.shape[0]; wide=q.shape[1]; nk=(TOP+1)*BLK; spans=n//BLK
    vm=pl.BlockSpec(memory_space=pltpu.VMEM)
    V=pltpu.VMEM
    shp=lambda *s: jax.ShapeDtypeStruct(s,f32)
    return pl.pallas_call(attend_kernel,
        grid_spec=pltpu.PrefetchScalarGridSpec(num_scalar_prefetch=2,grid=(spans,),
            in_specs=[pl.BlockSpec(memory_space=pl.ANY)]*9,
            out_specs=[vm]*4,
            scratch_shapes=[V(a.shape,a.dtype) for a in (q,kl,vl,low_t,grad_t,tw_t,qup,vup)]+[
              V((spans*TOP,ROWS,HD),bf16),V((nk,HD),bf16),V((nk,HD),bf16),V((RANK,nk),bf16),
              V((wide,HD),bf16),V((HD,wide),bf16),V((wide,HD),bf16),
              V((nk,wide),f32),V((nk,wide),bf16),
              V((wide,BLK),bf16),V((wide,BLK),bf16),V((nk,HD),f32),V((OWNERS,RANK,BLK),f32),
              pltpu.SemaphoreType.DMA((spans*TOP,)),pltpu.SemaphoreType.DMA((8,))]),
        out_shape=[shp(spans,TAGS+2*RANK,BLK),shp(RANK,wide),shp(RANK,HD),jax.ShapeDtypeStruct((OWNERS,RANK,BLK),bf16)],
        compiler_params=pltpu.CompilerParams(vmem_limit_bytes=60*2**20,dimension_semantics=("arbitrary",)),
    )(retrieval,boundary,q,kl,vl,low_t,grad_t,tw_t,qup,vup,pool)

def place():
    t=lax.axis_index("tm"); y=lax.axis_index("heads")
    return lax.div(t,ZC), y, lax.rem(t,ZC)

def reduce_kernel(asked_hbm, cols_hbm, qug_hbm, vug_hbm, mcot_hbm, slab_hbm, mem_hbm,
                  logit_out, grad_out,
                  asked_ref, cols_ref, qug_ref, vug_ref, mcot_ref, slab_ref, mem_ref, wbuf, xbuf, tbuf, zbuf, mall, cbuf, lall, call, g1, r1, x1, o1, g2, r2, x2, o2,
                  xs, ys, zs, ms, cs, ls, ks, a1, b1, d1, a2, b2, d2, lsem):
    x,y,q=place()
    def xp(k): return (lax.rem(x+k,X)*ZC+q, y)
    def yp(k): return (x*ZC+q, lax.rem(y+k,Y))
    def zp(k): return (x*ZC+lax.rem(q+k,ZC), y)
    def xyp(k): return (lax.rem(x+lax.div(k,Y),X)*ZC+q, lax.rem(y+lax.rem(k,Y),Y))
    def each(n,do):
        def body(k,_):
            do(k); return 0
        lax.fori_loop(1,n,body,0)
    def rc(src,dst,sems,k,dev):
        return pltpu.make_async_remote_copy(src_ref=src,dst_ref=dst,send_sem=sems.at[0,k],recv_sem=sems.at[1,k],device_id=dev,device_id_type=MESH)
    loads=[pltpu.make_async_copy(a,b,lsem.at[i]) for i,(a,b) in enumerate([(mcot_hbm,mcot_ref),(cols_hbm,cols_ref),(asked_hbm,asked_ref),(slab_hbm,slab_ref),(qug_hbm,qug_ref),(vug_hbm,vug_ref),(mem_hbm,mem_ref)])]
    for cp in loads: cp.start()
    bar=pltpu.get_barrier_semaphore()
    each(X*Y,lambda k: pl.semaphore_signal(bar,inc=1,device_id=xyp(k),device_id_type=MESH))
    each(ZC,lambda k: pl.semaphore_signal(bar,inc=1,device_id=zp(k),device_id_type=MESH))
    for i in range(2): loads[i].wait()
    pl.semaphore_wait(bar,X*Y+ZC-2)
    def slots(k): return pl.ds(lax.rem(x+lax.div(k,Y),X)*ZC+lax.rem(y+lax.rem(k,Y),Y)*4,4)
    mx=lambda k: rc(mcot_ref.at[slots(k)],xbuf.at[k],xs,k,xyp(k))
    cy=lambda k: rc(cols_ref.at[lax.rem(y+k,Y)],cbuf.at[k],cs,k,yp(k))
    each(X*Y,lambda k: mx(k).start())
    each(Y,lambda k: cy(k).start())
    def owner(j):
        half,core=(j//2,j%2) if isinstance(j,int) else (lax.div(j,2),lax.rem(j,2))
        return (y+Y*half)*2+core
    loads[2].wait()
    for j in range(4):
        for m in range(MB):
            for k in range(X):
                hit=jnp.where(asked_ref[k]==(x*ZC+owner(j))*MB+m,1.0,0.0).astype(f32)
                wbuf[j,m,k:k+1,:]=jnp.broadcast_to(jnp.max(jnp.max(hit,axis=0,keepdims=True),axis=1,keepdims=True),(1,128))
    each(Y,lambda k: cy(k).wait())
    total=cols_ref[y]+cbuf[1]+cbuf[2]+cbuf[3]
    lall[y]=total[:TAGS]
    call[y]=total[TAGS:].astype(bf16)
    ly=lambda k: rc(lall.at[y],lall.at[y],ls,k,yp(k))
    ky=lambda k: rc(call.at[y],call.at[y],ks,k,yp(k))
    each(Y,lambda k: ky(k).start())
    each(Y,lambda k: ly(k).start())
    xbuf[0]=mcot_ref[slots(0)]
    each(X*Y,lambda k: mx(k).wait())
    def expand(j,_):
        parts=[]
        for k in range(X):
            s=xbuf[Y*k,j].astype(f32)
            for i in range(1,Y): s=s+xbuf[Y*k+i,j].astype(f32)
            parts.append(s)
        for m in range(MB):
            acc=parts[0]*wbuf[j,m,0:1,:]
            for k in range(1,X):
                acc=acc+parts[k]*wbuf[j,m,k:k+1,:]
            tbuf[j,m]=acc.astype(bf16)
        return 0
    lax.fori_loop(0,4,expand,0)
    home=lax.rem(lax.div(q,2),Y)==y
    for j in range(4):
        @pl.when(owner(j)!=q)
        def _():
            pltpu.make_async_remote_copy(src_ref=tbuf.at[j],dst_ref=zbuf.at[q],send_sem=ys.at[0,j],recv_sem=zs.at[1,q],device_id=(x*ZC+owner(j),y),device_id_type=MESH).start()
    each(Y,lambda k: ky(k).wait())
    def split(ref,first,value):
        for j in range(value.shape[1]//128):
            ref[first+2*j]=value[0:8,j*128:(j+1)*128]
            ref[first+2*j+1]=value[8:16,j*128:(j+1)*128]
    qdg=jnp.zeros(qug_ref.shape,f32); vdg=jnp.zeros(qug_ref.shape,f32)
    for i in range(3,6): loads[i].wait()
    for s in range(Y):
        piece=slab_ref[s*BLK:(s+1)*BLK,:]
        qdg=qdg+jnp.dot(call[s,0:RANK],piece,preferred_element_type=f32)
        vdg=vdg+jnp.dot(call[s,RANK:],piece,preferred_element_type=f32)
    split(g1,0,qdg); split(g1,14,qug_ref[...]); split(g1,28,vug_ref[...])
    g1[30]=jnp.zeros((8,128),f32); g1[31]=jnp.zeros((8,128),f32)
    ga=lambda k: rc(g1.at[pl.ds(lax.rem(q+k,ZC)*2,2)],r1.at[k],a1,k,zp(k))
    each(ZC,lambda k: ga(k).start())
    from_y=lax.rem(lax.div(q,2),Y)
    my=lambda k: rc(mall,mall,ms,k,yp(k))
    @pl.when(home)
    def _():
        zbuf[q]=tbuf[lax.div(q,8)*2+lax.rem(q,2)]
        def arrive(s,_):
            @pl.when(s!=q)
            def _(): rc(tbuf.at[0],zbuf.at[s],zs,s,(x*ZC+q,y)).wait_recv()
            return 0
        lax.fori_loop(0,ZC,arrive,0)
        for m in range(MB):
            acc=zbuf[0,m].astype(f32)
            for s in range(1,ZC): acc=acc+zbuf[s,m].astype(f32)
            mall[m]=acc.astype(bf16)
        each(Y,lambda k: my(k).start())
    each(ZC,lambda k: ga(k).wait())
    acc=g1[pl.ds(q*2,2)]
    for k in range(1,ZC): acc=acc+r1[k]
    x1[x]=acc
    gb=lambda k: rc(x1.at[x],x1.at[x],b1,k,xp(k))
    each(X,lambda k: gb(k).start())
    @pl.when(jnp.logical_not(home))
    def _(): my(lax.rem(y+Y-from_y,Y)).wait_recv()
    loads[6].wait()
    for m in range(MB):
        vdg=vdg+jnp.dot(mall[m],mem_ref[m*BLK:(m+1)*BLK,:],preferred_element_type=f32)
    split(g2,0,vdg)
    g2[14]=jnp.zeros((8,128),f32); g2[15]=jnp.zeros((8,128),f32)
    ha=lambda k: rc(g2.at[lax.rem(q+k,ZC)],r2.at[k],a2,k,zp(k))
    each(ZC,lambda k: ha(k).start())
    each(X,lambda k: gb(k).wait())
    o1[q]=x1[0]+x1[1]+x1[2]+x1[3]
    gd=lambda k: rc(o1.at[q],o1.at[q],d1,k,zp(k))
    each(ZC,lambda k: gd(k).start())
    each(ZC,lambda k: ha(k).wait())
    acc=g2[q]
    for k in range(1,ZC): acc=acc+r2[k]
    x2[x]=acc
    hb=lambda k: rc(x2.at[x],x2.at[x],b2,k,xp(k))
    each(X,lambda k: hb(k).start())
    each(X,lambda k: hb(k).wait())
    o2[q]=x2[0]+x2[1]+x2[2]+x2[3]
    hd=lambda k: rc(o2.at[q],o2.at[q],d2,k,zp(k))
    each(ZC,lambda k: hd(k).start())
    each(Y,lambda k: ly(k).wait())
    for s in range(Y):
        logit_out[:,s*BLK:(s+1)*BLK]=lall[s]
    for j in range(4):
        @pl.when(owner(j)!=q)
        def _(): pltpu.make_async_remote_copy(src_ref=tbuf.at[j],dst_ref=zbuf.at[q],send_sem=ys.at[0,j],recv_sem=zs.at[1,q],device_id=(x*ZC+owner(j),y),device_id_type=MESH).wait_send()
    @pl.when(home)
    def _(): each(Y,lambda k: my(k).wait_send())
    each(ZC,lambda k: gd(k).wait())
    for k in range(15):
        for i in range(2):
            grad_out[i*8:(i+1)*8,k*128:(k+1)*128]=o1[k,i]
    each(ZC,lambda k: hd(k).wait())
    for k in range(14):
        grad_out[(k%2)*8:(k%2)*8+8,(15+k//2)*128:(16+k//2)*128]=o2[k]

def reduce_all(asked,cols,qug,vug,mcot,slab,mem):
    vm=pl.BlockSpec(memory_space=pltpu.VMEM)
    wide=qug.shape[1]
    V=pltpu.VMEM
    sem=lambda n: pltpu.SemaphoreType.DMA((2,n))
    return pl.pallas_call(reduce_kernel,
        in_specs=[pl.BlockSpec(memory_space=pl.ANY)]*7,
        out_specs=[vm,vm],
        out_shape=[jax.ShapeDtypeStruct((TAGS,slab.shape[0]),f32),jax.ShapeDtypeStruct((RANK,3*wide+HD),f32)],
        scratch_shapes=[V(a.shape,a.dtype) for a in (asked,cols,qug,vug,mcot,slab,mem)]+[V((4,MB,8,128),f32),V((X*Y,4,RANK,BLK),bf16),V((4,MB,RANK,BLK),bf16),V((ZC,MB,RANK,BLK),bf16),V((MB,RANK,BLK),bf16),
            V((Y,TAGS+2*RANK,BLK),f32),V((Y,TAGS,BLK),f32),V((Y,2*RANK,BLK),bf16),
            V((32,8,128),f32),V((ZC,2,8,128),f32),V((X,2,8,128),f32),V((ZC,2,8,128),f32),
            V((16,8,128),f32),V((ZC,8,128),f32),V((X,8,128),f32),V((ZC,8,128),f32),
            sem(X*Y),sem(4),sem(ZC),sem(Y),sem(Y),sem(Y),sem(Y),sem(ZC),sem(X),sem(ZC),sem(ZC),sem(X),sem(ZC),pltpu.SemaphoreType.DMA((7,))],
        compiler_params=pltpu.CompilerParams(collective_id=1,has_side_effects=True,vmem_limit_bytes=60*2**20),
    )(asked,cols,qug,vug,mcot,slab,mem)

def unpack_kernel(logits, grads, a, b, c, d, e, sems):
    wide=b.shape[1]
    jobs=[(logits,a),(grads.at[:,0:wide],b),(grads.at[:,wide:2*wide],c),(grads.at[:,2*wide+HD:],d),(grads.at[:,2*wide:2*wide+HD],e)]
    copies=[pltpu.make_async_copy(s,t,sems.at[i]) for i,(s,t) in enumerate(jobs)]
    for cp in copies: cp.start()
    for cp in copies: cp.wait()

def unpack(logits,grads,wide):
    S=jax.ShapeDtypeStruct; hbm=pl.BlockSpec(memory_space=pl.ANY)
    return pl.pallas_call(unpack_kernel,in_specs=[hbm]*2,out_specs=[hbm]*5,
        out_shape=[S(logits.shape,f32)]+[S((RANK,wide),f32)]*3+[S((RANK,HD),f32)],
        scratch_shapes=[pltpu.SemaphoreType.DMA((5,))],
        compiler_params=pltpu.CompilerParams(vmem_limit_bytes=60*2**20))(logits,grads)

UNITS=8
FIRST={-1: [0], 0: [1], 1: [2], 2: [3], 3: [4], 4: [5], 5: [6], 6: [7]}
LATE=1
PLAN={(1, 0): [(0, 1)], (2, 0): [(1, 1), (0, 2)], (2, 1): [], (3, 0): [(2, 1), (1, 2), (0, 3)], (4, 0): [(3, 1), (2, 2), (1, 3), (0, 4)], (5, 0): [(3, 2), (2, 3), (1, 4), (0, 5)], (6, 0): [(3, 3), (2, 4), (1, 5)], (7, 0): [(3, 4), (2, 5)], (7, 1): [(3, 5)]}

def gather_kernel(mem_ref, slab_ref, wq_ref, wk_ref, wv_ref, qdown_hbm, vdown_hbm, qup_hbm, vup_hbm, ret_hbm,
                  pool, q_out, k_out, v_out, low_out, asked_out,
                  feat, wq, wkv, qdown_ref, vdown_ref, qup_ref, vup_ref, ret_ref, stage, mine, ysem, ssem, rsem, lsem, psem, osem, xsem):
    t=lax.axis_index("tm"); y=lax.axis_index("heads")
    x=lax.div(t,ZC); z=lax.rem(lax.div(t,2),Z); c=lax.rem(t,2)
    def tm(xx,zz,cc): return (xx*Z+zz)*2+cc
    xk=[lax.rem(x+k,X) for k in range(X)]
    devx=[(tm(xk[k],z,c),y) for k in range(X)]
    devz=[(tm(x,lax.rem(z+1,Z),c),y),(tm(x,lax.rem(z+Z-1,Z),c),y)]
    devc=(tm(x,z,1-c),y)
    devy=[(t,lax.rem(y+1,Y)),(t,lax.rem(y+Y-1,Y))]
    def rows_of(u):
        return (mem_ref if u<MB else slab_ref).at[pl.ds((u%MB)*BLK,BLK)]
    own=lambda u: pltpu.make_async_copy(rows_of(u),feat.at[u,y],osem.at[u])
    loads=[pltpu.make_async_copy(a,b,lsem.at[i]) for i,(a,b) in enumerate([(wk_ref,wkv.at[:,0:HD]),(wv_ref,wkv.at[:,HD:2*HD]),(vdown_hbm,vdown_ref),(vup_hbm,vup_ref),(ret_hbm,ret_ref),(wq_ref,wq),(qdown_hbm,qdown_ref),(qup_hbm,qup_ref)])]
    bar=pltpu.get_barrier_semaphore()
    for dev in devx[1:]+devz+devy+[devc]:
        pl.semaphore_signal(bar,inc=1,device_id=dev,device_id_type=MESH)
    for cp in loads[:4]: cp.start()
    pl.semaphore_wait(bar,X-1+5)

    def rc(src,dst,s,r,dev):
        return pltpu.make_async_remote_copy(src_ref=src,dst_ref=dst,send_sem=s,recv_sem=r,device_id=dev,device_id_type=MESH)
    left=lax.rem(y+Y-1,Y); right=lax.rem(y+1,Y)
    H=BLK//2
    def y_first(u): return [rc(rows_of(u),feat.at[u,y],ysem.at[0,u,i],ysem.at[1,u,i],devy[i]) for i in range(2)]
    def y_pass(u): return [rc(feat.at[u,left,pl.ds(0,H)],feat.at[u,left,pl.ds(0,H)],ysem.at[0,u,2],ysem.at[1,u,2],devy[0]),
                           rc(feat.at[u,right,pl.ds(H,H)],feat.at[u,right,pl.ds(H,H)],ysem.at[0,u,3],ysem.at[1,u,3],devy[1])]
    def start(cs):
        for cp in cs: cp.start()
    asked=lambda k: rc(mine,asked_out.at[k],xsem.at[0,k],xsem.at[1,k],devx[k])

    def part(b,cc,xs,zs): return pool.at[b,cc,xs,zs]
    every=pl.ds(0,X)
    GROUP=[pl.ds(0,1),pl.ds(1,2),pl.ds(3,2),pl.ds(5,2),pl.ds(7,1)]
    def share(b,cc,g): return rc(part(b,cc,every,GROUP[g]),part(b,cc,every,GROUP[g]),ssem.at[b,32+g],rsem.at[b,32+g],devc)
    def keep(b): return pltpu.make_async_copy(stage.at[b],pool.at[b,c,x,0],psem.at[b])
    def x_own(b,k): return rc(stage.at[b],pool.at[b,0,x,0],ssem.at[b,k-1],rsem.at[b,k],devx[k])
    back=[x]+[lax.rem(x+X-k,X) for k in range(1,X)]
    def hop0(b,l,i,k):
        src=part(b,0,back[k],0 if l==0 else 2*l-1+i)
        return rc(stage.at[b] if l==0 and k==0 else src,part(b,0,back[k],2*l+1+i),ssem.at[b,3+8*l+2*k+i],rsem.at[b,4+8*l+2*k+i],devz[i])
    def last0(b,k):
        low=back[k]<X//2
        dev=(jnp.where(low,devz[0][0],devz[1][0]),y)
        return rc(part(b,0,back[k],jnp.where(low,5,6)),part(b,0,back[k],7),ssem.at[b,27+k],rsem.at[b,28+k],dev)
    def core0(b,phase):
        if phase==1:
            for k in range(1,X):
                x_own(b,k).wait_recv()
                for i in range(2): hop0(b,0,i,k).start()
            keep(b).wait()
        elif phase<5:
            l=phase-1
            for k in range(X):
                for i in range(2):
                    hop0(b,l-1,i,k).wait_recv()
                    if l<3: hop0(b,l,i,k).start()
                if l==3: last0(b,k).start()
        else:
            for k in range(X): last0(b,k).wait_recv()
        share(b,0,phase-1).start()
    def hop1(b,l,i):
        src=stage.at[b] if l==0 else pool.at[b,1,x,2*l-1+i]
        return rc(src,pool.at[b,1,x,2*l+1+i if l<3 else 7],ssem.at[b,3+2*l+i if l<3 else 9],rsem.at[b,4+2*l+i if l<3 else 10],devz[i])
    def spread(b,g,k):
        src=part(b,1,x,GROUP[g])
        return rc(stage.at[pl.ds(b,1)] if g==0 else src,src,ssem.at[b,12+5*(k-1)+g],rsem.at[b,12+5*(k-1)+g],devx[k])
    def pass_on(b,g):
        for k in range(1,X): spread(b,g,k).wait_recv()
        share(b,1,g).start()
    def core1(b,phase):
        if phase<4:
            l=phase
            for i in range(2):
                hop1(b,l-1,i).wait_recv()
                if l<3 or b%2==i: hop1(b,l,i).start()
            for k in range(1,X): spread(b,l,k).start()
        elif phase==4:
            hop1(b,3,b%2).wait_recv()
            for k in range(1,X): spread(b,4,k).start()
        if phase==1: keep(b).wait()
        if phase in (2,3,4): pass_on(b,phase-2)
        if phase==5:
            pass_on(b,3); pass_on(b,4)
    def begin(b):
        keep(b).start()
        @pl.when(c==0)
        def _():
            for i in range(2): hop0(b,0,i,0).start()
            for k in range(1,X): x_own(b,k).start()
        @pl.when(c==1)
        def _():
            for i in range(2): hop1(b,0,i).start()
            for k in range(1,X): spread(b,0,k).start()
    def step(b,phase):
        pl.when(c==0)(lambda: core0(b,phase))
        pl.when(c==1)(lambda: core1(b,phase))

    def project(u):
        own(u).wait()
        if u==0:
            for i in range(4): loads[i].wait()
        if u==MB:
            for i in range(5,8): loads[i].wait()
        memory=u<MB
        pair=jnp.zeros((BLK,2*HD),f32)
        low=jnp.zeros((RANK if memory else 2*RANK,BLK),f32)
        wide=wq.shape[1]
        for h in range(Y):
            cols=slice(h*wide,(h+1)*wide)
            piece=feat[u,h]
            pair=pair+jnp.dot(piece,wkv[cols,:],preferred_element_type=f32)
            down=vdown_ref[:,cols] if memory else jnp.concatenate([qdown_ref[:,cols],vdown_ref[:,cols]],axis=0)
            low=low+lax.dot_general(down,piece,NT,preferred_element_type=f32)
        low=low.astype(bf16)
        keys=pair[:,:HD].astype(bf16)
        values=(pair[:,HD:]+lax.dot_general(low[-RANK:],vup_ref[...],TN,preferred_element_type=f32)).astype(bf16)
        if memory:
            stage[u,0:BLK,:]=keys
            stage[u,BLK:2*BLK,:]=values
            stage[u,2*BLK:,:]=low
        else:
            b=u-MB
            rows=slice(b*BLK,(b+1)*BLK)
            k_out[rows,:]=keys
            v_out[rows,:]=values
            low_out[:,rows]=low
            acc=lax.dot_general(low[:RANK],qup_ref[...],TN,preferred_element_type=f32)
            for h in range(Y):
                acc=acc+jnp.dot(feat[u,h],wq[h*wide:(h+1)*wide,:],preferred_element_type=f32)
            q_out[rows,:]=acc.astype(bf16)

    for v in FIRST[-1]: start(y_first(v))
    for u in range(UNITS): own(u).start()
    for cp in loads[4:]: cp.start()
    mine[...]=jnp.full(mine.shape,-1,jnp.int32)
    loads[4].wait()
    mine[0:MB,0:TOP]=ret_ref[...]
    for k in range(1,X): asked(k).start()
    asked_out[0]=mine[...]
    for u in range(UNITS):
        for cp in y_first(u): cp.wait_recv()
        start(y_pass(u))
        for v in FIRST.get(u,[]): start(y_first(v))
        if LATE and u>MB: project(u-1)
        for b,p in PLAN.get((u,0),[]): step(b,p)
        for cp in y_pass(u): cp.wait_recv()
        if u<MB or not LATE: project(u)
        if u<MB: begin(u)
        for b,p in PLAN.get((u,1),[]): step(b,p)
    if LATE: project(UNITS-1)
    for k in range(1,X): asked(k).wait()
    for u in range(UNITS):
        for cp in y_first(u)+y_pass(u): cp.wait_send()
    for b in range(MB):
        for g in range(5):
            share(b,1-c,g).wait_recv()
            share(b,c,g).wait_send()
        @pl.when(c==0)
        def _():
            for k in range(1,X): x_own(b,k).wait_send()
            for k in range(X):
                for l in range(3):
                    for i in range(2): hop0(b,l,i,k).wait_send()
                last0(b,k).wait_send()
        @pl.when(c==1)
        def _():
            for l in range(3):
                for i in range(2): hop1(b,l,i).wait_send()
            hop1(b,3,b%2).wait_send()
            for g in range(5):
                for k in range(1,X): spread(b,g,k).wait_send()

def gather_all(mem,slab,wq,wk,wv,qdown,vdown,qup,vup,ret):
    vm=pl.BlockSpec(memory_space=pltpu.VMEM); hbm=pl.BlockSpec(memory_space=pl.ANY)
    n=slab.shape[0]; wide=wq.shape[1]
    S=jax.ShapeDtypeStruct; V=pltpu.VMEM; D=pltpu.SemaphoreType.DMA
    return pl.pallas_call(gather_kernel,
        in_specs=[hbm]*10,
        out_specs=[hbm]+[vm]*5,
        out_shape=[S((MB,2,X,Z,ROWS,HD),bf16),S((n,wide),bf16),S((n,HD),bf16),S((n,HD),bf16),S((2*RANK,n),bf16),S((X,8,128),jnp.int32)],
        scratch_shapes=[V((UNITS,Y,BLK,wide),bf16),V(wq.shape,bf16),V((wq.shape[0],2*HD),bf16),V(qdown.shape,bf16),V(vdown.shape,bf16),V(qup.shape,bf16),V(vup.shape,bf16),V(ret.shape,jnp.int32),
            V((MB,ROWS,HD),bf16),V((8,128),jnp.int32),
            D((2,UNITS,4)),D((MB,37)),D((MB,37)),D((8,)),D((MB,)),D((UNITS,)),D((2,X))],
        compiler_params=pltpu.CompilerParams(collective_id=2,has_side_effects=True,vmem_limit_bytes=60*2**20),
    )(mem,slab,wq,wk,wv,qdown,vdown,qup,vup,ret)

def local(slab_tokens,memory,query_weight,key_weight,value_weight,query_down,query_up,value_down,value_up,tag_weight,retrieval,boundary,grad_tags):
    pool,queries,keys,values,low_t,asked=gather_all(memory,slab_tokens,query_weight,key_weight,value_weight,query_down,value_down,query_up,value_up,retrieval)
    cols,qug,vug,mcot=attend(retrieval,boundary,queries,keys,values,low_t,grad_tags.T,tag_weight.T,query_up,value_up,pool)
    logits,grads=reduce_all(asked,cols,qug,vug,mcot,slab_tokens,memory)
    logits,a,b,c,d=unpack(logits,grads,qug.shape[1])
    return logits.T,a,b,c,d


def solution(mesh):
    in_specs=(P("tm","heads"),P("tm","heads"),P(None,"heads"),P(None,"heads"),P(None,"heads"),P(),P(None,"heads"),P(),P(None,"heads"),P("heads",None),P("tm",None),P("tm"),P("tm",None))
    out_specs=(P("tm",None),P(None,"heads"),P(None,"heads"),P(None,"heads"),P(None,"heads"))
    return jax.shard_map(local,mesh=mesh,in_specs=in_specs,out_specs=out_specs,check_vma=False)
```

```python
import functools
import jax, jax.numpy as jnp
from jax import lax
from jax.sharding import PartitionSpec as P
from jax.experimental import pallas as pl
from jax.experimental.pallas import tpu as pltpu
BLK=128; HD=128; TOP=8; RANK=16; TAGS=8
HIGHEST=lax.Precision.HIGHEST
NT=(((1,),(1,)),((),()))
TN=(((0,),(0,)),((),()))
f32=jnp.float32; bf16=jnp.bfloat16
MB=4; OWNERS=64; ROWS=272; CH=384; X=4; Y=4; Z=8; ZC=16; LOG2E=1.4426950408889634; MESH=pl.DeviceIdType.MESH
def attend_kernel(ret,bnd, q_hbm, kl_hbm, vl_hbm, low_hbm, gt_hbm, twt_hbm, qup_hbm, vup_hbm, pool_ref,
                  cols_ref, qug_ref, vug_ref, mcot_ref,
                  q_ref, kl_ref, vl_ref, low_ref, gt_ref, twt_ref, qup_ref, vup_ref,
                  land, kk, vv, lt, qs, gm, gs, st, pb, at, qg, vg, mc, sems, lsem):
    c=pl.program_id(0)
    heads=q_ref.shape[1]//HD
    wide=heads*BLK
    nkeys=(TOP+1)*BLK
    z=lax.rem(lax.div(lax.axis_index("tm"),2),Z)
    def fetch(i):
        g=ret[lax.div(i,TOP),lax.rem(i,TOP)]
        o=lax.div(g,MB)
        d=lax.rem(lax.rem(lax.div(o,2),Z)+Z-z,Z)
        slot=jnp.where(d==0,0,jnp.where(d<Z//2,2*d,jnp.where(d==Z//2,Z-1,2*(Z-d)-1)))
        return pltpu.make_async_copy(pool_ref.at[lax.rem(g,MB),lax.rem(o,2),lax.div(o,ZC),slot], land.at[i], sems.at[i])
    loads=[pltpu.make_async_copy(src,dst,lsem.at[i]) for i,(src,dst) in enumerate([(q_hbm,q_ref),(kl_hbm,kl_ref),(vl_hbm,vl_ref),(low_hbm,low_ref),(gt_hbm,gt_ref),(twt_hbm,twt_ref),(qup_hbm,qup_ref),(vup_hbm,vup_ref)])]
    @pl.when(c==0)
    def _():
        for cp in loads: cp.start()
        def go(i,_):
            fetch(i).start(); return 0
        lax.fori_loop(0,4*TOP,go,0)
        qug_ref[...]=jnp.zeros_like(qug_ref)
        vug_ref[...]=jnp.zeros_like(vug_ref)
        mc[...]=jnp.zeros_like(mc)
        for cp in loads: cp.wait()
    rows=pl.ds(pl.multiple_of(c*BLK,BLK),BLK)
    part=gt_ref[:,rows]
    terms=[]
    for _ in range(3):
        low=part.astype(bf16).astype(f32)
        terms.append(low); part=part-low
    grads=jnp.concatenate(terms+[jnp.zeros_like(part)],axis=0).astype(bf16)
    tags=jnp.concatenate([twt_ref[...].astype(f32)]*4,axis=0).astype(bf16)
    across=lax.dot_general(tags,grads,TN,preferred_element_type=f32).astype(bf16)
    down=lax.dot_general(grads,tags,TN,preferred_element_type=f32).astype(bf16)
    for h in range(heads):
        cols=slice(h*HD,(h+1)*HD)
        gm[:,cols]=across[cols,:]
        gs[cols,:]=down[:,cols]
        qs[cols,:]=q_ref[rows,cols]
    for s in range(TOP):
        i=c*TOP+s
        fetch(i).wait()
        for half in range(2):
            dst=slice(s*BLK+half*64,s*BLK+half*64+64)
            kk[dst,:]=land[i,half*128:half*128+64,:]
            vv[dst,:]=land[i,half*128+64:half*128+128,:]
        lt[:,s*BLK:(s+1)*BLK]=land[i,256:272,:]
    own=slice(TOP*BLK,nkeys)
    kk[own,:]=kl_ref[rows,:]
    vv[own,:]=vl_ref[rows,:]
    lt[:,own]=low_ref[RANK:,rows]
    edge=bnd[c]
    scale=HD**-0.5
    n_ch=nkeys//CH
    split=(heads+1)//2*HD
    groups=[slice(0,split),slice(split,wide)]
    span=[slice(j*CH,(j+1)*CH) for j in range(n_ch)]
    key=lax.broadcasted_iota(jnp.int32,(BLK,BLK),0)
    row=lax.broadcasted_iota(jnp.int32,(BLK,BLK),1)
    seen=(key<=row)&((key>=edge)|(row<edge))
    bias=jnp.where(seen,0.0,-jnp.inf).astype(f32)
    most=[jnp.full((1,g.stop-g.start),-jnp.inf,f32) for g in groups]
    total=[jnp.zeros((1,g.stop-g.start),f32) for g in groups]
    out=[jnp.zeros((HD,g.stop-g.start),f32) for g in groups]
    back=[jnp.zeros((HD,g.stop-g.start),f32) for g in groups]
    inv=[None,None]; dots=[None,None]
    def scores(n,j):
        g=groups[n]
        s=lax.dot_general(kk[span[j],:],qs[g,:],NT,preferred_element_type=f32)
        if j==n_ch-1:
            last=s[CH-BLK:]+jnp.concatenate([bias]*((g.stop-g.start)//BLK),axis=1)
            s=jnp.concatenate([s[:CH-BLK],last],axis=0)
        st[span[j],g]=s
        most[n]=jnp.maximum(most[n],jnp.max(s,axis=0,keepdims=True))
    def expo(n,j):
        e=jnp.exp2((st[span[j],groups[n]]-most[n])*(scale*LOG2E))
        st[span[j],groups[n]]=e
        total[n]=total[n]+jnp.sum(e,axis=0,keepdims=True)
    def attended(n,j):
        if j==0: inv[n]=1.0/total[n]
        low=(st[span[j],groups[n]]*inv[n]).astype(bf16)
        pb[span[j],groups[n]]=low
        out[n]=out[n]+lax.dot_general(vv[span[j],:],low,TN,preferred_element_type=f32)
    def backward(n,j):
        g=groups[n]
        if j==0:
            low=out[n].astype(bf16)
            for h in range(g.start//HD,g.stop//HD):
                at[h*HD:(h+1)*HD,:]=low[:,h*HD-g.start:(h+1)*HD-g.start]
            dots[n]=jnp.sum(gm[:,g].astype(f32)*low.astype(f32),axis=0,keepdims=True)
            inv[n]=inv[n]*scale
        pg=jnp.dot(vv[span[j],:],gm[:,g],preferred_element_type=f32)
        sg=((st[span[j],g]*inv[n])*(pg-dots[n])).astype(bf16)
        back[n]=back[n]+lax.dot_general(kk[span[j],:],sg,TN,preferred_element_type=f32)
        if j==n_ch-1:
            low=back[n].astype(bf16)
            for h in range(g.start//HD,g.stop//HD):
                qg[h*HD:(h+1)*HD,:]=low[:,h*HD-g.start:(h+1)*HD-g.start]
    for j in range(n_ch): scores(0,j)
    for j in range(n_ch): scores(1,j); expo(0,j)
    for j in range(n_ch): attended(0,j); expo(1,j)
    for j in range(n_ch): attended(1,j); backward(0,j)
    for j in range(n_ch):
        backward(1,j)
        vg[span[j],:]=jnp.dot(pb[span[j],:],gs[...],preferred_element_type=f32)
    cols_ref[c,0:TAGS,:]=jnp.dot(twt_ref[...],at[...],preferred_element_type=f32)
    cols_ref[c,TAGS:TAGS+RANK,:]=jnp.dot(qup_ref[...],qg[...],preferred_element_type=f32)
    qug_ref[...]+=lax.dot_general(low_ref[:RANK,rows],qg[...],NT,preferred_element_type=f32)
    whole=vg[...]
    high=whole.astype(bf16)
    rest=(whole-high.astype(f32)).astype(bf16)
    up=vup_ref[...]
    cot=lax.dot_general(up,high,NT,preferred_element_type=f32)+lax.dot_general(up,rest,NT,preferred_element_type=f32)
    cols_ref[c,TAGS+RANK:,:]=cot[:,own]
    for s in range(TOP):
        o=lax.div(ret[c,s],MB)
        zo=lax.rem(lax.div(o,2),Z)
        mc[lax.div(o,ZC)*ZC+lax.rem(zo,Y)*4+lax.div(zo,Y)*2+lax.rem(o,2)]+=cot[:,s*BLK:(s+1)*BLK]
    side=lt[...]
    vug_ref[...]+=jnp.dot(side,high,preferred_element_type=f32)+jnp.dot(side,rest,preferred_element_type=f32)
    @pl.when(c==pl.num_programs(0)-1)
    def _():
        mcot_ref[...]=mc[...].astype(bf16)

def attend(retrieval,boundary,q,kl,vl,low_t,grad_t,tw_t,qup,vup,pool):
    n=q.shape[0]; wide=q.shape[1]; nk=(TOP+1)*BLK; spans=n//BLK
    vm=pl.BlockSpec(memory_space=pltpu.VMEM)
    V=pltpu.VMEM
    shp=lambda *s: jax.ShapeDtypeStruct(s,f32)
    return pl.pallas_call(attend_kernel,
        grid_spec=pltpu.PrefetchScalarGridSpec(num_scalar_prefetch=2,grid=(spans,),
            in_specs=[pl.BlockSpec(memory_space=pl.ANY)]*9,
            out_specs=[vm]*4,
            scratch_shapes=[V(a.shape,a.dtype) for a in (q,kl,vl,low_t,grad_t,tw_t,qup,vup)]+[
              V((spans*TOP,ROWS,HD),bf16),V((nk,HD),bf16),V((nk,HD),bf16),V((RANK,nk),bf16),
              V((wide,HD),bf16),V((HD,wide),bf16),V((wide,HD),bf16),
              V((nk,wide),f32),V((nk,wide),bf16),
              V((wide,BLK),bf16),V((wide,BLK),bf16),V((nk,HD),f32),V((OWNERS,RANK,BLK),f32),
              pltpu.SemaphoreType.DMA((spans*TOP,)),pltpu.SemaphoreType.DMA((8,))]),
        out_shape=[shp(spans,TAGS+2*RANK,BLK),shp(RANK,wide),shp(RANK,HD),jax.ShapeDtypeStruct((OWNERS,RANK,BLK),bf16)],
        compiler_params=pltpu.CompilerParams(vmem_limit_bytes=60*2**20,dimension_semantics=("arbitrary",)),
    )(retrieval,boundary,q,kl,vl,low_t,grad_t,tw_t,qup,vup,pool)

def place():
    t=lax.axis_index("tm"); y=lax.axis_index("heads")
    return lax.div(t,ZC), y, lax.rem(t,ZC)

def reduce_kernel(asked_hbm, cols_hbm, qug_hbm, vug_hbm, mcot_hbm, slab_hbm, mem_hbm,
                  logit_out, grad_out,
                  asked_ref, cols_ref, qug_ref, vug_ref, mcot_ref, slab_ref, mem_ref, wbuf, xbuf, tbuf, zbuf, mall, cbuf, lall, call, g1, r1, x1, o1, g2, r2, x2, o2,
                  xs, ys, zs, ms, cs, ls, ks, a1, b1, d1, a2, b2, d2, lsem):
    x,y,q=place()
    def xp(k): return (lax.rem(x+k,X)*ZC+q, y)
    def yp(k): return (x*ZC+q, lax.rem(y+k,Y))
    def zp(k): return (x*ZC+lax.rem(q+k,ZC), y)
    def xyp(k): return (lax.rem(x+lax.div(k,Y),X)*ZC+q, lax.rem(y+lax.rem(k,Y),Y))
    def each(n,do):
        def body(k,_):
            do(k); return 0
        lax.fori_loop(1,n,body,0)
    def rc(src,dst,sems,k,dev):
        return pltpu.make_async_remote_copy(src_ref=src,dst_ref=dst,send_sem=sems.at[0,k],recv_sem=sems.at[1,k],device_id=dev,device_id_type=MESH)
    loads=[pltpu.make_async_copy(a,b,lsem.at[i]) for i,(a,b) in enumerate([(mcot_hbm,mcot_ref),(cols_hbm,cols_ref),(asked_hbm,asked_ref),(slab_hbm,slab_ref),(qug_hbm,qug_ref),(vug_hbm,vug_ref),(mem_hbm,mem_ref)])]
    for cp in loads: cp.start()
    bar=pltpu.get_barrier_semaphore()
    each(X*Y,lambda k: pl.semaphore_signal(bar,inc=1,device_id=xyp(k),device_id_type=MESH))
    each(ZC,lambda k: pl.semaphore_signal(bar,inc=1,device_id=zp(k),device_id_type=MESH))
    for i in range(2): loads[i].wait()
    pl.semaphore_wait(bar,X*Y+ZC-2)
    def slots(k): return pl.ds(lax.rem(x+lax.div(k,Y),X)*ZC+lax.rem(y+lax.rem(k,Y),Y)*4,4)
    mx=lambda k: rc(mcot_ref.at[slots(k)],xbuf.at[k],xs,k,xyp(k))
    cy=lambda k: rc(cols_ref.at[lax.rem(y+k,Y)],cbuf.at[k],cs,k,yp(k))
    each(X*Y,lambda k: mx(k).start())
    each(Y,lambda k: cy(k).start())
    def owner(j):
        half,core=(j//2,j%2) if isinstance(j,int) else (lax.div(j,2),lax.rem(j,2))
        return (y+Y*half)*2+core
    loads[2].wait()
    for j in range(4):
        for m in range(MB):
            for k in range(X):
                hit=jnp.where(asked_ref[k]==(x*ZC+owner(j))*MB+m,1.0,0.0).astype(f32)
                wbuf[j,m,k:k+1,:]=jnp.broadcast_to(jnp.max(jnp.max(hit,axis=0,keepdims=True),axis=1,keepdims=True),(1,128))
    each(Y,lambda k: cy(k).wait())
    total=cols_ref[y]+cbuf[1]+cbuf[2]+cbuf[3]
    lall[y]=total[:TAGS]
    call[y]=total[TAGS:].astype(bf16)
    ly=lambda k: rc(lall.at[y],lall.at[y],ls,k,yp(k))
    ky=lambda k: rc(call.at[y],call.at[y],ks,k,yp(k))
    each(Y,lambda k: ky(k).start())
    each(Y,lambda k: ly(k).start())
    xbuf[0]=mcot_ref[slots(0)]
    each(X*Y,lambda k: mx(k).wait())
    def expand(j,_):
        parts=[]
        for k in range(X):
            s=xbuf[Y*k,j].astype(f32)
            for i in range(1,Y): s=s+xbuf[Y*k+i,j].astype(f32)
            parts.append(s)
        for m in range(MB):
            acc=parts[0]*wbuf[j,m,0:1,:]
            for k in range(1,X):
                acc=acc+parts[k]*wbuf[j,m,k:k+1,:]
            tbuf[j,m]=acc.astype(bf16)
        return 0
    lax.fori_loop(0,4,expand,0)
    home=lax.rem(lax.div(q,2),Y)==y
    for j in range(4):
        @pl.when(owner(j)!=q)
        def _():
            pltpu.make_async_remote_copy(src_ref=tbuf.at[j],dst_ref=zbuf.at[q],send_sem=ys.at[0,j],recv_sem=zs.at[1,q],device_id=(x*ZC+owner(j),y),device_id_type=MESH).start()
    each(Y,lambda k: ky(k).wait())
    def split(ref,first,value):
        for j in range(value.shape[1]//128):
            ref[first+2*j]=value[0:8,j*128:(j+1)*128]
            ref[first+2*j+1]=value[8:16,j*128:(j+1)*128]
    qdg=jnp.zeros(qug_ref.shape,f32); vdg=jnp.zeros(qug_ref.shape,f32)
    for i in range(3,6): loads[i].wait()
    for s in range(Y):
        piece=slab_ref[s*BLK:(s+1)*BLK,:]
        qdg=qdg+jnp.dot(call[s,0:RANK],piece,preferred_element_type=f32)
        vdg=vdg+jnp.dot(call[s,RANK:],piece,preferred_element_type=f32)
    split(g1,0,qdg); split(g1,14,qug_ref[...]); split(g1,28,vug_ref[...])
    g1[30]=jnp.zeros((8,128),f32); g1[31]=jnp.zeros((8,128),f32)
    ga=lambda k: rc(g1.at[pl.ds(lax.rem(q+k,ZC)*2,2)],r1.at[k],a1,k,zp(k))
    each(ZC,lambda k: ga(k).start())
    from_y=lax.rem(lax.div(q,2),Y)
    my=lambda k: rc(mall,mall,ms,k,yp(k))
    @pl.when(home)
    def _():
        zbuf[q]=tbuf[lax.div(q,8)*2+lax.rem(q,2)]
        def arrive(s,_):
            @pl.when(s!=q)
            def _(): rc(tbuf.at[0],zbuf.at[s],zs,s,(x*ZC+q,y)).wait_recv()
            return 0
        lax.fori_loop(0,ZC,arrive,0)
        for m in range(MB):
            acc=zbuf[0,m].astype(f32)
            for s in range(1,ZC): acc=acc+zbuf[s,m].astype(f32)
            mall[m]=acc.astype(bf16)
        each(Y,lambda k: my(k).start())
    each(ZC,lambda k: ga(k).wait())
    acc=g1[pl.ds(q*2,2)]
    for k in range(1,ZC): acc=acc+r1[k]
    x1[x]=acc
    gb=lambda k: rc(x1.at[x],x1.at[x],b1,k,xp(k))
    each(X,lambda k: gb(k).start())
    @pl.when(jnp.logical_not(home))
    def _(): my(lax.rem(y+Y-from_y,Y)).wait_recv()
    loads[6].wait()
    for m in range(MB):
        vdg=vdg+jnp.dot(mall[m],mem_ref[m*BLK:(m+1)*BLK,:],preferred_element_type=f32)
    split(g2,0,vdg)
    g2[14]=jnp.zeros((8,128),f32); g2[15]=jnp.zeros((8,128),f32)
    ha=lambda k: rc(g2.at[lax.rem(q+k,ZC)],r2.at[k],a2,k,zp(k))
    each(ZC,lambda k: ha(k).start())
    each(X,lambda k: gb(k).wait())
    o1[q]=x1[0]+x1[1]+x1[2]+x1[3]
    gd=lambda k: rc(o1.at[q],o1.at[q],d1,k,zp(k))
    each(ZC,lambda k: gd(k).start())
    each(ZC,lambda k: ha(k).wait())
    acc=g2[q]
    for k in range(1,ZC): acc=acc+r2[k]
    x2[x]=acc
    hb=lambda k: rc(x2.at[x],x2.at[x],b2,k,xp(k))
    each(X,lambda k: hb(k).start())
    each(X,lambda k: hb(k).wait())
    o2[q]=x2[0]+x2[1]+x2[2]+x2[3]
    hd=lambda k: rc(o2.at[q],o2.at[q],d2,k,zp(k))
    each(ZC,lambda k: hd(k).start())
    each(Y,lambda k: ly(k).wait())
    for s in range(Y):
        logit_out[:,s*BLK:(s+1)*BLK]=lall[s]
    for j in range(4):
        @pl.when(owner(j)!=q)
        def _(): pltpu.make_async_remote_copy(src_ref=tbuf.at[j],dst_ref=zbuf.at[q],send_sem=ys.at[0,j],recv_sem=zs.at[1,q],device_id=(x*ZC+owner(j),y),device_id_type=MESH).wait_send()
    @pl.when(home)
    def _(): each(Y,lambda k: my(k).wait_send())
    each(ZC,lambda k: gd(k).wait())
    for k in range(15):
        for i in range(2):
            grad_out[i*8:(i+1)*8,k*128:(k+1)*128]=o1[k,i]
    each(ZC,lambda k: hd(k).wait())
    for k in range(14):
        grad_out[(k%2)*8:(k%2)*8+8,(15+k//2)*128:(16+k//2)*128]=o2[k]

def reduce_all(asked,cols,qug,vug,mcot,slab,mem):
    vm=pl.BlockSpec(memory_space=pltpu.VMEM)
    wide=qug.shape[1]
    V=pltpu.VMEM
    sem=lambda n: pltpu.SemaphoreType.DMA((2,n))
    return pl.pallas_call(reduce_kernel,
        in_specs=[pl.BlockSpec(memory_space=pl.ANY)]*7,
        out_specs=[vm,vm],
        out_shape=[jax.ShapeDtypeStruct((TAGS,slab.shape[0]),f32),jax.ShapeDtypeStruct((RANK,3*wide+HD),f32)],
        scratch_shapes=[V(a.shape,a.dtype) for a in (asked,cols,qug,vug,mcot,slab,mem)]+[V((4,MB,8,128),f32),V((X*Y,4,RANK,BLK),bf16),V((4,MB,RANK,BLK),bf16),V((ZC,MB,RANK,BLK),bf16),V((MB,RANK,BLK),bf16),
            V((Y,TAGS+2*RANK,BLK),f32),V((Y,TAGS,BLK),f32),V((Y,2*RANK,BLK),bf16),
            V((32,8,128),f32),V((ZC,2,8,128),f32),V((X,2,8,128),f32),V((ZC,2,8,128),f32),
            V((16,8,128),f32),V((ZC,8,128),f32),V((X,8,128),f32),V((ZC,8,128),f32),
            sem(X*Y),sem(4),sem(ZC),sem(Y),sem(Y),sem(Y),sem(Y),sem(ZC),sem(X),sem(ZC),sem(ZC),sem(X),sem(ZC),pltpu.SemaphoreType.DMA((7,))],
        compiler_params=pltpu.CompilerParams(collective_id=1,has_side_effects=True,vmem_limit_bytes=60*2**20),
    )(asked,cols,qug,vug,mcot,slab,mem)

def unpack_kernel(logits, grads, a, b, c, d, e):
    wide=b.shape[1]
    a[...]=logits[...]
    b[...]=grads[:,0:wide]
    c[...]=grads[:,wide:2*wide]
    d[...]=grads[:,2*wide+HD:]
    e[...]=grads[:,2*wide:2*wide+HD]

def unpack(logits,grads,wide):
    S=jax.ShapeDtypeStruct; vm=pl.BlockSpec(memory_space=pltpu.VMEM)
    return pl.pallas_call(unpack_kernel,in_specs=[vm]*2,out_specs=[vm]*5,
        out_shape=[S(logits.shape,f32)]+[S((RANK,wide),f32)]*3+[S((RANK,HD),f32)],
        compiler_params=pltpu.CompilerParams(vmem_limit_bytes=60*2**20))(logits,grads)

UNIT=[(0,0,64),(0,64,64),(1,0,128),(2,0,128),(3,0,128),(4,0,128),(5,0,128),(6,0,128),(7,0,128)]
ROUND=[(0,0,128),(0,128,272),(1,0,272),(2,0,272),(3,0,272)]
UNITS=len(UNIT); RN=len(ROUND)
FIRST={-1:[0],0:[1],1:[2],2:[3],3:[4],4:[5],5:[6],6:[7],7:[8]}
PLAN={(1, 0): [(0, 1)], (2, 0): [(0, 2), (1, 1)], (3, 0): [(0, 3), (1, 2), (2, 1)], (4, 0): [(0, 4), (1, 3), (2, 2), (3, 1)], (5, 0): [(0, 5), (1, 4), (2, 3), (3, 2), (4, 1)], (6, 0): [(1, 5), (2, 4), (3, 3), (4, 2)], (7, 0): [(2, 5), (3, 4), (4, 3)], (8, 0): [(3, 5), (4, 4)], (8, 1): [(4, 5)]}

def gather_kernel(mem_ref, slab_ref, wq_ref, wk_ref, wv_ref, qdown_hbm, vdown_hbm, qup_hbm, vup_hbm, ret_hbm,
                  pool, q_out, k_out, v_out, low_out, asked_out,
                  feat, wq, wkv, qdown_ref, vdown_ref, qup_ref, vup_ref, ret_ref, stage, mine, ysem, ssem, rsem, lsem, psem, osem, xsem):
    t=lax.axis_index("tm"); y=lax.axis_index("heads")
    x=lax.div(t,ZC); z=lax.rem(lax.div(t,2),Z); c=lax.rem(t,2)
    def tm(xx,zz,cc): return (xx*Z+zz)*2+cc
    xk=[lax.rem(x+k,X) for k in range(X)]
    devx=[(tm(xk[k],z,c),y) for k in range(X)]
    devz=[(tm(x,lax.rem(z+1,Z),c),y),(tm(x,lax.rem(z+Z-1,Z),c),y)]
    devc=(tm(x,z,1-c),y)
    devy=[(t,lax.rem(y+1,Y)),(t,lax.rem(y+Y-1,Y))]
    def rows_of(u):
        fb,r0,n=UNIT[u]
        return (mem_ref if fb<MB else slab_ref).at[pl.ds(fb%MB*BLK+r0,n)]
    own=lambda fb: pltpu.make_async_copy((mem_ref if fb<MB else slab_ref).at[pl.ds(fb%MB*BLK,BLK)],feat.at[fb,y],osem.at[fb])
    loads=[pltpu.make_async_copy(a,b,lsem.at[i]) for i,(a,b) in enumerate([(wk_ref,wkv.at[:,0:HD]),(wv_ref,wkv.at[:,HD:2*HD]),(vdown_hbm,vdown_ref),(vup_hbm,vup_ref),(ret_hbm,ret_ref),(wq_ref,wq),(qdown_hbm,qdown_ref),(qup_hbm,qup_ref)])]
    bar=pltpu.get_barrier_semaphore()
    for dev in devx[1:]+devz+devy+[devc]:
        pl.semaphore_signal(bar,inc=1,device_id=dev,device_id_type=MESH)
    for cp in loads[:4]: cp.start()
    pl.semaphore_wait(bar,X-1+5)

    def rc(src,dst,s,r,dev):
        return pltpu.make_async_remote_copy(src_ref=src,dst_ref=dst,send_sem=s,recv_sem=r,device_id=dev,device_id_type=MESH)
    left=lax.rem(y+Y-1,Y); right=lax.rem(y+1,Y)
    def piece_of(u,h,half=None):
        fb,r0,n=UNIT[u]
        return feat.at[fb,h,pl.ds(r0,n) if half is None else pl.ds(r0+half*(n//2),n//2)]
    def y_first(u): return [rc(rows_of(u),piece_of(u,y),ysem.at[0,u,i],ysem.at[1,u,i],devy[i]) for i in range(2)]
    def y_pass(u): return [rc(piece_of(u,h,i),piece_of(u,h,i),ysem.at[0,u,2+i],ysem.at[1,u,2+i],devy[i]) for i,h in enumerate((left,right))]
    def start(cs):
        for cp in cs: cp.start()
    asked=lambda k: rc(mine,asked_out.at[k],xsem.at[0,k],xsem.at[1,k],devx[k])

    def part(r,cc,xs,zs):
        b,lo,hi=ROUND[r]
        return pool.at[b,cc,xs,zs,pl.ds(lo,hi-lo)]
    def fresh(r):
        b,lo,hi=ROUND[r]
        return stage.at[b,pl.ds(lo,hi-lo)]
    every=pl.ds(0,X)
    GROUP=[pl.ds(0,1),pl.ds(1,2),pl.ds(3,2),pl.ds(5,2),pl.ds(7,1)]
    def share(b,cc,g): return rc(part(b,cc,every,GROUP[g]),part(b,cc,every,GROUP[g]),ssem.at[b,32+g],rsem.at[b,32+g],devc)
    def keep(b): return pltpu.make_async_copy(fresh(b),part(b,c,x,0),psem.at[b])
    def x_own(b,k): return rc(fresh(b),part(b,0,x,0),ssem.at[b,k-1],rsem.at[b,k],devx[k])
    back=[x]+[lax.rem(x+X-k,X) for k in range(1,X)]
    def hop0(b,l,i,k):
        src=part(b,0,back[k],0 if l==0 else 2*l-1+i)
        return rc(fresh(b) if l==0 and k==0 else src,part(b,0,back[k],2*l+1+i),ssem.at[b,3+8*l+2*k+i],rsem.at[b,4+8*l+2*k+i],devz[i])
    def last0(b,k):
        low=back[k]<X//2
        dev=(jnp.where(low,devz[0][0],devz[1][0]),y)
        return rc(part(b,0,back[k],jnp.where(low,5,6)),part(b,0,back[k],7),ssem.at[b,27+k],rsem.at[b,28+k],dev)
    def core0(b,phase):
        if phase==1:
            for k in range(1,X):
                x_own(b,k).wait_recv()
                for i in range(2): hop0(b,0,i,k).start()
            keep(b).wait()
        elif phase<5:
            l=phase-1
            for k in range(X):
                for i in range(2):
                    hop0(b,l-1,i,k).wait_recv()
                    if l<3: hop0(b,l,i,k).start()
                if l==3: last0(b,k).start()
        else:
            for k in range(X): last0(b,k).wait_recv()
        share(b,0,phase-1).start()
    def hop1(b,l,i):
        src=fresh(b) if l==0 else part(b,1,x,2*l-1+i)
        return rc(src,part(b,1,x,2*l+1+i if l<3 else 7),ssem.at[b,3+2*l+i if l<3 else 9],rsem.at[b,4+2*l+i if l<3 else 10],devz[i])
    def spread(b,g,k):
        src=part(b,1,x,0 if g==0 else GROUP[g])
        return rc(fresh(b) if g==0 else src,src,ssem.at[b,12+5*(k-1)+g],rsem.at[b,12+5*(k-1)+g],devx[k])
    def pass_on(b,g):
        for k in range(1,X): spread(b,g,k).wait_recv()
        share(b,1,g).start()
    def core1(b,phase):
        if phase<4:
            l=phase
            for i in range(2):
                hop1(b,l-1,i).wait_recv()
                if l<3 or b%2==i: hop1(b,l,i).start()
            for k in range(1,X): spread(b,l,k).start()
        elif phase==4:
            hop1(b,3,b%2).wait_recv()
            for k in range(1,X): spread(b,4,k).start()
        if phase==1: keep(b).wait()
        if phase in (2,3,4): pass_on(b,phase-2)
        if phase==5:
            pass_on(b,3); pass_on(b,4)
    def begin(b):
        keep(b).start()
        @pl.when(c==0)
        def _():
            for i in range(2): hop0(b,0,i,0).start()
            for k in range(1,X): x_own(b,k).start()
        @pl.when(c==1)
        def _():
            for i in range(2): hop1(b,0,i).start()
            for k in range(1,X): spread(b,0,k).start()
    def step(b,phase):
        pl.when(c==0)(lambda: core0(b,phase))
        pl.when(c==1)(lambda: core1(b,phase))

    def project(u):
        fb,r0,n=UNIT[u]
        if r0==0: own(fb).wait()
        if u==0:
            for i in range(4): loads[i].wait()
        memory=fb<MB
        if fb==MB:
            for i in range(5,8): loads[i].wait()
        pair=jnp.zeros((n,2*HD),f32)
        low=jnp.zeros((RANK if memory else 2*RANK,n),f32)
        wide=wq.shape[1]
        for h in range(Y):
            cols=slice(h*wide,(h+1)*wide)
            piece=feat[fb,h,r0:r0+n]
            pair=pair+jnp.dot(piece,wkv[cols,:],preferred_element_type=f32)
            down=vdown_ref[:,cols] if memory else jnp.concatenate([qdown_ref[:,cols],vdown_ref[:,cols]],axis=0)
            low=low+lax.dot_general(down,piece,NT,preferred_element_type=f32)
        low=low.astype(bf16)
        keys=pair[:,:HD].astype(bf16)
        values=(pair[:,HD:]+lax.dot_general(low[-RANK:],vup_ref[...],TN,preferred_element_type=f32)).astype(bf16)
        if memory:
            for i in range(0,n,64):
                stage[fb,2*(r0+i):2*(r0+i)+64,:]=keys[i:i+64]
                stage[fb,2*(r0+i)+64:2*(r0+i)+128,:]=values[i:i+64]
            stage[fb,2*BLK:,r0:r0+n]=low
        else:
            b=fb-MB
            rows=slice(b*BLK,(b+1)*BLK)
            k_out[rows,:]=keys
            v_out[rows,:]=values
            low_out[:,rows]=low
            acc=lax.dot_general(low[:RANK],qup_ref[...],TN,preferred_element_type=f32)
            for h in range(Y):
                acc=acc+jnp.dot(feat[fb,h],wq[h*wide:(h+1)*wide,:],preferred_element_type=f32)
            q_out[rows,:]=acc.astype(bf16)

    for v in FIRST[-1]: start(y_first(v))
    for fb in range(2*MB): own(fb).start()
    for cp in loads[4:]: cp.start()
    mine[...]=jnp.full(mine.shape,-1,jnp.int32)
    loads[4].wait()
    mine[0:MB,0:TOP]=ret_ref[...]
    for k in range(1,X): asked(k).start()
    asked_out[0]=mine[...]
    for u in range(UNITS):
        for cp in y_first(u): cp.wait_recv()
        start(y_pass(u))
        for v in FIRST.get(u,[]): start(y_first(v))
        if u>RN: project(u-1)
        for b,p in PLAN.get((u,0),[]): step(b,p)
        for cp in y_pass(u): cp.wait_recv()
        if u<RN:
            project(u)
            begin(u)
        for b,p in PLAN.get((u,1),[]): step(b,p)
    project(UNITS-1)
    for k in range(1,X): asked(k).wait()
    for u in range(UNITS):
        for cp in y_first(u)+y_pass(u): cp.wait_send()
    for b in range(RN):
        for g in range(5):
            share(b,1-c,g).wait_recv()
            share(b,c,g).wait_send()
        @pl.when(c==0)
        def _():
            for k in range(1,X): x_own(b,k).wait_send()
            for k in range(X):
                for l in range(3):
                    for i in range(2): hop0(b,l,i,k).wait_send()
                last0(b,k).wait_send()
        @pl.when(c==1)
        def _():
            for l in range(3):
                for i in range(2): hop1(b,l,i).wait_send()
            hop1(b,3,b%2).wait_send()
            for g in range(5):
                for k in range(1,X): spread(b,g,k).wait_send()

def gather_all(mem,slab,wq,wk,wv,qdown,vdown,qup,vup,ret):
    vm=pl.BlockSpec(memory_space=pltpu.VMEM); hbm=pl.BlockSpec(memory_space=pl.ANY)
    n=slab.shape[0]; wide=wq.shape[1]
    S=jax.ShapeDtypeStruct; V=pltpu.VMEM; D=pltpu.SemaphoreType.DMA
    return pl.pallas_call(gather_kernel,
        in_specs=[hbm]*10,
        out_specs=[hbm]+[vm]*5,
        out_shape=[S((MB,2,X,Z,ROWS,HD),bf16),S((n,wide),bf16),S((n,HD),bf16),S((n,HD),bf16),S((2*RANK,n),bf16),S((X,8,128),jnp.int32)],
        scratch_shapes=[V((2*MB,Y,BLK,wide),bf16),V(wq.shape,bf16),V((wq.shape[0],2*HD),bf16),V(qdown.shape,bf16),V(vdown.shape,bf16),V(qup.shape,bf16),V(vup.shape,bf16),V(ret.shape,jnp.int32),
            V((MB,ROWS,HD),bf16),V((8,128),jnp.int32),
            D((2,UNITS,4)),D((RN,37)),D((RN,37)),D((8,)),D((RN,)),D((2*MB,)),D((2,X))],
        compiler_params=pltpu.CompilerParams(collective_id=2,has_side_effects=True,vmem_limit_bytes=60*2**20),
    )(mem,slab,wq,wk,wv,qdown,vdown,qup,vup,ret)

def local(slab_tokens,memory,query_weight,key_weight,value_weight,query_down,query_up,value_down,value_up,tag_weight,retrieval,boundary,grad_tags):
    pool,queries,keys,values,low_t,asked=gather_all(memory,slab_tokens,query_weight,key_weight,value_weight,query_down,value_down,query_up,value_up,retrieval)
    cols,qug,vug,mcot=attend(retrieval,boundary,queries,keys,values,low_t,grad_tags.T,tag_weight.T,query_up,value_up,pool)
    logits,grads=reduce_all(asked,cols,qug,vug,mcot,slab_tokens,memory)
    logits,a,b,c,d=unpack(logits,grads,qug.shape[1])
    return logits.T,a,b,c,d


def solution(mesh):
    in_specs=(P("tm","heads"),P("tm","heads"),P(None,"heads"),P(None,"heads"),P(None,"heads"),P(),P(None,"heads"),P(),P(None,"heads"),P("heads",None),P("tm",None),P("tm"),P("tm",None))
    out_specs=(P("tm",None),P(None,"heads"),P(None,"heads"),P(None,"heads"),P(None,"heads"))
    return jax.shard_map(local,mesh=mesh,in_specs=in_specs,out_specs=out_specs,check_vma=False)
```

```python
import functools
import jax, jax.numpy as jnp
from jax import lax
from jax.sharding import PartitionSpec as P
from jax.experimental import pallas as pl
from jax.experimental.pallas import tpu as pltpu
BLK=128; HD=128; TOP=8; RANK=16; TAGS=8
HIGHEST=lax.Precision.HIGHEST
NT=(((1,),(1,)),((),()))
TN=(((0,),(0,)),((),()))
f32=jnp.float32; bf16=jnp.bfloat16
MB=4; OWNERS=64; ROWS=272; CH=384; X=4; Y=4; Z=8; ZC=16; LOG2E=1.4426950408889634; MESH=pl.DeviceIdType.MESH
def attend_kernel(ret,bnd, q_hbm, kl_hbm, vl_hbm, low_hbm, gt_hbm, twt_hbm, qup_hbm, vup_hbm, pool_ref,
                  cols_ref, qug_ref, vug_ref, mcot_ref,
                  q_ref, kl_ref, vl_ref, low_ref, gt_ref, twt_ref, qup_ref, vup_ref,
                  land, kk, vv, lt, qs, gm, gs, st, pb, at, qg, vg, mc, sems, lsem):
    c=pl.program_id(0)
    heads=q_ref.shape[1]//HD
    wide=heads*BLK
    nkeys=(TOP+1)*BLK
    z=lax.rem(lax.div(lax.axis_index("tm"),2),Z)
    def fetch(i):
        g=ret[lax.div(i,TOP),lax.rem(i,TOP)]
        o=lax.div(g,MB)
        d=lax.rem(lax.rem(lax.div(o,2),Z)+Z-z,Z)
        slot=jnp.where(d==0,0,jnp.where(d<Z//2,2*d,jnp.where(d==Z//2,Z-1,2*(Z-d)-1)))
        return pltpu.make_async_copy(pool_ref.at[lax.rem(g,MB),lax.rem(o,2),lax.div(o,ZC),slot], land.at[i], sems.at[i])
    loads=[pltpu.make_async_copy(src,dst,lsem.at[i]) for i,(src,dst) in enumerate([(q_hbm,q_ref),(kl_hbm,kl_ref),(vl_hbm,vl_ref),(low_hbm,low_ref),(gt_hbm,gt_ref),(twt_hbm,twt_ref),(qup_hbm,qup_ref),(vup_hbm,vup_ref)])]
    @pl.when(c==0)
    def _():
        for i in range(TOP): fetch(i).start()
        for cp in loads: cp.start()
        qug_ref[...]=jnp.zeros_like(qug_ref)
        vug_ref[...]=jnp.zeros_like(vug_ref)
        mc[...]=jnp.zeros_like(mc)
        for cp in loads: cp.wait()
    rows=pl.ds(pl.multiple_of(c*BLK,BLK),BLK)
    part=gt_ref[:,rows]
    terms=[]
    for _ in range(3):
        low=part.astype(bf16).astype(f32)
        terms.append(low); part=part-low
    grads=jnp.concatenate(terms+[jnp.zeros_like(part)],axis=0).astype(bf16)
    tags=jnp.concatenate([twt_ref[...].astype(f32)]*4,axis=0).astype(bf16)
    across=lax.dot_general(tags,grads,TN,preferred_element_type=f32).astype(bf16)
    down=lax.dot_general(grads,tags,TN,preferred_element_type=f32).astype(bf16)
    for h in range(heads):
        cols=slice(h*HD,(h+1)*HD)
        gm[:,cols]=across[cols,:]
        gs[cols,:]=down[:,cols]
        qs[cols,:]=q_ref[rows,cols]
    for s in range(TOP):
        i=c*TOP+s
        fetch(i).wait()
        for half in range(2):
            dst=slice(s*BLK+half*64,s*BLK+half*64+64)
            kk[dst,:]=land[i,half*128:half*128+64,:]
            vv[dst,:]=land[i,half*128+64:half*128+128,:]
        lt[:,s*BLK:(s+1)*BLK]=land[i,256:272,:]
    @pl.when(c<pl.num_programs(0)-1)
    def _():
        for s in range(TOP): fetch((c+1)*TOP+s).start()
    own=slice(TOP*BLK,nkeys)
    kk[own,:]=kl_ref[rows,:]
    vv[own,:]=vl_ref[rows,:]
    lt[:,own]=low_ref[RANK:,rows]
    edge=bnd[c]
    scale=HD**-0.5
    n_ch=nkeys//CH
    split=(heads+1)//2*HD
    groups=[slice(0,split),slice(split,wide)]
    span=[slice(j*CH,(j+1)*CH) for j in range(n_ch)]
    key=lax.broadcasted_iota(jnp.int32,(BLK,BLK),0)
    row=lax.broadcasted_iota(jnp.int32,(BLK,BLK),1)
    seen=(key<=row)&((key>=edge)|(row<edge))
    bias=jnp.where(seen,0.0,-jnp.inf).astype(f32)
    most=[jnp.full((1,g.stop-g.start),-jnp.inf,f32) for g in groups]
    total=[jnp.zeros((1,g.stop-g.start),f32) for g in groups]
    out=[jnp.zeros((HD,g.stop-g.start),f32) for g in groups]
    back=[jnp.zeros((HD,g.stop-g.start),f32) for g in groups]
    inv=[None,None]; dots=[None,None]
    def scores(n,j):
        g=groups[n]
        s=lax.dot_general(kk[span[j],:],qs[g,:],NT,preferred_element_type=f32)
        if j==n_ch-1:
            last=s[CH-BLK:]+jnp.concatenate([bias]*((g.stop-g.start)//BLK),axis=1)
            s=jnp.concatenate([s[:CH-BLK],last],axis=0)
        st[span[j],g]=s
        most[n]=jnp.maximum(most[n],jnp.max(s,axis=0,keepdims=True))
    def expo(n,j):
        e=jnp.exp2((st[span[j],groups[n]]-most[n])*(scale*LOG2E))
        st[span[j],groups[n]]=e
        total[n]=total[n]+jnp.sum(e,axis=0,keepdims=True)
    def attended(n,j):
        if j==0: inv[n]=1.0/total[n]
        low=(st[span[j],groups[n]]*inv[n]).astype(bf16)
        pb[span[j],groups[n]]=low
        out[n]=out[n]+lax.dot_general(vv[span[j],:],low,TN,preferred_element_type=f32)
    def backward(n,j):
        g=groups[n]
        if j==0:
            low=out[n].astype(bf16)
            for h in range(g.start//HD,g.stop//HD):
                at[h*HD:(h+1)*HD,:]=low[:,h*HD-g.start:(h+1)*HD-g.start]
            dots[n]=jnp.sum(gm[:,g].astype(f32)*low.astype(f32),axis=0,keepdims=True)
            inv[n]=inv[n]*scale
        pg=jnp.dot(vv[span[j],:],gm[:,g],preferred_element_type=f32)
        sg=((st[span[j],g]*inv[n])*(pg-dots[n])).astype(bf16)
        back[n]=back[n]+lax.dot_general(kk[span[j],:],sg,TN,preferred_element_type=f32)
        if j==n_ch-1:
            low=back[n].astype(bf16)
            for h in range(g.start//HD,g.stop//HD):
                qg[h*HD:(h+1)*HD,:]=low[:,h*HD-g.start:(h+1)*HD-g.start]
    for j in range(n_ch): scores(0,j)
    for j in range(n_ch): scores(1,j); expo(0,j)
    for j in range(n_ch): attended(0,j); expo(1,j)
    for j in range(n_ch): attended(1,j); backward(0,j)
    for j in range(n_ch):
        backward(1,j)
        vg[span[j],:]=jnp.dot(pb[span[j],:],gs[...],preferred_element_type=f32)
    cols_ref[c,0:TAGS,:]=jnp.dot(twt_ref[...],at[...],preferred_element_type=f32)
    cols_ref[c,TAGS:TAGS+RANK,:]=jnp.dot(qup_ref[...],qg[...],preferred_element_type=f32)
    qug_ref[...]+=lax.dot_general(low_ref[:RANK,rows],qg[...],NT,preferred_element_type=f32)
    whole=vg[...]
    high=whole.astype(bf16)
    rest=(whole-high.astype(f32)).astype(bf16)
    up=vup_ref[...]
    cot=lax.dot_general(up,high,NT,preferred_element_type=f32)+lax.dot_general(up,rest,NT,preferred_element_type=f32)
    cols_ref[c,TAGS+RANK:,:]=cot[:,own]
    for s in range(TOP):
        o=lax.div(ret[c,s],MB)
        zo=lax.rem(lax.div(o,2),Z)
        mc[lax.div(o,ZC)*ZC+lax.rem(zo,Y)*4+lax.div(zo,Y)*2+lax.rem(o,2)]+=cot[:,s*BLK:(s+1)*BLK]
    side=lt[...]
    vug_ref[...]+=jnp.dot(side,high,preferred_element_type=f32)+jnp.dot(side,rest,preferred_element_type=f32)
    @pl.when(c==pl.num_programs(0)-1)
    def _():
        mcot_ref[...]=mc[...].astype(bf16)

def attend(retrieval,boundary,q,kl,vl,low_t,grad_t,tw_t,qup,vup,pool):
    n=q.shape[0]; wide=q.shape[1]; nk=(TOP+1)*BLK; spans=n//BLK
    vm=pl.BlockSpec(memory_space=pltpu.VMEM)
    V=pltpu.VMEM
    shp=lambda *s: jax.ShapeDtypeStruct(s,f32)
    return pl.pallas_call(attend_kernel,
        grid_spec=pltpu.PrefetchScalarGridSpec(num_scalar_prefetch=2,grid=(spans,),
            in_specs=[pl.BlockSpec(memory_space=pl.ANY)]*9,
            out_specs=[vm]*4,
            scratch_shapes=[V(a.shape,a.dtype) for a in (q,kl,vl,low_t,grad_t,tw_t,qup,vup)]+[
              V((spans*TOP,ROWS,HD),bf16),V((nk,HD),bf16),V((nk,HD),bf16),V((RANK,nk),bf16),
              V((wide,HD),bf16),V((HD,wide),bf16),V((wide,HD),bf16),
              V((nk,wide),f32),V((nk,wide),bf16),
              V((wide,BLK),bf16),V((wide,BLK),bf16),V((nk,HD),f32),V((OWNERS,RANK,BLK),f32),
              pltpu.SemaphoreType.DMA((spans*TOP,)),pltpu.SemaphoreType.DMA((8,))]),
        out_shape=[shp(spans,TAGS+2*RANK,BLK),shp(RANK,wide),shp(RANK,HD),jax.ShapeDtypeStruct((OWNERS,RANK,BLK),bf16)],
        compiler_params=pltpu.CompilerParams(vmem_limit_bytes=60*2**20,dimension_semantics=("arbitrary",)),
    )(retrieval,boundary,q,kl,vl,low_t,grad_t,tw_t,qup,vup,pool)

def place():
    t=lax.axis_index("tm"); y=lax.axis_index("heads")
    return lax.div(t,ZC), y, lax.rem(t,ZC)

def reduce_kernel(asked_hbm, cols_hbm, qug_hbm, vug_hbm, mcot_hbm, slab_hbm, mem_hbm,
                  logit_out, grad_out,
                  asked_ref, cols_ref, qug_ref, vug_ref, mcot_ref, slab_ref, mem_ref, wbuf, xbuf, tbuf, zbuf, mall, cbuf, lall, call, g1, r1, x1, o1, g2, r2, x2, o2,
                  xs, ys, zs, ms, cs, ls, ks, a1, b1, d1, a2, b2, d2, lsem):
    x,y,q=place()
    def xp(k): return (lax.rem(x+k,X)*ZC+q, y)
    def yp(k): return (x*ZC+q, lax.rem(y+k,Y))
    def zp(k): return (x*ZC+lax.rem(q+k,ZC), y)
    def xyp(k): return (lax.rem(x+lax.div(k,Y),X)*ZC+q, lax.rem(y+lax.rem(k,Y),Y))
    def each(n,do):
        def body(k,_):
            do(k); return 0
        lax.fori_loop(1,n,body,0)
    def rc(src,dst,sems,k,dev):
        return pltpu.make_async_remote_copy(src_ref=src,dst_ref=dst,send_sem=sems.at[0,k],recv_sem=sems.at[1,k],device_id=dev,device_id_type=MESH)
    loads=[pltpu.make_async_copy(a,b,lsem.at[i]) for i,(a,b) in enumerate([(mcot_hbm,mcot_ref),(cols_hbm,cols_ref),(asked_hbm,asked_ref),(slab_hbm,slab_ref),(qug_hbm,qug_ref),(vug_hbm,vug_ref),(mem_hbm,mem_ref)])]
    for cp in loads: cp.start()
    bar=pltpu.get_barrier_semaphore()
    each(X*Y,lambda k: pl.semaphore_signal(bar,inc=1,device_id=xyp(k),device_id_type=MESH))
    each(ZC,lambda k: pl.semaphore_signal(bar,inc=1,device_id=zp(k),device_id_type=MESH))
    for i in range(2): loads[i].wait()
    pl.semaphore_wait(bar,X*Y+ZC-2)
    def slots(k): return pl.ds(lax.rem(x+lax.div(k,Y),X)*ZC+lax.rem(y+lax.rem(k,Y),Y)*4,4)
    mx=lambda k: rc(mcot_ref.at[slots(k)],xbuf.at[k],xs,k,xyp(k))
    cy=lambda k: rc(cols_ref.at[lax.rem(y+k,Y)],cbuf.at[k],cs,k,yp(k))
    each(X*Y,lambda k: mx(k).start())
    each(Y,lambda k: cy(k).start())
    def owner(j):
        half,core=(j//2,j%2) if isinstance(j,int) else (lax.div(j,2),lax.rem(j,2))
        return (y+Y*half)*2+core
    loads[2].wait()
    for j in range(4):
        for m in range(MB):
            for k in range(X):
                hit=jnp.where(asked_ref[k]==(x*ZC+owner(j))*MB+m,1.0,0.0).astype(f32)
                wbuf[j,m,k:k+1,:]=jnp.broadcast_to(jnp.max(jnp.max(hit,axis=0,keepdims=True),axis=1,keepdims=True),(1,128))
    each(Y,lambda k: cy(k).wait())
    total=cols_ref[y]+cbuf[1]+cbuf[2]+cbuf[3]
    lall[y]=total[:TAGS]
    call[y]=total[TAGS:].astype(bf16)
    ly=lambda k: rc(lall.at[y],lall.at[y],ls,k,yp(k))
    ky=lambda k: rc(call.at[y],call.at[y],ks,k,yp(k))
    each(Y,lambda k: ky(k).start())
    each(Y,lambda k: ly(k).start())
    xbuf[0]=mcot_ref[slots(0)]
    each(X*Y,lambda k: mx(k).wait())
    def expand(j,_):
        parts=[]
        for k in range(X):
            s=xbuf[Y*k,j].astype(f32)
            for i in range(1,Y): s=s+xbuf[Y*k+i,j].astype(f32)
            parts.append(s)
        for m in range(MB):
            acc=parts[0]*wbuf[j,m,0:1,:]
            for k in range(1,X):
                acc=acc+parts[k]*wbuf[j,m,k:k+1,:]
            tbuf[j,m]=acc.astype(bf16)
        return 0
    lax.fori_loop(0,4,expand,0)
    home=lax.rem(lax.div(q,2),Y)==y
    for j in range(4):
        @pl.when(owner(j)!=q)
        def _():
            pltpu.make_async_remote_copy(src_ref=tbuf.at[j],dst_ref=zbuf.at[q],send_sem=ys.at[0,j],recv_sem=zs.at[1,q],device_id=(x*ZC+owner(j),y),device_id_type=MESH).start()
    each(Y,lambda k: ky(k).wait())
    def split(ref,first,value):
        for j in range(value.shape[1]//128):
            ref[first+2*j]=value[0:8,j*128:(j+1)*128]
            ref[first+2*j+1]=value[8:16,j*128:(j+1)*128]
    qdg=jnp.zeros(qug_ref.shape,f32); vdg=jnp.zeros(qug_ref.shape,f32)
    for i in range(3,6): loads[i].wait()
    for s in range(Y):
        piece=slab_ref[s*BLK:(s+1)*BLK,:]
        qdg=qdg+jnp.dot(call[s,0:RANK],piece,preferred_element_type=f32)
        vdg=vdg+jnp.dot(call[s,RANK:],piece,preferred_element_type=f32)
    split(g1,0,qdg); split(g1,14,qug_ref[...]); split(g1,28,vug_ref[...])
    g1[30]=jnp.zeros((8,128),f32); g1[31]=jnp.zeros((8,128),f32)
    ga=lambda k: rc(g1.at[pl.ds(lax.rem(q+k,ZC)*2,2)],r1.at[k],a1,k,zp(k))
    each(ZC,lambda k: ga(k).start())
    from_y=lax.rem(lax.div(q,2),Y)
    my=lambda k: rc(mall,mall,ms,k,yp(k))
    @pl.when(home)
    def _():
        zbuf[q]=tbuf[lax.div(q,8)*2+lax.rem(q,2)]
        def arrive(s,_):
            @pl.when(s!=q)
            def _(): rc(tbuf.at[0],zbuf.at[s],zs,s,(x*ZC+q,y)).wait_recv()
            return 0
        lax.fori_loop(0,ZC,arrive,0)
        for m in range(MB):
            acc=zbuf[0,m].astype(f32)
            for s in range(1,ZC): acc=acc+zbuf[s,m].astype(f32)
            mall[m]=acc.astype(bf16)
        each(Y,lambda k: my(k).start())
    each(ZC,lambda k: ga(k).wait())
    acc=g1[pl.ds(q*2,2)]
    for k in range(1,ZC): acc=acc+r1[k]
    x1[x]=acc
    gb=lambda k: rc(x1.at[x],x1.at[x],b1,k,xp(k))
    each(X,lambda k: gb(k).start())
    @pl.when(jnp.logical_not(home))
    def _(): my(lax.rem(y+Y-from_y,Y)).wait_recv()
    loads[6].wait()
    for m in range(MB):
        vdg=vdg+jnp.dot(mall[m],mem_ref[m*BLK:(m+1)*BLK,:],preferred_element_type=f32)
    split(g2,0,vdg)
    g2[14]=jnp.zeros((8,128),f32); g2[15]=jnp.zeros((8,128),f32)
    ha=lambda k: rc(g2.at[lax.rem(q+k,ZC)],r2.at[k],a2,k,zp(k))
    each(ZC,lambda k: ha(k).start())
    each(X,lambda k: gb(k).wait())
    o1[q]=x1[0]+x1[1]+x1[2]+x1[3]
    gd=lambda k: rc(o1.at[q],o1.at[q],d1,k,zp(k))
    each(ZC,lambda k: gd(k).start())
    each(ZC,lambda k: ha(k).wait())
    acc=g2[q]
    for k in range(1,ZC): acc=acc+r2[k]
    x2[x]=acc
    hb=lambda k: rc(x2.at[x],x2.at[x],b2,k,xp(k))
    each(X,lambda k: hb(k).start())
    each(X,lambda k: hb(k).wait())
    o2[q]=x2[0]+x2[1]+x2[2]+x2[3]
    hd=lambda k: rc(o2.at[q],o2.at[q],d2,k,zp(k))
    each(ZC,lambda k: hd(k).start())
    each(Y,lambda k: ly(k).wait())
    for s in range(Y):
        logit_out[:,s*BLK:(s+1)*BLK]=lall[s]
    for j in range(4):
        @pl.when(owner(j)!=q)
        def _(): pltpu.make_async_remote_copy(src_ref=tbuf.at[j],dst_ref=zbuf.at[q],send_sem=ys.at[0,j],recv_sem=zs.at[1,q],device_id=(x*ZC+owner(j),y),device_id_type=MESH).wait_send()
    @pl.when(home)
    def _(): each(Y,lambda k: my(k).wait_send())
    each(ZC,lambda k: gd(k).wait())
    for k in range(15):
        for i in range(2):
            grad_out[i*8:(i+1)*8,k*128:(k+1)*128]=o1[k,i]
    each(ZC,lambda k: hd(k).wait())
    for k in range(14):
        grad_out[(k%2)*8:(k%2)*8+8,(15+k//2)*128:(16+k//2)*128]=o2[k]

def reduce_all(asked,cols,qug,vug,mcot,slab,mem):
    vm=pl.BlockSpec(memory_space=pltpu.VMEM)
    wide=qug.shape[1]
    V=pltpu.VMEM
    sem=lambda n: pltpu.SemaphoreType.DMA((2,n))
    return pl.pallas_call(reduce_kernel,
        in_specs=[pl.BlockSpec(memory_space=pl.ANY)]*7,
        out_specs=[vm,vm],
        out_shape=[jax.ShapeDtypeStruct((TAGS,slab.shape[0]),f32),jax.ShapeDtypeStruct((RANK,3*wide+HD),f32)],
        scratch_shapes=[V(a.shape,a.dtype) for a in (asked,cols,qug,vug,mcot,slab,mem)]+[V((4,MB,8,128),f32),V((X*Y,4,RANK,BLK),bf16),V((4,MB,RANK,BLK),bf16),V((ZC,MB,RANK,BLK),bf16),V((MB,RANK,BLK),bf16),
            V((Y,TAGS+2*RANK,BLK),f32),V((Y,TAGS,BLK),f32),V((Y,2*RANK,BLK),bf16),
            V((32,8,128),f32),V((ZC,2,8,128),f32),V((X,2,8,128),f32),V((ZC,2,8,128),f32),
            V((16,8,128),f32),V((ZC,8,128),f32),V((X,8,128),f32),V((ZC,8,128),f32),
            sem(X*Y),sem(4),sem(ZC),sem(Y),sem(Y),sem(Y),sem(Y),sem(ZC),sem(X),sem(ZC),sem(ZC),sem(X),sem(ZC),pltpu.SemaphoreType.DMA((7,))],
        compiler_params=pltpu.CompilerParams(collective_id=1,has_side_effects=True,vmem_limit_bytes=60*2**20),
    )(asked,cols,qug,vug,mcot,slab,mem)

def unpack_kernel(logits, grads, a, b, c, d, e):
    wide=b.shape[1]
    a[...]=logits[...]
    b[...]=grads[:,0:wide]
    c[...]=grads[:,wide:2*wide]
    d[...]=grads[:,2*wide+HD:]
    e[...]=grads[:,2*wide:2*wide+HD]

def unpack(logits,grads,wide):
    S=jax.ShapeDtypeStruct; vm=pl.BlockSpec(memory_space=pltpu.VMEM)
    return pl.pallas_call(unpack_kernel,in_specs=[vm]*2,out_specs=[vm]*5,
        out_shape=[S(logits.shape,f32)]+[S((RANK,wide),f32)]*3+[S((RANK,HD),f32)],
        compiler_params=pltpu.CompilerParams(vmem_limit_bytes=60*2**20))(logits,grads)

UNIT=[(0,0,64),(0,64,64),(1,0,128),(2,0,128),(3,0,128),(4,0,128),(5,0,128),(6,0,128),(7,0,128)]
ROUND=[(0,0,128),(0,128,272),(1,0,272),(2,0,272),(3,0,272)]
UNITS=len(UNIT); RN=len(ROUND); DONE=3
FIRST={-1:[0],0:[1],1:[2],2:[3],3:[4],4:[5],5:[6],6:[7],7:[8]}
PLAN={(1, 0): [(0, 1)], (2, 0): [(0, 2), (1, 1)], (3, 0): [(0, 3), (1, 2), (2, 1)], (4, 0): [(0, 4), (1, 3), (2, 2), (3, 1)], (5, 0): [(0, 5), (1, 4), (2, 3), (3, 2), (4, 1)], (6, 0): [(1, 5), (2, 4), (3, 3), (4, 2)], (7, 0): [(2, 5), (3, 4), (4, 3)], (8, 0): [(3, 5), (4, 4)], (8, 1): [(4, 5)]}

def gather_kernel(mem_ref, slab_ref, wq_ref, wk_ref, wv_ref, qdown_hbm, vdown_hbm, qup_hbm, vup_hbm, ret_hbm,
                  pool, q_hbm, k_hbm, v_hbm, low_hbm, asked_out,
                  q_out, k_out, v_out, low_out, feat, wq, wkv, qdown_ref, vdown_ref, qup_ref, vup_ref, ret_ref, stage, mine, ysem, ssem, rsem, lsem, psem, osem, xsem, wsem):
    t=lax.axis_index("tm"); y=lax.axis_index("heads")
    x=lax.div(t,ZC); z=lax.rem(lax.div(t,2),Z); c=lax.rem(t,2)
    def tm(xx,zz,cc): return (xx*Z+zz)*2+cc
    xk=[lax.rem(x+k,X) for k in range(X)]
    devx=[(tm(xk[k],z,c),y) for k in range(X)]
    devz=[(tm(x,lax.rem(z+1,Z),c),y),(tm(x,lax.rem(z+Z-1,Z),c),y)]
    devc=(tm(x,z,1-c),y)
    devy=[(t,lax.rem(y+1,Y)),(t,lax.rem(y+Y-1,Y))]
    def rows_of(u):
        fb,r0,n=UNIT[u]
        return (mem_ref if fb<MB else slab_ref).at[pl.ds(fb%MB*BLK+r0,n)]
    own=lambda fb: pltpu.make_async_copy((mem_ref if fb<MB else slab_ref).at[pl.ds(fb%MB*BLK,BLK)],feat.at[fb,y],osem.at[fb])
    loads=[pltpu.make_async_copy(a,b,lsem.at[i]) for i,(a,b) in enumerate([(wk_ref,wkv.at[:,0:HD]),(wv_ref,wkv.at[:,HD:2*HD]),(vdown_hbm,vdown_ref),(vup_hbm,vup_ref),(ret_hbm,ret_ref),(wq_ref,wq),(qdown_hbm,qdown_ref),(qup_hbm,qup_ref)])]
    bar=pltpu.get_barrier_semaphore()
    for dev in devx[1:]+devz+devy+[devc]:
        pl.semaphore_signal(bar,inc=1,device_id=dev,device_id_type=MESH)
    for cp in loads[:4]: cp.start()
    pl.semaphore_wait(bar,X-1+5)

    def rc(src,dst,s,r,dev):
        return pltpu.make_async_remote_copy(src_ref=src,dst_ref=dst,send_sem=s,recv_sem=r,device_id=dev,device_id_type=MESH)
    left=lax.rem(y+Y-1,Y); right=lax.rem(y+1,Y)
    def piece_of(u,h,half=None):
        fb,r0,n=UNIT[u]
        return feat.at[fb,h,pl.ds(r0,n) if half is None else pl.ds(r0+half*(n//2),n//2)]
    def y_first(u): return [rc(rows_of(u),piece_of(u,y),ysem.at[0,u,i],ysem.at[1,u,i],devy[i]) for i in range(2)]
    def y_pass(u): return [rc(piece_of(u,h,i),piece_of(u,h,i),ysem.at[0,u,2+i],ysem.at[1,u,2+i],devy[i]) for i,h in enumerate((left,right))]
    def start(cs):
        for cp in cs: cp.start()
    asked=lambda k: rc(mine,asked_out.at[k],xsem.at[0,k],xsem.at[1,k],devx[k])

    def part(r,cc,xs,zs):
        b,lo,hi=ROUND[r]
        return pool.at[b,cc,xs,zs,pl.ds(lo,hi-lo)]
    def fresh(r):
        b,lo,hi=ROUND[r]
        return stage.at[b,pl.ds(lo,hi-lo)]
    every=pl.ds(0,X)
    GROUP=[pl.ds(0,1),pl.ds(1,2),pl.ds(3,2),pl.ds(5,2),pl.ds(7,1)]
    def share(b,cc,g): return rc(part(b,cc,every,GROUP[g]),part(b,cc,every,GROUP[g]),ssem.at[b,32+g],rsem.at[b,32+g],devc)
    def keep(b): return pltpu.make_async_copy(fresh(b),part(b,c,x,0),psem.at[b])
    def x_own(b,k): return rc(fresh(b),part(b,0,x,0),ssem.at[b,k-1],rsem.at[b,k],devx[k])
    back=[x]+[lax.rem(x+X-k,X) for k in range(1,X)]
    def hop0(b,l,i,k):
        src=part(b,0,back[k],0 if l==0 else 2*l-1+i)
        return rc(fresh(b) if l==0 and k==0 else src,part(b,0,back[k],2*l+1+i),ssem.at[b,3+8*l+2*k+i],rsem.at[b,4+8*l+2*k+i],devz[i])
    def last0(b,k):
        low=back[k]<X//2
        dev=(jnp.where(low,devz[0][0],devz[1][0]),y)
        return rc(part(b,0,back[k],jnp.where(low,5,6)),part(b,0,back[k],7),ssem.at[b,27+k],rsem.at[b,28+k],dev)
    def core0(b,phase):
        if phase==1:
            for k in range(1,X):
                x_own(b,k).wait_recv()
                for i in range(2): hop0(b,0,i,k).start()
            keep(b).wait()
        elif phase<5:
            l=phase-1
            for k in range(X):
                for i in range(2):
                    hop0(b,l-1,i,k).wait_recv()
                    if l<3: hop0(b,l,i,k).start()
                if l==3: last0(b,k).start()
        else:
            for k in range(X): last0(b,k).wait_recv()
        share(b,0,phase-1).start()
    def hop1(b,l,i):
        src=fresh(b) if l==0 else part(b,1,x,2*l-1+i)
        return rc(src,part(b,1,x,2*l+1+i if l<3 else 7),ssem.at[b,3+2*l+i if l<3 else 9],rsem.at[b,4+2*l+i if l<3 else 10],devz[i])
    def spread(b,g,k):
        src=part(b,1,x,0 if g==0 else GROUP[g])
        return rc(fresh(b) if g==0 else src,src,ssem.at[b,12+5*(k-1)+g],rsem.at[b,12+5*(k-1)+g],devx[k])
    def pass_on(b,g):
        for k in range(1,X): spread(b,g,k).wait_recv()
        share(b,1,g).start()
    def core1(b,phase):
        if phase<4:
            l=phase
            for i in range(2):
                hop1(b,l-1,i).wait_recv()
                if l<3 or b%2==i: hop1(b,l,i).start()
            for k in range(1,X): spread(b,l,k).start()
        elif phase==4:
            hop1(b,3,b%2).wait_recv()
            for k in range(1,X): spread(b,4,k).start()
        if phase==1: keep(b).wait()
        if phase in (2,3,4): pass_on(b,phase-2)
        if phase==5:
            pass_on(b,3); pass_on(b,4)
    def begin(b):
        keep(b).start()
        @pl.when(c==0)
        def _():
            for i in range(2): hop0(b,0,i,0).start()
            for k in range(1,X): x_own(b,k).start()
        @pl.when(c==1)
        def _():
            for i in range(2): hop1(b,0,i).start()
            for k in range(1,X): spread(b,0,k).start()
    def step(b,phase):
        pl.when(c==0)(lambda: core0(b,phase))
        pl.when(c==1)(lambda: core1(b,phase))

    def leave(b):
        rows=pl.ds(b*BLK,BLK)
        jobs=[(q_out.at[rows],q_hbm.at[rows]),(k_out.at[rows],k_hbm.at[rows]),(v_out.at[rows],v_hbm.at[rows]),(low_out.at[:,rows],low_hbm.at[:,rows])]
        return [pltpu.make_async_copy(src,dst,wsem.at[b,i]) for i,(src,dst) in enumerate(jobs)]
    def project(u):
        fb,r0,n=UNIT[u]
        if r0==0: own(fb).wait()
        if u==0:
            for i in range(4): loads[i].wait()
        memory=fb<MB
        if fb==MB:
            for i in range(5,8): loads[i].wait()
        pair=jnp.zeros((n,2*HD),f32)
        low=jnp.zeros((RANK if memory else 2*RANK,n),f32)
        wide=wq.shape[1]
        for h in range(Y):
            cols=slice(h*wide,(h+1)*wide)
            piece=feat[fb,h,r0:r0+n]
            pair=pair+jnp.dot(piece,wkv[cols,:],preferred_element_type=f32)
            down=vdown_ref[:,cols] if memory else jnp.concatenate([qdown_ref[:,cols],vdown_ref[:,cols]],axis=0)
            low=low+lax.dot_general(down,piece,NT,preferred_element_type=f32)
        low=low.astype(bf16)
        keys=pair[:,:HD].astype(bf16)
        values=(pair[:,HD:]+lax.dot_general(low[-RANK:],vup_ref[...],TN,preferred_element_type=f32)).astype(bf16)
        if memory:
            for i in range(0,n,64):
                stage[fb,2*(r0+i):2*(r0+i)+64,:]=keys[i:i+64]
                stage[fb,2*(r0+i)+64:2*(r0+i)+128,:]=values[i:i+64]
            stage[fb,2*BLK:,r0:r0+n]=low
        else:
            b=fb-MB
            rows=slice(b*BLK,(b+1)*BLK)
            k_out[rows,:]=keys
            v_out[rows,:]=values
            low_out[:,rows]=low
            acc=lax.dot_general(low[:RANK],qup_ref[...],TN,preferred_element_type=f32)
            for h in range(Y):
                acc=acc+jnp.dot(feat[fb,h],wq[h*wide:(h+1)*wide,:],preferred_element_type=f32)
            q_out[rows,:]=acc.astype(bf16)
            for cp in leave(b): cp.start()

    def over(b):
        for g in range(5):
            share(b,1-c,g).wait_recv()
            share(b,c,g).wait_send()
        keepers(b)
    def keepers(b):
        @pl.when(c==0)
        def _():
            for k in range(1,X): x_own(b,k).wait_send()
            for k in range(X):
                for l in range(3):
                    for i in range(2): hop0(b,l,i,k).wait_send()
                last0(b,k).wait_send()
        @pl.when(c==1)
        def _():
            for l in range(3):
                for i in range(2): hop1(b,l,i).wait_send()
            hop1(b,3,b%2).wait_send()
            for g in range(5):
                for k in range(1,X): spread(b,g,k).wait_send()
    def settled(u):
        for cp in y_first(u)+y_pass(u): cp.wait_send()

    for v in FIRST[-1]: start(y_first(v))
    for fb in range(2*MB): own(fb).start()
    for cp in loads[4:]: cp.start()
    mine[...]=jnp.full(mine.shape,-1,jnp.int32)
    loads[4].wait()
    mine[0:MB,0:TOP]=ret_ref[...]
    for k in range(1,X): asked(k).start()
    asked_out[0]=mine[...]
    for u in range(UNITS):
        for cp in y_first(u): cp.wait_recv()
        start(y_pass(u))
        for v in FIRST.get(u,[]): start(y_first(v))
        if u>RN: project(u-1)
        if u>=2: settled(u-2)
        if u==3:
            for k in range(1,X): asked(k).wait()
        if 0<=u-RN-1<DONE: over(u-RN-1)
        for b,p in PLAN.get((u,0),[]): step(b,p)
        for cp in y_pass(u): cp.wait_recv()
        if u<RN:
            project(u)
            begin(u)
        elif u==UNITS-1: project(u)
        for b,p in PLAN.get((u,1),[]): step(b,p)
    for u in range(UNITS-2,UNITS): settled(u)
    for b in range(DONE,RN): over(b)
    for b in range(MB):
        for cp in leave(b): cp.wait()

def gather_all(mem,slab,wq,wk,wv,qdown,vdown,qup,vup,ret):
    vm=pl.BlockSpec(memory_space=pltpu.VMEM); hbm=pl.BlockSpec(memory_space=pl.ANY)
    n=slab.shape[0]; wide=wq.shape[1]
    S=jax.ShapeDtypeStruct; V=pltpu.VMEM; D=pltpu.SemaphoreType.DMA
    return pl.pallas_call(gather_kernel,
        in_specs=[hbm]*10,
        out_specs=[hbm]*5+[vm],
        out_shape=[S((MB,2,X,Z,ROWS,HD),bf16),S((n,wide),bf16),S((n,HD),bf16),S((n,HD),bf16),S((2*RANK,n),bf16),S((X,8,128),jnp.int32)],
        scratch_shapes=[V((n,wide),bf16),V((n,HD),bf16),V((n,HD),bf16),V((2*RANK,n),bf16),V((2*MB,Y,BLK,wide),bf16),V(wq.shape,bf16),V((wq.shape[0],2*HD),bf16),V(qdown.shape,bf16),V(vdown.shape,bf16),V(qup.shape,bf16),V(vup.shape,bf16),V(ret.shape,jnp.int32),
            V((MB,ROWS,HD),bf16),V((8,128),jnp.int32),
            D((2,UNITS,4)),D((RN,37)),D((RN,37)),D((8,)),D((RN,)),D((2*MB,)),D((2,X)),D((MB,4))],
        compiler_params=pltpu.CompilerParams(collective_id=2,has_side_effects=True,vmem_limit_bytes=60*2**20),
    )(mem,slab,wq,wk,wv,qdown,vdown,qup,vup,ret)

def local(slab_tokens,memory,query_weight,key_weight,value_weight,query_down,query_up,value_down,value_up,tag_weight,retrieval,boundary,grad_tags):
    pool,queries,keys,values,low_t,asked=gather_all(memory,slab_tokens,query_weight,key_weight,value_weight,query_down,value_down,query_up,value_up,retrieval)
    cols,qug,vug,mcot=attend(retrieval,boundary,queries,keys,values,low_t,grad_tags.T,tag_weight.T,query_up,value_up,pool)
    logits,grads=reduce_all(asked,cols,qug,vug,mcot,slab_tokens,memory)
    logits,a,b,c,d=unpack(logits,grads,qug.shape[1])
    return logits.T,a,b,c,d


def solution(mesh):
    in_specs=(P("tm","heads"),P("tm","heads"),P(None,"heads"),P(None,"heads"),P(None,"heads"),P(),P(None,"heads"),P(),P(None,"heads"),P("heads",None),P("tm",None),P("tm"),P("tm",None))
    out_specs=(P("tm",None),P(None,"heads"),P(None,"heads"),P(None,"heads"),P(None,"heads"))
    return jax.shard_map(local,mesh=mesh,in_specs=in_specs,out_specs=out_specs,check_vma=False)
```

```python
import functools
import jax, jax.numpy as jnp
from jax import lax
from jax.sharding import PartitionSpec as P
from jax.experimental import pallas as pl
from jax.experimental.pallas import tpu as pltpu
BLK=128; HD=128; TOP=8; RANK=16; TAGS=8
HIGHEST=lax.Precision.HIGHEST
NT=(((1,),(1,)),((),()))
TN=(((0,),(0,)),((),()))
f32=jnp.float32; bf16=jnp.bfloat16
MB=4; OWNERS=64; ROWS=272; CH=384; X=4; Y=4; Z=8; ZC=16; LOG2E=1.4426950408889634; MESH=pl.DeviceIdType.MESH
def attend_kernel(ret,bnd, q_hbm, kl_hbm, vl_hbm, low_hbm, gt_hbm, twt_hbm, qup_hbm, vup_hbm, pool_ref,
                  cols_ref, qug_ref, vug_ref, mcot_ref,
                  q_ref, kl_ref, vl_ref, low_ref, gt_ref, twt_ref, qup_ref, vup_ref,
                  land, kk, vv, lt, qs, gm, gs, st, pb, at, qg, vg, mc, sems, lsem):
    c=pl.program_id(0)
    heads=q_ref.shape[1]//HD
    wide=heads*BLK
    nkeys=(TOP+1)*BLK
    z=lax.rem(lax.div(lax.axis_index("tm"),2),Z)
    def fetch(i):
        g=ret[lax.div(i,TOP),lax.rem(i,TOP)]
        o=lax.div(g,MB)
        d=lax.rem(lax.rem(lax.div(o,2),Z)+Z-z,Z)
        slot=jnp.where(d==0,0,jnp.where(d<Z//2,2*d,jnp.where(d==Z//2,Z-1,2*(Z-d)-1)))
        return pltpu.make_async_copy(pool_ref.at[lax.rem(g,MB),lax.rem(o,2),lax.div(o,ZC),slot], land.at[i], sems.at[i])
    loads=[pltpu.make_async_copy(src,dst,lsem.at[i]) for i,(src,dst) in enumerate([(q_hbm,q_ref),(kl_hbm,kl_ref),(vl_hbm,vl_ref),(low_hbm,low_ref),(gt_hbm,gt_ref),(twt_hbm,twt_ref),(qup_hbm,qup_ref),(vup_hbm,vup_ref)])]
    @pl.when(c==0)
    def _():
        for cp in loads: cp.start()
        def go(i,_):
            fetch(i).start(); return 0
        lax.fori_loop(0,4*TOP,go,0)
        qug_ref[...]=jnp.zeros_like(qug_ref)
        vug_ref[...]=jnp.zeros_like(vug_ref)
        mc[...]=jnp.zeros_like(mc)
        for cp in loads: cp.wait()
    rows=pl.ds(pl.multiple_of(c*BLK,BLK),BLK)
    part=gt_ref[:,rows]
    terms=[]
    for _ in range(3):
        low=part.astype(bf16).astype(f32)
        terms.append(low); part=part-low
    grads=jnp.concatenate(terms+[jnp.zeros_like(part)],axis=0).astype(bf16)
    tags=jnp.concatenate([twt_ref[...].astype(f32)]*4,axis=0).astype(bf16)
    across=lax.dot_general(tags,grads,TN,preferred_element_type=f32).astype(bf16)
    down=lax.dot_general(grads,tags,TN,preferred_element_type=f32).astype(bf16)
    for h in range(heads):
        cols=slice(h*HD,(h+1)*HD)
        gm[:,cols]=across[cols,:]
        gs[cols,:]=down[:,cols]
        qs[cols,:]=q_ref[rows,cols]
    for s in range(TOP):
        i=c*TOP+s
        fetch(i).wait()
        for half in range(2):
            dst=slice(s*BLK+half*64,s*BLK+half*64+64)
            kk[dst,:]=land[i,half*128:half*128+64,:]
            vv[dst,:]=land[i,half*128+64:half*128+128,:]
        lt[:,s*BLK:(s+1)*BLK]=land[i,256:272,:]
    own=slice(TOP*BLK,nkeys)
    kk[own,:]=kl_ref[rows,:]
    vv[own,:]=vl_ref[rows,:]
    lt[:,own]=low_ref[RANK:,rows]
    edge=bnd[c]
    scale=HD**-0.5
    n_ch=nkeys//CH
    split=(heads+1)//2*HD
    groups=[slice(0,split),slice(split,wide)]
    span=[slice(j*CH,(j+1)*CH) for j in range(n_ch)]
    key=lax.broadcasted_iota(jnp.int32,(BLK,BLK),0)
    row=lax.broadcasted_iota(jnp.int32,(BLK,BLK),1)
    seen=(key<=row)&((key>=edge)|(row<edge))
    bias=jnp.where(seen,0.0,-jnp.inf).astype(f32)
    most=[jnp.full((1,g.stop-g.start),-jnp.inf,f32) for g in groups]
    total=[jnp.zeros((1,g.stop-g.start),f32) for g in groups]
    out=[jnp.zeros((HD,g.stop-g.start),f32) for g in groups]
    back=[jnp.zeros((HD,g.stop-g.start),f32) for g in groups]
    inv=[None,None]; dots=[None,None]
    def scores(n,j):
        g=groups[n]
        s=lax.dot_general(kk[span[j],:],qs[g,:],NT,preferred_element_type=f32)
        if j==n_ch-1:
            last=s[CH-BLK:]+jnp.concatenate([bias]*((g.stop-g.start)//BLK),axis=1)
            s=jnp.concatenate([s[:CH-BLK],last],axis=0)
        st[span[j],g]=s
        most[n]=jnp.maximum(most[n],jnp.max(s,axis=0,keepdims=True))
    def expo(n,j):
        e=jnp.exp2((st[span[j],groups[n]]-most[n])*(scale*LOG2E))
        st[span[j],groups[n]]=e
        total[n]=total[n]+jnp.sum(e,axis=0,keepdims=True)
    def attended(n,j):
        if j==0: inv[n]=1.0/total[n]
        low=(st[span[j],groups[n]]*inv[n]).astype(bf16)
        pb[span[j],groups[n]]=low
        out[n]=out[n]+lax.dot_general(vv[span[j],:],low,TN,preferred_element_type=f32)
    def backward(n,j):
        g=groups[n]
        if j==0:
            low=out[n].astype(bf16)
            for h in range(g.start//HD,g.stop//HD):
                at[h*HD:(h+1)*HD,:]=low[:,h*HD-g.start:(h+1)*HD-g.start]
            dots[n]=jnp.sum(gm[:,g].astype(f32)*low.astype(f32),axis=0,keepdims=True)
            inv[n]=inv[n]*scale
        pg=jnp.dot(vv[span[j],:],gm[:,g],preferred_element_type=f32)
        sg=((st[span[j],g]*inv[n])*(pg-dots[n])).astype(bf16)
        back[n]=back[n]+lax.dot_general(kk[span[j],:],sg,TN,preferred_element_type=f32)
        if j==n_ch-1:
            low=back[n].astype(bf16)
            for h in range(g.start//HD,g.stop//HD):
                qg[h*HD:(h+1)*HD,:]=low[:,h*HD-g.start:(h+1)*HD-g.start]
    for j in range(n_ch): scores(0,j)
    for j in range(n_ch): scores(1,j); expo(0,j)
    for j in range(n_ch): attended(0,j); expo(1,j)
    for j in range(n_ch): attended(1,j); backward(0,j)
    for j in range(n_ch):
        backward(1,j)
        vg[span[j],:]=jnp.dot(pb[span[j],:],gs[...],preferred_element_type=f32)
    cols_ref[c,0:TAGS,:]=jnp.dot(twt_ref[...],at[...],preferred_element_type=f32)
    cols_ref[c,TAGS:TAGS+RANK,:]=jnp.dot(qup_ref[...],qg[...],preferred_element_type=f32)
    qug_ref[...]+=lax.dot_general(low_ref[:RANK,rows],qg[...],NT,preferred_element_type=f32)
    whole=vg[...]
    high=whole.astype(bf16)
    rest=(whole-high.astype(f32)).astype(bf16)
    up=vup_ref[...]
    both=jnp.concatenate([high,rest],axis=1)
    cot=lax.dot_general(jnp.concatenate([up,up],axis=1),both,NT,preferred_element_type=f32)
    cols_ref[c,TAGS+RANK:,:]=cot[:,own]
    for s in range(TOP):
        o=lax.div(ret[c,s],MB)
        zo=lax.rem(lax.div(o,2),Z)
        mc[lax.div(o,ZC)*ZC+lax.rem(zo,Y)*4+lax.div(zo,Y)*2+lax.rem(o,2)]+=cot[:,s*BLK:(s+1)*BLK]
    side=lt[...]
    sums=jnp.dot(side,both,preferred_element_type=f32)
    vug_ref[...]+=sums[:,:HD]+sums[:,HD:]
    @pl.when(c==pl.num_programs(0)-1)
    def _():
        mcot_ref[...]=mc[...].astype(bf16)

def attend(retrieval,boundary,q,kl,vl,low_t,grad_t,tw_t,qup,vup,pool):
    n=q.shape[0]; wide=q.shape[1]; nk=(TOP+1)*BLK; spans=n//BLK
    vm=pl.BlockSpec(memory_space=pltpu.VMEM)
    V=pltpu.VMEM
    shp=lambda *s: jax.ShapeDtypeStruct(s,f32)
    return pl.pallas_call(attend_kernel,
        grid_spec=pltpu.PrefetchScalarGridSpec(num_scalar_prefetch=2,grid=(spans,),
            in_specs=[pl.BlockSpec(memory_space=pl.ANY)]*9,
            out_specs=[vm]*4,
            scratch_shapes=[V(a.shape,a.dtype) for a in (q,kl,vl,low_t,grad_t,tw_t,qup,vup)]+[
              V((spans*TOP,ROWS,HD),bf16),V((nk,HD),bf16),V((nk,HD),bf16),V((RANK,nk),bf16),
              V((wide,HD),bf16),V((HD,wide),bf16),V((wide,HD),bf16),
              V((nk,wide),f32),V((nk,wide),bf16),
              V((wide,BLK),bf16),V((wide,BLK),bf16),V((nk,HD),f32),V((OWNERS,RANK,BLK),f32),
              pltpu.SemaphoreType.DMA((spans*TOP,)),pltpu.SemaphoreType.DMA((8,))]),
        out_shape=[shp(spans,TAGS+2*RANK,BLK),shp(RANK,wide),shp(RANK,HD),jax.ShapeDtypeStruct((OWNERS,RANK,BLK),bf16)],
        compiler_params=pltpu.CompilerParams(vmem_limit_bytes=60*2**20,dimension_semantics=("arbitrary",)),
    )(retrieval,boundary,q,kl,vl,low_t,grad_t,tw_t,qup,vup,pool)

def place():
    t=lax.axis_index("tm"); y=lax.axis_index("heads")
    return lax.div(t,ZC), y, lax.rem(t,ZC)

def reduce_kernel(asked_hbm, cols_hbm, qug_hbm, vug_hbm, mcot_hbm, slab_hbm, mem_hbm,
                  logit_out, grad_out,
                  asked_ref, cols_ref, qug_ref, vug_ref, mcot_ref, slab_ref, mem_ref, wbuf, xbuf, tbuf, zbuf, mall, cbuf, lall, call, g1, r1, x1, o1, g2, r2, x2, o2,
                  xs, ys, zs, ms, cs, ls, ks, a1, b1, d1, a2, b2, d2, lsem):
    x,y,q=place()
    def xp(k): return (lax.rem(x+k,X)*ZC+q, y)
    def yp(k): return (x*ZC+q, lax.rem(y+k,Y))
    def zp(k): return (x*ZC+lax.rem(q+k,ZC), y)
    def xyp(k): return (lax.rem(x+lax.div(k,Y),X)*ZC+q, lax.rem(y+lax.rem(k,Y),Y))
    def each(n,do):
        def body(k,_):
            do(k); return 0
        lax.fori_loop(1,n,body,0)
    def rc(src,dst,sems,k,dev):
        return pltpu.make_async_remote_copy(src_ref=src,dst_ref=dst,send_sem=sems.at[0,k],recv_sem=sems.at[1,k],device_id=dev,device_id_type=MESH)
    loads=[pltpu.make_async_copy(a,b,lsem.at[i]) for i,(a,b) in enumerate([(mcot_hbm,mcot_ref),(cols_hbm,cols_ref),(asked_hbm,asked_ref),(slab_hbm,slab_ref),(qug_hbm,qug_ref),(vug_hbm,vug_ref),(mem_hbm,mem_ref)])]
    for cp in loads: cp.start()
    bar=pltpu.get_barrier_semaphore()
    each(X*Y,lambda k: pl.semaphore_signal(bar,inc=1,device_id=xyp(k),device_id_type=MESH))
    each(ZC,lambda k: pl.semaphore_signal(bar,inc=1,device_id=zp(k),device_id_type=MESH))
    for i in range(2): loads[i].wait()
    pl.semaphore_wait(bar,X*Y+ZC-2)
    def slots(k): return pl.ds(lax.rem(x+lax.div(k,Y),X)*ZC+lax.rem(y+lax.rem(k,Y),Y)*4,4)
    mx=lambda k: rc(mcot_ref.at[slots(k)],xbuf.at[k],xs,k,xyp(k))
    cy=lambda k: rc(cols_ref.at[lax.rem(y+k,Y)],cbuf.at[k],cs,k,yp(k))
    each(X*Y,lambda k: mx(k).start())
    each(Y,lambda k: cy(k).start())
    def owner(j):
        half,core=(j//2,j%2) if isinstance(j,int) else (lax.div(j,2),lax.rem(j,2))
        return (y+Y*half)*2+core
    loads[2].wait()
    for j in range(4):
        for m in range(MB):
            for k in range(X):
                hit=jnp.where(asked_ref[k]==(x*ZC+owner(j))*MB+m,1.0,0.0).astype(f32)
                wbuf[j,m,k:k+1,:]=jnp.broadcast_to(jnp.max(jnp.max(hit,axis=0,keepdims=True),axis=1,keepdims=True),(1,128))
    each(Y,lambda k: cy(k).wait())
    total=cols_ref[y]+cbuf[1]+cbuf[2]+cbuf[3]
    lall[y]=total[:TAGS]
    call[y]=total[TAGS:].astype(bf16)
    ly=lambda k: rc(lall.at[y],lall.at[y],ls,k,yp(k))
    ky=lambda k: rc(call.at[y],call.at[y],ks,k,yp(k))
    each(Y,lambda k: ky(k).start())
    each(Y,lambda k: ly(k).start())
    xbuf[0]=mcot_ref[slots(0)]
    each(X*Y,lambda k: mx(k).wait())
    def expand(j,_):
        parts=[]
        for k in range(X):
            s=xbuf[Y*k,j].astype(f32)
            for i in range(1,Y): s=s+xbuf[Y*k+i,j].astype(f32)
            parts.append(s)
        for m in range(MB):
            acc=parts[0]*wbuf[j,m,0:1,:]
            for k in range(1,X):
                acc=acc+parts[k]*wbuf[j,m,k:k+1,:]
            tbuf[j,m]=acc.astype(bf16)
        return 0
    lax.fori_loop(0,4,expand,0)
    home=lax.rem(lax.div(q,2),Y)==y
    for j in range(4):
        @pl.when(owner(j)!=q)
        def _():
            pltpu.make_async_remote_copy(src_ref=tbuf.at[j],dst_ref=zbuf.at[q],send_sem=ys.at[0,j],recv_sem=zs.at[1,q],device_id=(x*ZC+owner(j),y),device_id_type=MESH).start()
    each(Y,lambda k: ky(k).wait())
    def split(ref,first,value):
        for j in range(value.shape[1]//128):
            ref[first+2*j]=value[0:8,j*128:(j+1)*128]
            ref[first+2*j+1]=value[8:16,j*128:(j+1)*128]
    qdg=jnp.zeros(qug_ref.shape,f32); vdg=jnp.zeros(qug_ref.shape,f32)
    for i in range(3,6): loads[i].wait()
    for s in range(Y):
        piece=slab_ref[s*BLK:(s+1)*BLK,:]
        qdg=qdg+jnp.dot(call[s,0:RANK],piece,preferred_element_type=f32)
        vdg=vdg+jnp.dot(call[s,RANK:],piece,preferred_element_type=f32)
    split(g1,0,qdg); split(g1,14,qug_ref[...]); split(g1,28,vug_ref[...])
    g1[30]=jnp.zeros((8,128),f32); g1[31]=jnp.zeros((8,128),f32)
    ga=lambda k: rc(g1.at[pl.ds(lax.rem(q+k,ZC)*2,2)],r1.at[k],a1,k,zp(k))
    each(ZC,lambda k: ga(k).start())
    from_y=lax.rem(lax.div(q,2),Y)
    my=lambda k: rc(mall,mall,ms,k,yp(k))
    @pl.when(home)
    def _():
        zbuf[q]=tbuf[lax.div(q,8)*2+lax.rem(q,2)]
        def arrive(s,_):
            @pl.when(s!=q)
            def _(): rc(tbuf.at[0],zbuf.at[s],zs,s,(x*ZC+q,y)).wait_recv()
            return 0
        lax.fori_loop(0,ZC,arrive,0)
        for m in range(MB):
            acc=zbuf[0,m].astype(f32)
            for s in range(1,ZC): acc=acc+zbuf[s,m].astype(f32)
            mall[m]=acc.astype(bf16)
        each(Y,lambda k: my(k).start())
    each(ZC,lambda k: ga(k).wait())
    acc=g1[pl.ds(q*2,2)]
    for k in range(1,ZC): acc=acc+r1[k]
    x1[x]=acc
    gb=lambda k: rc(x1.at[x],x1.at[x],b1,k,xp(k))
    each(X,lambda k: gb(k).start())
    @pl.when(jnp.logical_not(home))
    def _(): my(lax.rem(y+Y-from_y,Y)).wait_recv()
    loads[6].wait()
    for m in range(MB):
        vdg=vdg+jnp.dot(mall[m],mem_ref[m*BLK:(m+1)*BLK,:],preferred_element_type=f32)
    split(g2,0,vdg)
    g2[14]=jnp.zeros((8,128),f32); g2[15]=jnp.zeros((8,128),f32)
    ha=lambda k: rc(g2.at[lax.rem(q+k,ZC)],r2.at[k],a2,k,zp(k))
    each(ZC,lambda k: ha(k).start())
    each(X,lambda k: gb(k).wait())
    o1[q]=x1[0]+x1[1]+x1[2]+x1[3]
    gd=lambda k: rc(o1.at[q],o1.at[q],d1,k,zp(k))
    each(ZC,lambda k: gd(k).start())
    each(ZC,lambda k: ha(k).wait())
    acc=g2[q]
    for k in range(1,ZC): acc=acc+r2[k]
    x2[x]=acc
    hb=lambda k: rc(x2.at[x],x2.at[x],b2,k,xp(k))
    each(X,lambda k: hb(k).start())
    each(X,lambda k: hb(k).wait())
    o2[q]=x2[0]+x2[1]+x2[2]+x2[3]
    hd=lambda k: rc(o2.at[q],o2.at[q],d2,k,zp(k))
    each(ZC,lambda k: hd(k).start())
    each(Y,lambda k: ly(k).wait())
    for s in range(Y):
        logit_out[:,s*BLK:(s+1)*BLK]=lall[s]
    for j in range(4):
        @pl.when(owner(j)!=q)
        def _(): pltpu.make_async_remote_copy(src_ref=tbuf.at[j],dst_ref=zbuf.at[q],send_sem=ys.at[0,j],recv_sem=zs.at[1,q],device_id=(x*ZC+owner(j),y),device_id_type=MESH).wait_send()
    @pl.when(home)
    def _(): each(Y,lambda k: my(k).wait_send())
    each(ZC,lambda k: gd(k).wait())
    for k in range(15):
        for i in range(2):
            grad_out[i*8:(i+1)*8,k*128:(k+1)*128]=o1[k,i]
    each(ZC,lambda k: hd(k).wait())
    for k in range(14):
        grad_out[(k%2)*8:(k%2)*8+8,(15+k//2)*128:(16+k//2)*128]=o2[k]

def reduce_all(asked,cols,qug,vug,mcot,slab,mem):
    vm=pl.BlockSpec(memory_space=pltpu.VMEM)
    wide=qug.shape[1]
    V=pltpu.VMEM
    sem=lambda n: pltpu.SemaphoreType.DMA((2,n))
    return pl.pallas_call(reduce_kernel,
        in_specs=[pl.BlockSpec(memory_space=pl.ANY)]*7,
        out_specs=[vm,vm],
        out_shape=[jax.ShapeDtypeStruct((TAGS,slab.shape[0]),f32),jax.ShapeDtypeStruct((RANK,3*wide+HD),f32)],
        scratch_shapes=[V(a.shape,a.dtype) for a in (asked,cols,qug,vug,mcot,slab,mem)]+[V((4,MB,8,128),f32),V((X*Y,4,RANK,BLK),bf16),V((4,MB,RANK,BLK),bf16),V((ZC,MB,RANK,BLK),bf16),V((MB,RANK,BLK),bf16),
            V((Y,TAGS+2*RANK,BLK),f32),V((Y,TAGS,BLK),f32),V((Y,2*RANK,BLK),bf16),
            V((32,8,128),f32),V((ZC,2,8,128),f32),V((X,2,8,128),f32),V((ZC,2,8,128),f32),
            V((16,8,128),f32),V((ZC,8,128),f32),V((X,8,128),f32),V((ZC,8,128),f32),
            sem(X*Y),sem(4),sem(ZC),sem(Y),sem(Y),sem(Y),sem(Y),sem(ZC),sem(X),sem(ZC),sem(ZC),sem(X),sem(ZC),pltpu.SemaphoreType.DMA((7,))],
        compiler_params=pltpu.CompilerParams(collective_id=1,has_side_effects=True,vmem_limit_bytes=60*2**20),
    )(asked,cols,qug,vug,mcot,slab,mem)

def unpack_kernel(logits, grads, a, b, c, d, e):
    wide=b.shape[1]
    a[...]=logits[...]
    b[...]=grads[:,0:wide]
    c[...]=grads[:,wide:2*wide]
    d[...]=grads[:,2*wide+HD:]
    e[...]=grads[:,2*wide:2*wide+HD]

def unpack(logits,grads,wide):
    S=jax.ShapeDtypeStruct; vm=pl.BlockSpec(memory_space=pltpu.VMEM)
    return pl.pallas_call(unpack_kernel,in_specs=[vm]*2,out_specs=[vm]*5,
        out_shape=[S(logits.shape,f32)]+[S((RANK,wide),f32)]*3+[S((RANK,HD),f32)],
        compiler_params=pltpu.CompilerParams(vmem_limit_bytes=60*2**20))(logits,grads)

UNIT=[(0,0,64),(0,64,64),(1,0,128),(2,0,128),(3,0,128),(4,0,128),(5,0,128),(6,0,128),(7,0,128)]
ROUND=[(0,0,128),(0,128,272),(1,0,272),(2,0,272),(3,0,272)]
UNITS=len(UNIT); RN=len(ROUND); DONE=3
FIRST={-1:[0],0:[1],1:[2],2:[3],3:[4],4:[5],5:[6],6:[7],7:[8]}
PLAN={(1, 0): [(0, 1)], (2, 0): [(0, 2), (1, 1)], (3, 0): [(0, 3), (1, 2), (2, 1)], (4, 0): [(0, 4), (1, 3), (2, 2), (3, 1)], (5, 0): [(0, 5), (1, 4), (2, 3), (3, 2), (4, 1)], (6, 0): [(1, 5), (2, 4), (3, 3), (4, 2)], (7, 0): [(2, 5), (3, 4), (4, 3)], (8, 0): [(3, 5), (4, 4)], (8, 1): [(4, 5)]}

def gather_kernel(mem_ref, slab_ref, wq_ref, wk_ref, wv_ref, qdown_hbm, vdown_hbm, qup_hbm, vup_hbm, ret_hbm,
                  pool, q_hbm, k_hbm, v_hbm, low_hbm, asked_out,
                  q_out, k_out, v_out, low_out, feat, wq, wkv, qdown_ref, vdown_ref, qup_ref, vup_ref, ret_ref, stage, mine, ysem, ssem, rsem, lsem, psem, osem, xsem, wsem):
    t=lax.axis_index("tm"); y=lax.axis_index("heads")
    x=lax.div(t,ZC); z=lax.rem(lax.div(t,2),Z); c=lax.rem(t,2)
    def tm(xx,zz,cc): return (xx*Z+zz)*2+cc
    xk=[lax.rem(x+k,X) for k in range(X)]
    devx=[(tm(xk[k],z,c),y) for k in range(X)]
    devz=[(tm(x,lax.rem(z+1,Z),c),y),(tm(x,lax.rem(z+Z-1,Z),c),y)]
    devc=(tm(x,z,1-c),y)
    devy=[(t,lax.rem(y+1,Y)),(t,lax.rem(y+Y-1,Y))]
    def rows_of(u):
        fb,r0,n=UNIT[u]
        return (mem_ref if fb<MB else slab_ref).at[pl.ds(fb%MB*BLK+r0,n)]
    own=lambda fb: pltpu.make_async_copy((mem_ref if fb<MB else slab_ref).at[pl.ds(fb%MB*BLK,BLK)],feat.at[fb,y],osem.at[fb])
    loads=[pltpu.make_async_copy(a,b,lsem.at[i]) for i,(a,b) in enumerate([(wk_ref,wkv.at[:,0:HD]),(wv_ref,wkv.at[:,HD:2*HD]),(vdown_hbm,vdown_ref),(vup_hbm,vup_ref),(ret_hbm,ret_ref),(wq_ref,wq),(qdown_hbm,qdown_ref),(qup_hbm,qup_ref)])]
    bar=pltpu.get_barrier_semaphore()
    for dev in devx[1:]+devz+devy+[devc]:
        pl.semaphore_signal(bar,inc=1,device_id=dev,device_id_type=MESH)
    for cp in loads[:4]: cp.start()
    pl.semaphore_wait(bar,X-1+5)

    def rc(src,dst,s,r,dev):
        return pltpu.make_async_remote_copy(src_ref=src,dst_ref=dst,send_sem=s,recv_sem=r,device_id=dev,device_id_type=MESH)
    left=lax.rem(y+Y-1,Y); right=lax.rem(y+1,Y)
    def piece_of(u,h,half=None):
        fb,r0,n=UNIT[u]
        return feat.at[fb,h,pl.ds(r0,n) if half is None else pl.ds(r0+half*(n//2),n//2)]
    def y_first(u): return [rc(rows_of(u),piece_of(u,y),ysem.at[0,u,i],ysem.at[1,u,i],devy[i]) for i in range(2)]
    def y_pass(u): return [rc(piece_of(u,h,i),piece_of(u,h,i),ysem.at[0,u,2+i],ysem.at[1,u,2+i],devy[i]) for i,h in enumerate((left,right))]
    def start(cs):
        for cp in cs: cp.start()
    asked=lambda k: rc(mine,asked_out.at[k],xsem.at[0,k],xsem.at[1,k],devx[k])

    def part(r,cc,xs,zs):
        b,lo,hi=ROUND[r]
        return pool.at[b,cc,xs,zs,pl.ds(lo,hi-lo)]
    def fresh(r):
        b,lo,hi=ROUND[r]
        return stage.at[b,pl.ds(lo,hi-lo)]
    every=pl.ds(0,X)
    GROUP=[pl.ds(0,1),pl.ds(1,2),pl.ds(3,2),pl.ds(5,2),pl.ds(7,1)]
    def share(b,cc,g): return rc(part(b,cc,every,GROUP[g]),part(b,cc,every,GROUP[g]),ssem.at[b,32+g],rsem.at[b,32+g],devc)
    def keep(b): return pltpu.make_async_copy(fresh(b),part(b,c,x,0),psem.at[b])
    def x_own(b,k): return rc(fresh(b),part(b,0,x,0),ssem.at[b,k-1],rsem.at[b,k],devx[k])
    back=[x]+[lax.rem(x+X-k,X) for k in range(1,X)]
    def hop0(b,l,i,k):
        src=part(b,0,back[k],0 if l==0 else 2*l-1+i)
        return rc(fresh(b) if l==0 and k==0 else src,part(b,0,back[k],2*l+1+i),ssem.at[b,3+8*l+2*k+i],rsem.at[b,4+8*l+2*k+i],devz[i])
    def last0(b,k):
        low=back[k]<X//2
        dev=(jnp.where(low,devz[0][0],devz[1][0]),y)
        return rc(part(b,0,back[k],jnp.where(low,5,6)),part(b,0,back[k],7),ssem.at[b,27+k],rsem.at[b,28+k],dev)
    def core0(b,phase):
        if phase==1:
            for k in range(1,X):
                x_own(b,k).wait_recv()
                for i in range(2): hop0(b,0,i,k).start()
            keep(b).wait()
        elif phase<5:
            l=phase-1
            for k in range(X):
                for i in range(2):
                    hop0(b,l-1,i,k).wait_recv()
                    if l<3: hop0(b,l,i,k).start()
                if l==3: last0(b,k).start()
        else:
            for k in range(X): last0(b,k).wait_recv()
        share(b,0,phase-1).start()
    def hop1(b,l,i):
        src=fresh(b) if l==0 else part(b,1,x,2*l-1+i)
        return rc(src,part(b,1,x,2*l+1+i if l<3 else 7),ssem.at[b,3+2*l+i if l<3 else 9],rsem.at[b,4+2*l+i if l<3 else 10],devz[i])
    def spread(b,g,k):
        src=part(b,1,x,0 if g==0 else GROUP[g])
        return rc(fresh(b) if g==0 else src,src,ssem.at[b,12+5*(k-1)+g],rsem.at[b,12+5*(k-1)+g],devx[k])
    def pass_on(b,g):
        for k in range(1,X): spread(b,g,k).wait_recv()
        share(b,1,g).start()
    def core1(b,phase):
        if phase<4:
            l=phase
            for i in range(2):
                hop1(b,l-1,i).wait_recv()
                if l<3 or b%2==i: hop1(b,l,i).start()
            for k in range(1,X): spread(b,l,k).start()
        elif phase==4:
            hop1(b,3,b%2).wait_recv()
            for k in range(1,X): spread(b,4,k).start()
        if phase==1: keep(b).wait()
        if phase in (2,3,4): pass_on(b,phase-2)
        if phase==5:
            pass_on(b,3); pass_on(b,4)
    def begin(b):
        keep(b).start()
        @pl.when(c==0)
        def _():
            for i in range(2): hop0(b,0,i,0).start()
            for k in range(1,X): x_own(b,k).start()
        @pl.when(c==1)
        def _():
            for i in range(2): hop1(b,0,i).start()
            for k in range(1,X): spread(b,0,k).start()
    def step(b,phase):
        pl.when(c==0)(lambda: core0(b,phase))
        pl.when(c==1)(lambda: core1(b,phase))

    def leave(b):
        rows=pl.ds(b*BLK,BLK)
        jobs=[(q_out.at[rows],q_hbm.at[rows]),(k_out.at[rows],k_hbm.at[rows]),(v_out.at[rows],v_hbm.at[rows]),(low_out.at[:,rows],low_hbm.at[:,rows])]
        return [pltpu.make_async_copy(src,dst,wsem.at[b,i]) for i,(src,dst) in enumerate(jobs)]
    def project(u):
        fb,r0,n=UNIT[u]
        if r0==0: own(fb).wait()
        if u==0:
            for i in range(4): loads[i].wait()
        memory=fb<MB
        if fb==MB:
            for i in range(5,8): loads[i].wait()
        pair=jnp.zeros((n,2*HD),f32)
        low=jnp.zeros((RANK if memory else 2*RANK,n),f32)
        wide=wq.shape[1]
        for h in range(Y):
            cols=slice(h*wide,(h+1)*wide)
            piece=feat[fb,h,r0:r0+n]
            pair=pair+jnp.dot(piece,wkv[cols,:],preferred_element_type=f32)
            down=vdown_ref[:,cols] if memory else jnp.concatenate([qdown_ref[:,cols],vdown_ref[:,cols]],axis=0)
            low=low+lax.dot_general(down,piece,NT,preferred_element_type=f32)
        low=low.astype(bf16)
        keys=pair[:,:HD].astype(bf16)
        values=(pair[:,HD:]+lax.dot_general(low[-RANK:],vup_ref[...],TN,preferred_element_type=f32)).astype(bf16)
        if memory:
            for i in range(0,n,64):
                stage[fb,2*(r0+i):2*(r0+i)+64,:]=keys[i:i+64]
                stage[fb,2*(r0+i)+64:2*(r0+i)+128,:]=values[i:i+64]
            stage[fb,2*BLK:,r0:r0+n]=low
        else:
            b=fb-MB
            rows=slice(b*BLK,(b+1)*BLK)
            k_out[rows,:]=keys
            v_out[rows,:]=values
            low_out[:,rows]=low
            acc=lax.dot_general(low[:RANK],qup_ref[...],TN,preferred_element_type=f32)
            for h in range(Y):
                acc=acc+jnp.dot(feat[fb,h],wq[h*wide:(h+1)*wide,:],preferred_element_type=f32)
            q_out[rows,:]=acc.astype(bf16)
            for cp in leave(b): cp.start()

    def over(b):
        for g in range(5):
            share(b,1-c,g).wait_recv()
            share(b,c,g).wait_send()
        keepers(b)
    def keepers(b):
        @pl.when(c==0)
        def _():
            for k in range(1,X): x_own(b,k).wait_send()
            for k in range(X):
                for l in range(3):
                    for i in range(2): hop0(b,l,i,k).wait_send()
                last0(b,k).wait_send()
        @pl.when(c==1)
        def _():
            for l in range(3):
                for i in range(2): hop1(b,l,i).wait_send()
            hop1(b,3,b%2).wait_send()
            for g in range(5):
                for k in range(1,X): spread(b,g,k).wait_send()
    def settled(u):
        for cp in y_first(u)+y_pass(u): cp.wait_send()

    for v in FIRST[-1]: start(y_first(v))
    for fb in range(2*MB): own(fb).start()
    for cp in loads[4:]: cp.start()
    mine[...]=jnp.full(mine.shape,-1,jnp.int32)
    loads[4].wait()
    mine[0:MB,0:TOP]=ret_ref[...]
    for k in range(1,X): asked(k).start()
    asked_out[0]=mine[...]
    for u in range(UNITS):
        for cp in y_first(u): cp.wait_recv()
        start(y_pass(u))
        for v in FIRST.get(u,[]): start(y_first(v))
        if u>RN: project(u-1)
        if u>=2: settled(u-2)
        if u==3:
            for k in range(1,X): asked(k).wait()
        if 0<=u-RN-1<DONE: over(u-RN-1)
        for b,p in PLAN.get((u,0),[]): step(b,p)
        for cp in y_pass(u): cp.wait_recv()
        if u<RN:
            project(u)
            begin(u)
        elif u==UNITS-1: project(u)
        for b,p in PLAN.get((u,1),[]): step(b,p)
    for u in range(UNITS-2,UNITS): settled(u)
    for b in range(DONE,RN): over(b)
    for b in range(MB):
        for cp in leave(b): cp.wait()

def gather_all(mem,slab,wq,wk,wv,qdown,vdown,qup,vup,ret):
    vm=pl.BlockSpec(memory_space=pltpu.VMEM); hbm=pl.BlockSpec(memory_space=pl.ANY)
    n=slab.shape[0]; wide=wq.shape[1]
    S=jax.ShapeDtypeStruct; V=pltpu.VMEM; D=pltpu.SemaphoreType.DMA
    return pl.pallas_call(gather_kernel,
        in_specs=[hbm]*10,
        out_specs=[hbm]*5+[vm],
        out_shape=[S((MB,2,X,Z,ROWS,HD),bf16),S((n,wide),bf16),S((n,HD),bf16),S((n,HD),bf16),S((2*RANK,n),bf16),S((X,8,128),jnp.int32)],
        scratch_shapes=[V((n,wide),bf16),V((n,HD),bf16),V((n,HD),bf16),V((2*RANK,n),bf16),V((2*MB,Y,BLK,wide),bf16),V(wq.shape,bf16),V((wq.shape[0],2*HD),bf16),V(qdown.shape,bf16),V(vdown.shape,bf16),V(qup.shape,bf16),V(vup.shape,bf16),V(ret.shape,jnp.int32),
            V((MB,ROWS,HD),bf16),V((8,128),jnp.int32),
            D((2,UNITS,4)),D((RN,37)),D((RN,37)),D((8,)),D((RN,)),D((2*MB,)),D((2,X)),D((MB,4))],
        compiler_params=pltpu.CompilerParams(collective_id=2,has_side_effects=True,vmem_limit_bytes=60*2**20),
    )(mem,slab,wq,wk,wv,qdown,vdown,qup,vup,ret)

def local(slab_tokens,memory,query_weight,key_weight,value_weight,query_down,query_up,value_down,value_up,tag_weight,retrieval,boundary,grad_tags):
    pool,queries,keys,values,low_t,asked=gather_all(memory,slab_tokens,query_weight,key_weight,value_weight,query_down,value_down,query_up,value_up,retrieval)
    cols,qug,vug,mcot=attend(retrieval,boundary,queries,keys,values,low_t,grad_tags.T,tag_weight.T,query_up,value_up,pool)
    logits,grads=reduce_all(asked,cols,qug,vug,mcot,slab_tokens,memory)
    logits,a,b,c,d=unpack(logits,grads,qug.shape[1])
    return logits.T,a,b,c,d


def solution(mesh):
    in_specs=(P("tm","heads"),P("tm","heads"),P(None,"heads"),P(None,"heads"),P(None,"heads"),P(),P(None,"heads"),P(),P(None,"heads"),P("heads",None),P("tm",None),P("tm"),P("tm",None))
    out_specs=(P("tm",None),P(None,"heads"),P(None,"heads"),P(None,"heads"),P(None,"heads"))
    return jax.shard_map(local,mesh=mesh,in_specs=in_specs,out_specs=out_specs,check_vma=False)
```
